32 devices in a mesh: layer: 4 (over z), plane: 8 (over y, x, core).
Axes of the slice: x: 2, y: 2, z: 4, core: 2. Of those that a mesh axis runs over, the one named last changes fastest.
Arguments:
- velocity: bfloat16 [2, 32, 32768], P(None, 'layer', 'plane'), may hold values from -6 to 6
- adjoint: bfloat16 [2, 32, 32768], P(None, 'layer', 'plane'), may hold values from -6 to 6
- corners: int32 [4, 32768], P(None, 'plane'), may hold values from 0 to 4607, as said below
- shared: int32 [4, 1024], P(None, 'plane'), may hold values from 0 to 4096, as said below
- stretch: float32 [2, 32768], P(None, 'plane'), may hold values from 0.5 to 2
- shear_part: float32 [2, 32768], P(None, 'plane'), may hold values from -0.2 to 0.2
- thickness: float32 [32, 32768], P('layer', 'plane'), may hold values from 0.3 to 3
- rate_factor: float32 [32, 32768], P('layer', 'plane'), may hold values from 0.5 to 2
- retention: float32 [32, 32768], P('layer', 'plane'), may hold values from 0.2 to 1
- weight: float32 [32, 32768], P('layer', 'plane'), may hold values from 0.5 to 2
Outputs:
- gradient: float32 [32768], P('plane')
The draws below stay inside these ranges and needn't reach their ends.
Inputs may be any that keep to these rules, and one draw needn't show every extreme that they name: `corners`: below 4096 a number names an owned node; 4096 + j * 128 + s names slot s of the ghost block of direction j (plane offsets -2, -1, +1, +2). Every slot of a block whose partition exists is named by exactly one corner, corner 0 of some element; blocks of directions beyond the ends of the plane axis are named by none. `shared`: row j, block p lists 128 distinct owned nodes of partition p that the partition at offset o_j (-2, -1, +1, +2) holds as ghosts; the block is 4096 throughout where that partition does not exist.
All inputs are finite; a program needn't handle non-finite values.
Results may differ from the reference program's by a relative error of at most 0.0003.
Values may be sent and summed in bfloat16 or wider, within the bound.
No kernel may reach another device: no remote copies, remote signals or barrier semaphores. Data moves between devices by JAX's collectives and lax.ppermute only.
A program may use at most 128 MiB of HBM per device.

```python
import math
import jax
import jax.numpy as jnp
from jax import lax

ELEM_DEV = 4096
SLOT = 128
NOWN = 4096
LAYER_TOTAL = 32
ELEMS = 32768
NODES = 32768
N_PLANE = 8


OFFSETS = (-2, -1, 1, 2)


def direction_valid():
    owners = jnp.arange(N_PLANE, dtype=jnp.int32)
    offset_list = jnp.array(OFFSETS, dtype=jnp.int32)
    source = owners[:, None] + offset_list[None, :]
    return (source >= 0) & (source < N_PLANE)


def draw_shared(key, part):

    def one_list(list_index):
        return jax.random.permutation(jax.random.fold_in(key, list_index), NOWN)[:SLOT].astype(jnp.int32)
    lists = jax.vmap(one_list)(jnp.arange(N_PLANE * 4, dtype=jnp.int32))
    lists = lists.reshape(N_PLANE, 4, SLOT)
    valid_mask = direction_valid()
    lists = jnp.where(valid_mask[:, :, None], lists, NOWN)
    return jnp.transpose(lists, (1, 0, 2)).reshape(4, N_PLANE * SLOT).astype(jnp.int32)


def draw_corners(key, part):
    key_base = jax.random.fold_in(key, 11)
    key_perm = jax.random.fold_in(key, 12)
    base_nodes = jax.random.randint(key_base, (4, N_PLANE, ELEM_DEV), 0, NOWN, dtype=jnp.int32)

    def one_perm(plane_index):
        return jax.random.permutation(jax.random.fold_in(key_perm, plane_index), ELEM_DEV)[:4 * SLOT].astype(jnp.int32)
    places = jax.vmap(one_perm)(jnp.arange(N_PLANE, dtype=jnp.int32))
    slot_ids = jnp.arange(4 * SLOT, dtype=jnp.int32)
    valid_mask = direction_valid()[:, slot_ids // SLOT]
    plane_rows = jnp.broadcast_to(jnp.arange(N_PLANE, dtype=jnp.int32)[:, None], places.shape)
    first_corner = base_nodes[0]
    current = first_corner[plane_rows, places]
    chosen = jnp.where(valid_mask, NOWN + slot_ids[None, :], current).astype(jnp.int32)
    first_corner = first_corner.at[plane_rows, places].set(chosen)
    base_nodes = base_nodes.at[0].set(first_corner)
    return base_nodes.reshape(4, N_PLANE * ELEM_DEV).astype(jnp.int32)


def draw_retention(key, part):
    random_key_sequence = [jax.random.fold_in(key, 21 + offset_index) for offset_index in range(6)]
    lattice_shape = (LAYER_TOTAL, ELEMS)
    slow_share = 0.5
    slow_mask = jax.random.bernoulli(random_key_sequence[0], slow_share, (1, ELEMS))
    total_keep = jnp.exp(jax.random.uniform(random_key_sequence[1], (1, ELEMS), jnp.float32, math.log(0.5), math.log(0.9)))
    layer_factor = jnp.exp(jax.random.uniform(random_key_sequence[2], (LAYER_TOTAL, 1), jnp.float32, math.log(0.5), math.log(1.5)))
    constant_flow_rate = jnp.exp(jnp.log(total_keep) * layer_factor / LAYER_TOTAL)
    sudden_event_mask = jax.random.bernoulli(random_key_sequence[3], 2.0 / LAYER_TOTAL, lattice_shape)
    sudden_keep_flag = jax.random.uniform(random_key_sequence[4], lattice_shape, jnp.float32, 0.5, 0.8)
    gentle_flow_rate = jnp.where(sudden_event_mask, constant_flow_rate * sudden_keep_flag, constant_flow_rate)
    fast_rate = jax.random.uniform(random_key_sequence[5], lattice_shape, jnp.float32, 0.2, 0.6)
    return jnp.where(slow_mask, gentle_flow_rate, fast_rate).astype(jnp.float32)


def levels(rng, shape, split, low, largest):
    gain = 1.0
    for axis_at, blocks in split:
        heights = jax.random.uniform(jax.random.fold_in(jax.random.fold_in(rng, 6), axis_at), (blocks,), jnp.float32, low / len(split), largest / len(split))
        gain = gain * jnp.repeat(jnp.exp(heights), shape[axis_at] // blocks).reshape((-1,) + (1,) * (len(shape) - 1 - axis_at))
    return gain


def centred(own_key, extent, scale, most, shards=(), held_as=jnp.bfloat16):
    loudness = levels(own_key, extent, shards, -0.22, 0.18) if shards else 1.0
    result = jax.random.normal(own_key, extent, jnp.float32) * scale * loudness
    return jnp.minimum(jnp.maximum(result, -most), most).astype(held_as)


def setup_inputs(seed: int = 0) -> dict:
    arg_keys = jax.random.split(jax.random.key(seed), 11)
    return {
        "velocity": centred(arg_keys[0], (2, LAYER_TOTAL, NODES), 1.0, 6.0, ((1, 4), (2, 8))),
        "adjoint": centred(arg_keys[1], (2, LAYER_TOTAL, NODES), 1.0, 6.0, ((1, 4), (2, 8))),
        "corners": draw_corners(jax.random.fold_in(arg_keys[10], 71), 0),
        "shared": draw_shared(jax.random.fold_in(arg_keys[10], 71), 0),
        "stretch": jnp.clip(jnp.exp(math.log(2.0) - 1.3862944 * jax.random.uniform(arg_keys[4], (2, ELEMS), jnp.float32) ** levels(arg_keys[4], (2, ELEMS), ((1, 8),), -0.2, 0.2)), 0.5, 2.0),
        "shear_part": jnp.clip(jax.random.uniform(arg_keys[5], (2, ELEMS), jnp.float32, -0.2, 0.2) * levels(arg_keys[5], (2, ELEMS), ((1, 8),), -0.4, 0.0), -0.2, 0.2),
        "thickness": jnp.clip(jnp.exp(math.log(3.0) - 2.3025851 * jax.random.uniform(arg_keys[6], (LAYER_TOTAL, ELEMS), jnp.float32) ** levels(arg_keys[6], (LAYER_TOTAL, ELEMS), ((0, 4), (1, 8)), -0.2, 0.2)), 0.3, 3.0),
        "rate_factor": jnp.clip(jnp.exp(math.log(2.0) - 1.3862944 * jax.random.uniform(arg_keys[7], (LAYER_TOTAL, ELEMS), jnp.float32) ** levels(arg_keys[7], (LAYER_TOTAL, ELEMS), ((0, 4), (1, 8)), -0.2, 0.2)), 0.5, 2.0),
        "retention": draw_retention(jax.random.fold_in(arg_keys[10], 71), 0),
        "weight": jnp.clip(jnp.exp(math.log(2.0) - 1.3862944 * jax.random.uniform(arg_keys[9], (LAYER_TOTAL, ELEMS), jnp.float32) ** levels(arg_keys[9], (LAYER_TOTAL, ELEMS), ((0, 4), (1, 8)), -0.2, 0.2)), 0.5, 2.0),
    }


OFFSETS = (-2, -1, 1, 2)
STRAIN_EPS = 0.01

def basis_table():
    gauss_point = 1.0 / math.sqrt(3.0)
    xi_signs = [-1.0, 1.0, 1.0, -1.0, -1.0, 1.0, 1.0, -1.0]
    eta_signs = [-1.0, -1.0, 1.0, 1.0, -1.0, -1.0, 1.0, 1.0]
    zeta_signs = [1.0, 1.0, 1.0, 1.0, -1.0, -1.0, -1.0, -1.0]
    shape_table = [[0.0] * 8 for row_index in range(24)]
    for point_index in range(8):
        xi_point = gauss_point if point_index & 1 else -gauss_point
        eta_point = gauss_point if point_index & 2 else -gauss_point
        zeta_point = gauss_point if point_index & 4 else -gauss_point
        for node_index in range(8):
            along_xi = 1.0 + xi_signs[node_index] * xi_point
            along_eta = 1.0 + eta_signs[node_index] * eta_point
            along_zeta = 1.0 + zeta_signs[node_index] * zeta_point
            shape_table[point_index][node_index] = xi_signs[node_index] * along_eta * along_zeta / 8.0
            shape_table[8 + point_index][node_index] = eta_signs[node_index] * along_xi * along_zeta / 8.0
            shape_table[16 + point_index][node_index] = zeta_signs[node_index] * along_xi * along_eta / 8.0
    return shape_table

def strain_of(grad_x, grad_y, grad_z, first_comp, second_comp):
    return (grad_x[first_comp], grad_y[second_comp], 0.5 * (grad_y[first_comp] + grad_x[second_comp]), 0.5 * grad_z[first_comp], 0.5 * grad_z[second_comp])

def pairing(left_strain, right_strain):
    return left_strain[0] * right_strain[0] + left_strain[1] * right_strain[1] + 0.5 * (left_strain[0] * right_strain[1] + left_strain[1] * right_strain[0]) + left_strain[2] * right_strain[2] + left_strain[3] * right_strain[3] + left_strain[4] * right_strain[4]

def element_terms(nodal_values, stretch, shear_part, thickness, rate_factor):
    layer_count = nodal_values.shape[1] - 1
    width = nodal_values.shape[3]
    top_nodes = nodal_values[:, :-1]
    bottom_nodes = nodal_values[:, 1:]
    hexa_nodes = jnp.concatenate([top_nodes, bottom_nodes], axis=2)
    basis = jnp.asarray(basis_table(), dtype=jnp.float32)
    derived = jnp.einsum('rn,clnb->clrb', basis, hexa_nodes, precision=lax.Precision.HIGHEST)
    derived = derived.reshape(4, layer_count, 3, 8, width)
    along_xi = derived[:, :, 0]
    along_eta = derived[:, :, 1]
    along_zeta = derived[:, :, 2]
    grad_x = stretch[0] * along_xi + shear_part[0] * along_eta
    grad_y = shear_part[1] * along_xi + stretch[1] * along_eta
    grad_z = (2.0 / thickness)[None, :, None, :] * along_zeta
    flow_strain = strain_of(grad_x, grad_y, grad_z, 0, 1)
    adjoint_strain = strain_of(grad_x, grad_y, grad_z, 2, 3)
    effective = pairing(flow_strain, flow_strain) + STRAIN_EPS
    viscosity = 0.5 * rate_factor[:, None, :] * jnp.power(effective, -1.0 / 3.0)
    volume = 0.5 * thickness / (stretch[0] * stretch[1] - shear_part[0] * shear_part[1])
    return volume * lax.optimization_barrier(jnp.sum(4.0 * viscosity * pairing(flow_strain, adjoint_strain), axis=1))

def reference(velocity, adjoint, corners, shared, stretch, shear_part, thickness, rate_factor, retention, weight):
    fields = jnp.concatenate([velocity, adjoint], axis=0).astype(jnp.float32)
    fields = jnp.concatenate([fields, jnp.zeros((4, 1, NODES), jnp.float32)], axis=1)
    ghost_pos = jnp.arange(4 * SLOT, dtype=jnp.int32)
    direction = ghost_pos // SLOT
    slot_pos = ghost_pos % SLOT
    offset_of = jnp.array(OFFSETS, dtype=jnp.int32)[direction]
    owners = jnp.arange(N_PLANE, dtype=jnp.int32)
    source = owners[:, None] + offset_of[None, :]
    valid_mask = (source >= 0) & (source < N_PLANE)
    safe_source = jnp.clip(source, 0, N_PLANE - 1)
    owned_at = shared[(3 - direction)[None, :], safe_source * SLOT + slot_pos[None, :]]
    ghost_global = jnp.where(valid_mask, safe_source * NOWN + owned_at, 0).astype(jnp.int32)
    own_global = owners[:, None] * NOWN + jnp.arange(NOWN, dtype=jnp.int32)[None, :]
    global_table = jnp.concatenate([own_global, ghost_global], axis=1)
    plane_of = jnp.arange(ELEMS, dtype=jnp.int32) // ELEM_DEV
    global_corners = global_table[plane_of[None, :], corners].astype(jnp.int32)
    block_size = min(1024, ELEM_DEV)
    block_count = ELEMS // block_size

    def one_block(block_start):
        corner_ids = lax.dynamic_slice_in_dim(global_corners, block_start, block_size, 1)
        nodal_values = jnp.take(fields, corner_ids, axis=2)
        return element_terms(nodal_values, lax.dynamic_slice_in_dim(stretch, block_start, block_size, 1), lax.dynamic_slice_in_dim(shear_part, block_start, block_size, 1), lax.dynamic_slice_in_dim(thickness, block_start, block_size, 1), lax.dynamic_slice_in_dim(rate_factor, block_start, block_size, 1))
    starts = jnp.arange(block_count, dtype=jnp.int32) * block_size
    layer_terms = lax.map(one_block, starts)
    layer_terms = jnp.transpose(layer_terms, (1, 0, 2)).reshape(LAYER_TOTAL, ELEMS)

    def layer_step(running, inputs):
        keep_share, layer_weight, layer_term = inputs
        running_next = keep_share * running + (1.0 - keep_share) * layer_weight
        return (running_next, running_next * layer_term)
    _, weighted = lax.scan(layer_step, jnp.zeros((ELEMS,), jnp.float32), (retention, weight, layer_terms))
    column = lax.optimization_barrier(jnp.sum(weighted, axis=0))
    spread = jnp.tile(0.25 * column, 4)
    return jax.ops.segment_sum(spread, global_corners.reshape(-1), num_segments=NODES)
```

```python
import functools
import math

import jax
import jax.numpy as jnp
from jax import lax
from jax.experimental import pallas as pl
from jax.experimental.pallas import tpu as pltpu
from jax.sharding import PartitionSpec as P

OFFSETS = (-2, -1, 1, 2)
STRAIN_EPS = 0.01
GAUSS = 1.0 / math.sqrt(3.0)
SPAN = 256
LANES = 128
F32, BF16 = jnp.float32, jnp.bfloat16
NT = (((1,), (1,)), ((), ()))


def shifted(value, axis, steps):
    count = lax.axis_size(axis)
    first, last = (max(0, -steps), min(count, count - steps))
    return lax.ppermute(value, axis, [(source, source + steps) for source in range(first, last)])


def kernel_call(body, out_shape, flops, *args):
    vmem = pl.BlockSpec(memory_space=pltpu.VMEM)
    return pl.pallas_call(
        body,
        out_shape=out_shape,
        in_specs=[vmem] * len(args),
        out_specs=jax.tree.map(lambda _: vmem, out_shape),
        compiler_params=pltpu.CompilerParams(vmem_limit_bytes=48 * 2**20),
        cost_estimate=pl.CostEstimate(flops=flops, bytes_accessed=2**20, transcendentals=0),
    )(*args)


def node_table(velocity, adjoint):
    rows = 4 * velocity.shape[1]
    fields = jnp.concatenate(
        [velocity[0], velocity[1], adjoint[0], adjoint[1]], axis=0
    )
    blocks = fields.shape[1] // SPAN
    return jnp.concatenate([fields[:, h * SPAN : (h + 1) * SPAN] for h in range(blocks)], axis=0), rows


def below_table(below):
    wide = below.astype(F32)
    blocks = wide.shape[1] // SPAN
    return jnp.concatenate(
        [wide[:, h * SPAN : (h + 1) * SPAN] for h in range(blocks)], axis=0
    ).astype(BF16)


def one_hot(low, dtype=BF16):
    width = low.shape[1]
    rows = lax.broadcasted_iota(jnp.int32, (SPAN, width), 0)
    return (rows == low).astype(F32).astype(dtype)


def choose(picked, high, rows):
    parts = [picked[i : i + rows] for i in range(0, picked.shape[0], rows)]
    bit = 1
    while len(parts) > 1:
        odd = (high & bit) != 0
        parts = [jnp.where(odd, parts[i + 1], parts[i]) for i in range(0, len(parts), 2)]
        bit *= 2
    return parts[0]


def pick(table, rows, ids):
    low, high = ids & (SPAN - 1), ids >> 8
    picked = jnp.dot(table, one_hot(low), preferred_element_type=F32)
    return choose(picked, high, rows)


def element_kernel(corners, thickness, rate, retention, weight, stretch, shear, data, ids):
    elems = corners.shape[1]
    slots = data.shape[1]
    owned = elems
    chunk = min(512, elems)

    def step(i, total):
        at = pl.ds(pl.multiple_of(i * chunk, chunk), chunk)
        values = jnp.concatenate(
            [
                thickness[:, at],
                rate[:, at],
                retention[:, at],
                weight[:, at],
                stretch[:, at],
                shear[:, at],
                jnp.zeros((4, chunk), F32),
            ],
            axis=0,
        )
        coarse = values.astype(BF16).astype(F32)
        names = corners[:, at]
        rows = jnp.concatenate(
            [
                coarse,
                values - coarse,
                (names & (SPAN - 1)).astype(F32),
                (names >> 8).astype(F32),
                jnp.zeros((8, chunk), F32),
            ],
            axis=0,
        ).astype(BF16)
        slot = lax.broadcasted_iota(jnp.int32, (slots, chunk), 0) + owned
        mine = (slot == names[0:1]).astype(F32).astype(BF16)
        return total + lax.dot_general(rows, mine, NT, preferred_element_type=F32)

    total = lax.fori_loop(0, elems // chunk, step, jnp.zeros((96, slots), F32))
    data[...] = total[:80].astype(BF16)
    ids[...] = total[80:88].astype(jnp.int32)


def message_kernel(velocity, adjoint, below, shared, data, ids, own, *messages):
    table, rows = node_table(velocity, adjoint)
    low_table = below_table(below[...])
    slot = shared.shape[1]
    high_count = velocity.shape[2] // SPAN
    lists = [jnp.concatenate([shared[j : j + 1, :] for j in range(4)], axis=1)]
    lists += [ids[c : c + 1, :] + ids[4 + c : 5 + c, :] * SPAN for c in (1, 2, 3)]
    upper, lower = [], []
    for names in lists:
        low, high = names & (SPAN - 1), names >> 8
        hot = one_hot(low)
        picked = choose(jnp.dot(table, hot, preferred_element_type=F32), high, rows)
        upper.append(picked)
        lower.append(choose(jnp.dot(low_table, hot, preferred_element_type=F32), high, 4))
    bottom = jnp.concatenate(lower, axis=0)
    own[...] = jnp.concatenate([upper[0], bottom], axis=0).astype(BF16)
    everything = jnp.concatenate(upper + [bottom], axis=0).astype(BF16)
    for j in range(4):
        at = slice(j * slot, (j + 1) * slot)
        messages[j][: 4 * rows + 16, :] = everything[:, at]
        messages[j][4 * rows + 16 :, :] = data[:, at]


def pick_kernel(velocity, adjoint, below, corners, upper, lower):
    table, rows = node_table(velocity, adjoint)
    low_table = below_table(below[...])
    elems = corners.shape[1]
    chunk = SPAN

    def step(i, _):
        at = pl.ds(pl.multiple_of(i * chunk, chunk), chunk)
        bottom = []
        for c in range(4):
            names = corners[c : c + 1, at]
            low, high = names & (SPAN - 1), names >> 8
            hot = one_hot(low)
            picked = choose(jnp.dot(table, hot, preferred_element_type=F32), high, rows)
            upper[c * rows : (c + 1) * rows, at] = picked.astype(BF16)
            bottom.append(choose(jnp.dot(low_table, hot, preferred_element_type=F32), high, 4))
        lower[:, at] = jnp.concatenate(bottom, axis=0).astype(BF16)
        return 0

    lax.fori_loop(0, elems // chunk, step, 0)


def plane_modes(a0, a1, a2, a3):
    s01, d01, s23, d23 = a0 + a1, a1 - a0, a2 + a3, a2 - a3
    return s01 + s23, d01 + d23, s23 - s01, d23 - d01


def terms(upper, bottom, stretch, shear, thickness, rate):
    layers, n = thickness.shape
    last = lax.broadcasted_iota(jnp.int32, (layers, n), 0) == layers - 1
    plus, minus, depth = [], [], []
    for comp in range(4):
        top = plane_modes(*[upper[c][comp] for c in range(4)])
        end = plane_modes(*[bottom[c][comp] for c in range(4)])
        under = [
            jnp.where(last, jnp.broadcast_to(e, t.shape), pltpu.roll(t, layers - 1, 0))
            for t, e in zip(top, end)
        ]
        depth_parts = [top[0] - under[0]]
        plus_parts, minus_parts = [], []
        for t, u in zip(top[1:], under[1:]):
            total, half = t + u, GAUSS * (t - u)
            plus_parts.append(total + half)
            minus_parts.append(total - half)
            depth_parts.append(half)
        plus.append(plus_parts)
        minus.append(minus_parts)
        depth.append(depth_parts)
    s0, s1 = stretch[0:1] * (1.0 / 16.0), stretch[1:2] * (1.0 / 16.0)
    h0, h1 = shear[0:1] * (1.0 / 16.0), shear[1:2] * (1.0 / 16.0)
    gs0, gs1, gh0, gh1 = s0 * GAUSS, s1 * GAUSS, h0 * GAUSS, h1 * GAUSS

    def plane_fields(part, first):
        (xa, ya, wa), (xb, yb, wb) = part[first], part[first + 1]
        p1, p2 = s0 * xa + h0 * ya, h1 * xb + s1 * yb
        x1, x2 = gh0 * wa, gs1 * wb
        y1, y2 = gs0 * wa, gh1 * wb
        return (
            (p1 + p2, x1 + x2, y1 + y2),
            (p1 - p2, x1 - x2, y1 - y2),
            (
                (h1 * xa + s1 * ya) + (s0 * xb + h0 * yb),
                gs1 * wa + gh0 * wb,
                gh1 * wa + gs0 * wb,
            ),
        )

    def four(field):
        base, along_x, along_y = field
        up, um = base + along_x, base - along_x
        return up + along_y, up - along_y, um + along_y, um - along_y

    inverse = 0.125 / thickness
    inverse_g = inverse * GAUSS

    def depth_four(parts):
        q0, qx, qy, qw = (
            parts[0] * inverse,
            parts[1] * inverse,
            parts[2] * inverse,
            parts[3] * inverse_g,
        )
        p, m, r, t = q0 + qx, q0 - qx, qy + qw, qy - qw
        return p + r, p - r, m + t, m - t

    za, zb, zc, zd = [depth_four(depth[comp]) for comp in range(4)]
    shear_ff = [za[k] * za[k] + zb[k] * zb[k] + STRAIN_EPS for k in range(4)]
    shear_fa = [za[k] * zc[k] + zb[k] * zd[k] for k in range(4)]
    total = None
    for part in (plus, minus):
        flow = [four(f) for f in plane_fields(part, 0)]
        other = [four(f) for f in plane_fields(part, 2)]
        for k in range(4):
            s, d, x = flow[0][k], flow[1][k], flow[2][k]
            triple = 3.0 * s
            effective = (triple * s + d * d) + (x * x + shear_ff[k])
            paired = (triple * other[0][k] + d * other[1][k]) + (x * other[2][k] + shear_fa[k])
            value = jnp.exp(jnp.log(effective) * (-1.0 / 3.0)) * paired
            total = value if total is None else total + value
    det = stretch[0:1] * stretch[1:2] - shear[0:1] * shear[1:2]
    return total * (rate * thickness / det)


def group_maps(retention, weight, term):
    layers, n = retention.shape
    row = lax.broadcasted_iota(jnp.int32, (layers, n), 0)
    factor, offset = retention, (1.0 - retention) * weight
    step = 1
    while step < layers:
        seen = row >= step
        before_f = jnp.where(seen, pltpu.roll(factor, step, 0), 1.0)
        before_o = jnp.where(seen, pltpu.roll(offset, step, 0), 0.0)
        offset = factor * before_o + offset
        factor = factor * before_f
        step *= 2
    return jnp.concatenate(
        [
            factor[layers - 1 :],
            offset[layers - 1 :],
            jnp.sum(factor * term, axis=0, keepdims=True),
            jnp.sum(offset * term, axis=0, keepdims=True),
        ],
        axis=0,
    )


def physics_kernel(
    upper, lower, own, in0, in1, in2, in3, corners, shared,
    stretch, shear, thickness, rate, retention, weight, out,
):
    incoming = (in0, in1, in2, in3)
    layers, elems = thickness.shape
    rows = 4 * layers
    slot = shared.shape[1]
    slots = 4 * slot
    got = jnp.concatenate([ref[...] for ref in incoming], axis=1)
    ghost = got[:rows]
    ghost_low = got[4 * rows : 4 * rows + 4]
    blocks = slots // SPAN
    first = elems // SPAN
    table = jnp.concatenate([ghost[:, h * SPAN : (h + 1) * SPAN] for h in range(blocks)], axis=0)
    low_table = below_table(ghost_low)
    chunk = SPAN

    def step(i, _):
        at = pl.ds(pl.multiple_of(i * chunk, chunk), chunk)
        names = corners[0:1, at]
        low, high = names & (SPAN - 1), (names >> 8) - first
        hot = one_hot(low)
        is_ghost = high >= 0
        picked = choose(jnp.dot(table, hot, preferred_element_type=F32), high, rows)
        picked_low = choose(jnp.dot(low_table, hot, preferred_element_type=F32), high, 4)
        corner0 = jnp.where(is_ghost, picked, upper[:rows, at].astype(F32))
        low_rows = lower[:, at].astype(F32)
        low0 = jnp.where(is_ghost, picked_low, low_rows[:4])
        full = [corner0] + [upper[c * rows : (c + 1) * rows, at].astype(F32) for c in (1, 2, 3)]
        ends = [low0] + [low_rows[4 * c : 4 * c + 4] for c in (1, 2, 3)]
        for k in range(chunk // LANES):
            cut = slice(k * LANES, (k + 1) * LANES)
            here = pl.ds(pl.multiple_of(i * chunk + k * LANES, LANES), LANES)
            tops = [[f[m * layers : (m + 1) * layers, cut] for m in range(4)] for f in full]
            bots = [[e[m : m + 1, cut] for m in range(4)] for e in ends]
            term = terms(
                tops, bots, stretch[:, here], shear[:, here], thickness[:, here], rate[:, here]
            )
            out[:, here] = group_maps(retention[:, here], weight[:, here], term)
        return 0

    lax.fori_loop(0, elems // chunk, step, 0)

    mine = own[...].astype(F32)
    wide = got.astype(F32)
    base = 4 * rows + 16
    data = wide[base : base + 40] + wide[base + 40 : base + 80]
    for k in range(slots // LANES):
        cut = slice(k * LANES, (k + 1) * LANES)
        tops = [[mine[m * layers : (m + 1) * layers, cut] for m in range(4)]]
        bots = [[mine[rows + m : rows + m + 1, cut] for m in range(4)]]
        for c in (1, 2, 3):
            tops.append(
                [wide[c * rows + m * layers : c * rows + (m + 1) * layers, cut] for m in range(4)]
            )
            bots.append(
                [wide[4 * rows + 4 * c + m : 4 * rows + 4 * c + m + 1, cut] for m in range(4)]
            )
        part = data[:, cut]
        term = terms(
            tops, bots, part[4 * layers : 4 * layers + 2], part[4 * layers + 2 : 4 * layers + 4],
            part[:layers], part[layers : 2 * layers],
        )
        out[:, elems + k * LANES : elems + (k + 1) * LANES] = group_maps(
            part[2 * layers : 3 * layers], part[3 * layers : 4 * layers], term
        )


def sum_kernel(earlier, later, corners, shared, out):
    elems = corners.shape[1]
    slot = shared.shape[1]
    high_count = out.shape[0]
    chunk = min(512, elems)

    def add(total, names, values):
        width = names.shape[1]
        low, high = names & (LANES - 1), names >> 7
        coarse = values.astype(BF16).astype(F32)
        fine = values - coarse
        here = lax.broadcasted_iota(jnp.int32, (high_count, width), 0) == high
        left = jnp.concatenate([jnp.where(here, coarse, 0.0), jnp.where(here, fine, 0.0)], axis=0)
        hot = (lax.broadcasted_iota(jnp.int32, (LANES, width), 0) == low).astype(F32).astype(BF16)
        return total + lax.dot_general(left.astype(BF16), hot, NT, preferred_element_type=F32)

    def column(at):
        first, second = earlier[:, at], later[:, at]
        return 0.25 * (first[3:4] + second[3:4] + first[1:2] * second[2:3])

    def step(i, total):
        at = pl.ds(pl.multiple_of(i * chunk, chunk), chunk)
        values = column(at)
        for c in range(4):
            total = add(total, corners[c : c + 1, at], values)
        return total

    total = lax.fori_loop(0, elems // chunk, step, jnp.zeros((2 * high_count, LANES), F32))
    names = jnp.concatenate([shared[j : j + 1, :] for j in range(4)], axis=1)
    values = column(pl.ds(elems, 4 * slot))
    values = jnp.where(names < elems, values, 0.0)
    total = add(total, names, values)
    out[...] = total[:high_count] + total[high_count:]


def compose(one, two):
    return jnp.stack(
        [
            one[0] * two[0],
            two[0] * one[1] + two[1],
            one[2] + one[0] * two[2],
            one[3] + two[3] + one[1] * two[2],
        ]
    )


def shards(
    velocity, adjoint, corners, shared, stretch, shear_part, thickness, rate_factor, retention, weight
):
    layers, owned = velocity.shape[1:]
    elems = corners.shape[1]
    slot = shared.shape[1]
    slots = 4 * slot
    rows = 4 * layers
    shape = jax.ShapeDtypeStruct
    below = shifted(
        jnp.concatenate([velocity[:, 0], adjoint[:, 0]], axis=0), "layer", -1
    )
    data, ids = kernel_call(
        element_kernel,
        (shape((80, slots), BF16), shape((8, slots), jnp.int32)),
        2 * 10**9,
        corners, thickness, rate_factor, retention, weight, stretch, shear_part,
    )
    own, *messages = kernel_call(
        message_kernel,
        (shape((rows + 16, slots), BF16),) + (shape((4 * rows + 96, slot), BF16),) * 4,
        10**9,
        velocity, adjoint, below, shared, data, ids,
    )
    incoming = [shifted(messages[3 - j], "plane", -OFFSETS[j]) for j in range(4)]
    upper, lower = kernel_call(
        pick_kernel,
        (shape((4 * rows, elems), BF16), shape((16, elems), BF16)),
        8 * 10**9,
        velocity, adjoint, below, corners,
    )
    state = kernel_call(
        physics_kernel,
        shape((4, elems + slots), F32),
        4 * 10**9,
        upper, lower, own, *incoming, corners, shared,
        stretch, shear_part, thickness, rate_factor, retention, weight,
    )
    groups, place = lax.axis_size("layer"), lax.axis_index("layer")
    step = 1
    earlier = later = state
    while step < groups:
        if step > 1:
            state = compose(earlier, later)
        other = lax.ppermute(state, "layer", [(i, i ^ step) for i in range(groups)])
        second = (place & step) != 0
        earlier, later = jnp.where(second, other, state), jnp.where(second, state, other)
        step *= 2
    gradient = kernel_call(
        sum_kernel,
        shape((owned // LANES, LANES), F32),
        2 * 10**9,
        earlier, later, corners, shared,
    )
    return gradient.reshape(owned)


def solution(mesh):
    return jax.shard_map(
        shards,
        mesh=mesh,
        in_specs=(
            P(None, "layer", "plane"),
            P(None, "layer", "plane"),
            P(None, "plane"),
            P(None, "plane"),
            P(None, "plane"),
            P(None, "plane"),
            P("layer", "plane"),
            P("layer", "plane"),
            P("layer", "plane"),
            P("layer", "plane"),
        ),
        out_specs=P("plane"),
        check_vma=False,
    )
```

```python
import math

import jax
import jax.numpy as jnp
from jax import lax
from jax.experimental import pallas as pl
from jax.experimental.pallas import tpu as pltpu
from jax.sharding import PartitionSpec as P

OFFSETS = (-2, -1, 1, 2)
STRAIN_EPS = 0.01
GAUSS = 1.0 / math.sqrt(3.0)
SPAN = 256
LANES = 128
F32, BF16 = jnp.float32, jnp.bfloat16
NT = (((1,), (1,)), ((), ()))


def shifted(value, axis, steps):
    count = lax.axis_size(axis)
    first, last = (max(0, -steps), min(count, count - steps))
    return lax.ppermute(value, axis, [(source, source + steps) for source in range(first, last)])


def kernel_call(body, out_shape, flops, *args, spaces=None, scratch=()):
    vmem = pl.BlockSpec(memory_space=pltpu.VMEM)
    far = pl.BlockSpec(memory_space=pl.ANY)
    return pl.pallas_call(
        body,
        out_shape=out_shape,
        in_specs=[far if spaces == "far" else vmem for _ in args],
        out_specs=jax.tree.map(lambda _: vmem, out_shape),
        scratch_shapes=list(scratch),
        compiler_params=pltpu.CompilerParams(vmem_limit_bytes=48 * 2**20),
        cost_estimate=pl.CostEstimate(flops=flops, bytes_accessed=2**20, transcendentals=0),
    )(*args)


def fetch(pairs, semaphores):
    copies = [
        pltpu.make_async_copy(source, target, semaphores.at[i])
        for i, (source, target) in enumerate(pairs)
    ]
    for copy in copies:
        copy.start()
    for copy in copies:
        copy.wait()


def node_table(fields):
    blocks = fields.shape[1] // SPAN
    return jnp.concatenate([fields[:, h * SPAN : (h + 1) * SPAN] for h in range(blocks)], axis=0)


def below_table(below):
    wide = below.astype(F32)
    blocks = wide.shape[1] // SPAN
    return jnp.concatenate(
        [wide[:, h * SPAN : (h + 1) * SPAN] for h in range(blocks)], axis=0
    ).astype(BF16)


def one_hot(low, dtype=BF16):
    width = low.shape[1]
    rows = lax.broadcasted_iota(jnp.int32, (SPAN, width), 0)
    return (rows == low).astype(F32).astype(dtype)


def choose(picked, high, rows):
    parts = [picked[i : i + rows] for i in range(0, picked.shape[0], rows)]
    bit = 1
    while len(parts) > 1:
        odd = (high & bit) != 0
        parts = [jnp.where(odd, parts[i + 1], parts[i]) for i in range(0, len(parts), 2)]
        bit *= 2
    return parts[0]


def pick_both(table, ids, rows):
    low, high = ids & (SPAN - 1), ids >> 8
    split = table.shape[0] * rows // (rows + 4)
    picked = jnp.dot(table, one_hot(low), preferred_element_type=F32)
    return choose(picked[:split], high, rows), choose(picked[split:], high, 4)


def level_kernel(velocity, adjoint, fields, top, first, second, semaphores):
    fetch([(velocity, first), (adjoint, second)], semaphores)
    layers = first.shape[1]
    parts = [first[0], first[1], second[0], second[1]]
    fields[...] = jnp.concatenate(parts, axis=0)
    wide = [part.astype(F32)[0:1] for part in parts]
    top[...] = jnp.concatenate(wide, axis=0).astype(BF16)


def element_kernel(
    corners, shared, thickness, rate, retention, weight, stretch, shear,
    data, ids, params, names, sends, stretch_here, shear_here, shared_here, semaphores,
):
    layers, elems = thickness.shape
    slots = data.shape[1]
    slot = shared_here.shape[1]
    layered = (thickness, rate, retention, weight)
    fetch(
        [(corners, names), (shared, shared_here), (stretch, stretch_here), (shear, shear_here)]
        + [(ref, params.at[pl.ds(i * layers, layers)]) for i, ref in enumerate(layered)],
        semaphores,
    )
    params[4 * layers :, :] = jnp.concatenate(
        [stretch_here[...], shear_here[...], jnp.zeros((4, elems), F32)], axis=0
    )
    sends[...] = jnp.concatenate([shared_here[j : j + 1, :] for j in range(4)], axis=1)
    chunk = min(1024, elems)

    def step(i, total):
        at = pl.ds(pl.multiple_of(i * chunk, chunk), chunk)
        values = params[:, at]
        coarse = values.astype(BF16).astype(F32)
        here = names[:, at]
        rows = jnp.concatenate(
            [
                coarse,
                values - coarse,
                (here & (SPAN - 1)).astype(F32),
                (here >> 8).astype(F32),
                jnp.zeros((8, chunk), F32),
            ],
            axis=0,
        ).astype(BF16)
        wanted = lax.broadcasted_iota(jnp.int32, (slots, chunk), 0) + elems
        mine = (wanted == here[0:1]).astype(F32).astype(BF16)
        return total + lax.dot_general(rows, mine, NT, preferred_element_type=F32)

    total = lax.fori_loop(0, elems // chunk, step, jnp.zeros((96, slots), F32))
    data[...] = total[:80].astype(BF16)
    ids[...] = total[80:88].astype(jnp.int32)


def message_kernel(fields, below, sends, data, ids, own, messages):
    rows = fields.shape[0]
    table = jnp.concatenate([node_table(fields), below_table(below[...])], axis=0)
    slot = messages.shape[2]
    lists = [sends[...]]
    lists += [ids[c : c + 1, :] + ids[4 + c : 5 + c, :] * SPAN for c in (1, 2, 3)]
    upper, lower = zip(*[pick_both(table, names, rows) for names in lists])
    bottom = jnp.concatenate(lower, axis=0)
    own[...] = jnp.concatenate([upper[0], bottom], axis=0).astype(BF16)
    everything = jnp.concatenate(list(upper) + [bottom], axis=0).astype(BF16)
    place, count = lax.axis_index("plane"), messages.shape[0]
    for j, offset in enumerate(OFFSETS):
        at = slice(j * slot, (j + 1) * slot)
        target = place + offset

        @pl.when((target >= 0) & (target < count))
        def _():
            messages[target, : 4 * rows + 16, :] = everything[:, at]
            messages[target, 4 * rows + 16 :, :] = data[:, at]


def pick_kernel(fields, below, corners, upper, lower):
    rows = fields.shape[0]
    table = jnp.concatenate([node_table(fields), below_table(below[...])], axis=0)
    elems = corners.shape[1]
    chunk = min(1024, elems)

    def step(i, _):
        at = pl.ds(pl.multiple_of(i * chunk, chunk), chunk)
        bottom = []
        for c in range(4):
            picked, ends = pick_both(table, corners[c : c + 1, at], rows)
            upper[c * rows : (c + 1) * rows, at] = picked.astype(BF16)
            bottom.append(ends)
        lower[:, at] = jnp.concatenate(bottom, axis=0).astype(BF16)
        return 0

    lax.fori_loop(0, elems // chunk, step, 0)


def plane_modes(a0, a1, a2, a3):
    s01, d01, s23, d23 = a0 + a1, a1 - a0, a2 + a3, a2 - a3
    return s01 + s23, d01 + d23, s23 - s01, d23 - d01


def terms(upper, bottom, stretch, shear, thickness, rate):
    layers, n = thickness.shape
    last = lax.broadcasted_iota(jnp.int32, (layers, n), 0) == layers - 1
    plus, minus, depth = [], [], []
    for comp in range(4):
        top = plane_modes(*[upper[c][comp] for c in range(4)])
        end = plane_modes(*[bottom[c][comp] for c in range(4)])
        under = [
            jnp.where(last, jnp.broadcast_to(e, t.shape), pltpu.roll(t, layers - 1, 0))
            for t, e in zip(top, end)
        ]
        depth_parts = [top[0] - under[0]]
        plus_parts, minus_parts = [], []
        for t, u in zip(top[1:], under[1:]):
            total, half = t + u, GAUSS * (t - u)
            plus_parts.append(total + half)
            minus_parts.append(total - half)
            depth_parts.append(half)
        plus.append(plus_parts)
        minus.append(minus_parts)
        depth.append(depth_parts)
    s0, s1 = stretch[0:1] * (1.0 / 16.0), stretch[1:2] * (1.0 / 16.0)
    h0, h1 = shear[0:1] * (1.0 / 16.0), shear[1:2] * (1.0 / 16.0)
    gs0, gs1, gh0, gh1 = s0 * GAUSS, s1 * GAUSS, h0 * GAUSS, h1 * GAUSS

    def plane_fields(part, first):
        (xa, ya, wa), (xb, yb, wb) = part[first], part[first + 1]
        p1, p2 = s0 * xa + h0 * ya, h1 * xb + s1 * yb
        x1, x2 = gh0 * wa, gs1 * wb
        y1, y2 = gs0 * wa, gh1 * wb
        return (
            (p1 + p2, x1 + x2, y1 + y2),
            (p1 - p2, x1 - x2, y1 - y2),
            (
                (h1 * xa + s1 * ya) + (s0 * xb + h0 * yb),
                gs1 * wa + gh0 * wb,
                gh1 * wa + gs0 * wb,
            ),
        )

    def four(field):
        base, along_x, along_y = field
        up, um = base + along_x, base - along_x
        return up + along_y, up - along_y, um + along_y, um - along_y

    inverse = 0.125 / thickness
    inverse_g = inverse * GAUSS

    def depth_four(parts):
        q0, qx, qy, qw = (
            parts[0] * inverse,
            parts[1] * inverse,
            parts[2] * inverse,
            parts[3] * inverse_g,
        )
        p, m, r, t = q0 + qx, q0 - qx, qy + qw, qy - qw
        return p + r, p - r, m + t, m - t

    za, zb, zc, zd = [depth_four(depth[comp]) for comp in range(4)]
    shear_ff = [za[k] * za[k] + zb[k] * zb[k] + STRAIN_EPS for k in range(4)]
    shear_fa = [za[k] * zc[k] + zb[k] * zd[k] for k in range(4)]
    total = None
    for part in (plus, minus):
        flow = [four(f) for f in plane_fields(part, 0)]
        other = [four(f) for f in plane_fields(part, 2)]
        for k in range(4):
            s, d, x = flow[0][k], flow[1][k], flow[2][k]
            triple = 3.0 * s
            effective = (triple * s + d * d) + (x * x + shear_ff[k])
            paired = (triple * other[0][k] + d * other[1][k]) + (x * other[2][k] + shear_fa[k])
            value = jnp.exp(jnp.log(effective) * (-1.0 / 3.0)) * paired
            total = value if total is None else total + value
    det = stretch[0:1] * stretch[1:2] - shear[0:1] * shear[1:2]
    return total * (rate * thickness / det)


def group_maps(retention, weight, term):
    layers, n = retention.shape
    row = lax.broadcasted_iota(jnp.int32, (layers, n), 0)
    factor, offset = retention, (1.0 - retention) * weight
    step = 1
    while step < layers:
        seen = row >= step
        before_f = jnp.where(seen, pltpu.roll(factor, step, 0), 1.0)
        before_o = jnp.where(seen, pltpu.roll(offset, step, 0), 0.0)
        offset = factor * before_o + offset
        factor = factor * before_f
        step *= 2
    return jnp.concatenate(
        [
            factor[layers - 1 :],
            offset[layers - 1 :],
            jnp.sum(factor * term, axis=0, keepdims=True),
            jnp.sum(offset * term, axis=0, keepdims=True),
        ],
        axis=0,
    )


def element_maps(tops, bots, params):
    layers = (params.shape[0] - 8) // 4
    thickness, rate, retention, weight = [
        params[i * layers : (i + 1) * layers] for i in range(4)
    ]
    stretch, shear = params[4 * layers : 4 * layers + 2], params[4 * layers + 2 : 4 * layers + 4]
    return group_maps(retention, weight, terms(tops, bots, stretch, shear, thickness, rate))


def physics_kernel(upper, lower, own, messages, corners, params, out):
    elems = corners.shape[1]
    layers = (params.shape[0] - 8) // 4
    rows = 4 * layers
    slot = messages.shape[2]
    slots = 4 * slot
    place, count = lax.axis_index("plane"), messages.shape[0]
    pieces = []
    for offset in OFFSETS:
        source = place + offset
        block = messages[jnp.clip(source, 0, count - 1)]
        valid = (source >= 0) & (source < count)
        pieces.append(jnp.where(valid, block, jnp.zeros_like(block)))
    got = jnp.concatenate(pieces, axis=1)
    ghost = got[:rows]
    ghost_low = got[4 * rows : 4 * rows + 4]
    blocks = slots // SPAN
    first = elems // SPAN
    table = jnp.concatenate([ghost[:, h * SPAN : (h + 1) * SPAN] for h in range(blocks)], axis=0)
    low_table = below_table(ghost_low)
    chunk = SPAN

    def step(i, _):
        at = pl.ds(pl.multiple_of(i * chunk, chunk), chunk)
        names = corners[0:1, at]
        low, high = names & (SPAN - 1), (names >> 8) - first
        hot = one_hot(low)
        is_ghost = high >= 0
        picked = choose(jnp.dot(table, hot, preferred_element_type=F32), high, rows)
        picked_low = choose(jnp.dot(low_table, hot, preferred_element_type=F32), high, 4)
        corner0 = jnp.where(is_ghost, picked, upper[:rows, at].astype(F32))
        low_rows = lower[:, at].astype(F32)
        low0 = jnp.where(is_ghost, picked_low, low_rows[:4])
        full = [corner0] + [upper[c * rows : (c + 1) * rows, at].astype(F32) for c in (1, 2, 3)]
        ends = [low0] + [low_rows[4 * c : 4 * c + 4] for c in (1, 2, 3)]
        for k in range(chunk // LANES):
            cut = slice(k * LANES, (k + 1) * LANES)
            here = pl.ds(pl.multiple_of(i * chunk + k * LANES, LANES), LANES)
            tops = [[f[m * layers : (m + 1) * layers, cut] for m in range(4)] for f in full]
            bots = [[e[m : m + 1, cut] for m in range(4)] for e in ends]
            out[:, here] = element_maps(tops, bots, params[:, here])
        return 0

    lax.fori_loop(0, elems // chunk, step, 0)

    mine = own[...].astype(F32)
    wide = got.astype(F32)
    base = 4 * rows + 16
    data = wide[base : base + 40] + wide[base + 40 : base + 80]
    for k in range(slots // LANES):
        cut = slice(k * LANES, (k + 1) * LANES)
        tops = [[mine[m * layers : (m + 1) * layers, cut] for m in range(4)]]
        bots = [[mine[rows + m : rows + m + 1, cut] for m in range(4)]]
        for c in (1, 2, 3):
            tops.append(
                [wide[c * rows + m * layers : c * rows + (m + 1) * layers, cut] for m in range(4)]
            )
            bots.append(
                [wide[4 * rows + 4 * c + m : 4 * rows + 4 * c + m + 1, cut] for m in range(4)]
            )
        out[:, elems + k * LANES : elems + (k + 1) * LANES] = element_maps(
            tops, bots, data[:, cut]
        )


def sum_kernel(earlier, later, corners, sends, out):
    elems = corners.shape[1]
    high_count = out.shape[0]
    chunk = min(512, elems)

    def add(total, names, values):
        width = names.shape[1]
        low, high = names & (LANES - 1), names >> 7
        coarse = values.astype(BF16).astype(F32)
        fine = values - coarse
        here = lax.broadcasted_iota(jnp.int32, (high_count, width), 0) == high
        left = jnp.concatenate([jnp.where(here, coarse, 0.0), jnp.where(here, fine, 0.0)], axis=0)
        hot = (lax.broadcasted_iota(jnp.int32, (LANES, width), 0) == low).astype(F32).astype(BF16)
        return total + lax.dot_general(left.astype(BF16), hot, NT, preferred_element_type=F32)

    def column(at):
        first, second = earlier[:, at], later[:, at]
        return 0.25 * (first[3:4] + second[3:4] + first[1:2] * second[2:3])

    def step(i, total):
        at = pl.ds(pl.multiple_of(i * chunk, chunk), chunk)
        values = column(at)
        for c in range(4):
            total = add(total, corners[c : c + 1, at], values)
        return total

    total = lax.fori_loop(0, elems // chunk, step, jnp.zeros((2 * high_count, LANES), F32))
    names = sends[...]
    values = column(pl.ds(elems, names.shape[1]))
    values = jnp.where(names < elems, values, 0.0)
    total = add(total, names, values)
    out[...] = total[:high_count] + total[high_count:]


def compose(one, two):
    return jnp.stack(
        [
            one[0] * two[0],
            two[0] * one[1] + two[1],
            one[2] + one[0] * two[2],
            one[3] + two[3] + one[1] * two[2],
        ]
    )


def shards(
    velocity, adjoint, corners, shared, stretch, shear_part, thickness, rate_factor, retention, weight
):
    layers, owned = velocity.shape[1:]
    elems = corners.shape[1]
    slot = shared.shape[1]
    slots = 4 * slot
    rows = 4 * layers
    shape = jax.ShapeDtypeStruct
    parts = lax.axis_size("plane")
    fields, top = kernel_call(
        level_kernel,
        (shape((rows, owned), BF16), shape((4, owned), BF16)),
        10**6,
        velocity, adjoint,
        spaces="far",
        scratch=(
            pltpu.VMEM(velocity.shape, BF16),
            pltpu.VMEM(adjoint.shape, BF16),
            pltpu.SemaphoreType.DMA((2,)),
        ),
    )
    below = shifted(top, "layer", -1)
    data, ids, params, names, sends = kernel_call(
        element_kernel,
        (
            shape((80, slots), BF16),
            shape((8, slots), jnp.int32),
            shape((rows + 8, elems), F32),
            shape(corners.shape, jnp.int32),
            shape((1, slots), jnp.int32),
        ),
        2 * 10**9,
        corners, shared, thickness, rate_factor, retention, weight, stretch, shear_part,
        spaces="far",
        scratch=(
            pltpu.VMEM(stretch.shape, F32),
            pltpu.VMEM(shear_part.shape, F32),
            pltpu.VMEM(shared.shape, jnp.int32),
            pltpu.SemaphoreType.DMA((8,)),
        ),
    )
    own, messages = kernel_call(
        message_kernel,
        (shape((rows + 16, slots), BF16), shape((parts, 4 * rows + 96, slot), BF16)),
        10**9,
        fields, below, sends, data, ids,
    )
    incoming = lax.all_to_all(messages, "plane", 0, 0)
    upper, lower = kernel_call(
        pick_kernel,
        (shape((4 * rows, elems), BF16), shape((16, elems), BF16)),
        8 * 10**9,
        fields, below, names,
    )
    state = kernel_call(
        physics_kernel,
        shape((4, elems + slots), F32),
        4 * 10**9,
        upper, lower, own, incoming, names, params,
    )
    groups, place = lax.axis_size("layer"), lax.axis_index("layer")
    step = 1
    earlier = later = state
    while step < groups:
        if step > 1:
            state = compose(earlier, later)
        other = lax.ppermute(state, "layer", [(i, i ^ step) for i in range(groups)])
        second = (place & step) != 0
        earlier, later = jnp.where(second, other, state), jnp.where(second, state, other)
        step *= 2
    gradient = kernel_call(
        sum_kernel,
        shape((owned // LANES, LANES), F32),
        2 * 10**9,
        earlier, later, names, sends,
    )
    return gradient.reshape(owned)


def solution(mesh):
    return jax.shard_map(
        shards,
        mesh=mesh,
        in_specs=(
            P(None, "layer", "plane"),
            P(None, "layer", "plane"),
            P(None, "plane"),
            P(None, "plane"),
            P(None, "plane"),
            P(None, "plane"),
            P("layer", "plane"),
            P("layer", "plane"),
            P("layer", "plane"),
            P("layer", "plane"),
        ),
        out_specs=P("plane"),
        check_vma=False,
    )
```

```python
import math

import jax
import jax.numpy as jnp
from jax import lax
from jax.experimental import pallas as pl
from jax.experimental.pallas import tpu as pltpu
from jax.sharding import PartitionSpec as P

OFFSETS = (-2, -1, 1, 2)
STRAIN_EPS = 0.01
GAUSS = 1.0 / math.sqrt(3.0)
SPAN = 256
LANES = 128
F32, BF16 = jnp.float32, jnp.bfloat16
NT = (((1,), (1,)), ((), ()))


def shifted(value, axis, steps):
    count = lax.axis_size(axis)
    first, last = (max(0, -steps), min(count, count - steps))
    return lax.ppermute(value, axis, [(source, source + steps) for source in range(first, last)])


def kernel_call(body, out_shape, flops, *args, spaces=None, scratch=()):
    vmem = pl.BlockSpec(memory_space=pltpu.VMEM)
    far = pl.BlockSpec(memory_space=pltpu.HBM)
    return pl.pallas_call(
        body,
        out_shape=out_shape,
        in_specs=[far if spaces == "far" else vmem for _ in args],
        out_specs=jax.tree.map(lambda _: vmem, out_shape),
        scratch_shapes=list(scratch),
        compiler_params=pltpu.CompilerParams(vmem_limit_bytes=48 * 2**20),
        cost_estimate=pl.CostEstimate(flops=flops, bytes_accessed=2**20, transcendentals=0),
    )(*args)


def node_table(fields):
    blocks = fields.shape[1] // SPAN
    return jnp.concatenate([fields[:, h * SPAN : (h + 1) * SPAN] for h in range(blocks)], axis=0)


def below_table(below):
    wide = below.astype(F32)
    blocks = wide.shape[1] // SPAN
    return jnp.concatenate(
        [wide[:, h * SPAN : (h + 1) * SPAN] for h in range(blocks)], axis=0
    ).astype(BF16)


def one_hot(low, dtype=BF16):
    width = low.shape[1]
    rows = lax.broadcasted_iota(jnp.int32, (SPAN, width), 0)
    return (rows == low).astype(F32).astype(dtype)


def choose(picked, high, rows):
    parts = [picked[i : i + rows] for i in range(0, picked.shape[0], rows)]
    bit = 1
    while len(parts) > 1:
        odd = (high & bit) != 0
        parts = [jnp.where(odd, parts[i + 1], parts[i]) for i in range(0, len(parts), 2)]
        bit *= 2
    return parts[0]


def pick_both(table, ids, rows):
    low, high = ids & (SPAN - 1), ids >> 8
    split = table.shape[0] * rows // (rows + 4)
    picked = jnp.dot(table, one_hot(low), preferred_element_type=F32)
    return choose(picked[:split], high, rows), choose(picked[split:], high, 4)


def fetch_kernel(
    velocity, adjoint, corners, shared, thickness, rate, retention, weight, stretch, shear,
    fields, top, params, names, sends,
    first, second, stretch_here, shear_here, shared_here, semaphores,
):
    layers, elems = thickness.shape
    pairs = [(velocity, first), (adjoint, second), (corners, names), (shared, shared_here)]
    pairs += [(stretch, stretch_here), (shear, shear_here)]
    for i, ref in enumerate((thickness, rate, retention, weight)):
        pairs.append((ref, params.at[pl.ds(i * layers, layers)]))
    copies = [
        pltpu.make_async_copy(source, target, semaphores.at[i])
        for i, (source, target) in enumerate(pairs)
    ]
    for copy in copies:
        copy.start()
    for copy in copies[:2]:
        copy.wait()
    parts = [first[0], first[1], second[0], second[1]]
    fields[...] = jnp.concatenate(parts, axis=0)
    wide = [part.astype(F32)[0:1] for part in parts]
    top[...] = jnp.concatenate(wide, axis=0).astype(BF16)
    for copy in copies[2:]:
        copy.wait()
    params[4 * layers :, :] = jnp.concatenate(
        [stretch_here[...], shear_here[...], jnp.zeros((4, elems), F32)], axis=0
    )
    sends[...] = jnp.concatenate([shared_here[j : j + 1, :] for j in range(4)], axis=1)


def element_kernel(params, names, data, ids):
    elems = names.shape[1]
    slots = data.shape[1]
    chunk = min(1024, elems)

    def step(i, total):
        at = pl.ds(pl.multiple_of(i * chunk, chunk), chunk)
        values = params[:, at]
        coarse = values.astype(BF16).astype(F32)
        here = names[:, at]
        rows = jnp.concatenate(
            [
                coarse,
                values - coarse,
                (here & (SPAN - 1)).astype(F32),
                (here >> 8).astype(F32),
                jnp.zeros((8, chunk), F32),
            ],
            axis=0,
        ).astype(BF16)
        wanted = lax.broadcasted_iota(jnp.int32, (slots, chunk), 0) + elems
        mine = (wanted == here[0:1]).astype(F32).astype(BF16)
        return total + lax.dot_general(rows, mine, NT, preferred_element_type=F32)

    total = lax.fori_loop(0, elems // chunk, step, jnp.zeros((96, slots), F32))
    data[...] = total[:80].astype(BF16)
    ids[...] = total[80:88].astype(jnp.int32)


def message_kernel(fields, below, sends, data, ids, own, messages):
    rows = fields.shape[0]
    table = jnp.concatenate([node_table(fields), below_table(below[...])], axis=0)
    slot = messages.shape[2]
    lists = [sends[...]]
    lists += [ids[c : c + 1, :] + ids[4 + c : 5 + c, :] * SPAN for c in (1, 2, 3)]
    upper, lower = zip(*[pick_both(table, names, rows) for names in lists])
    bottom = jnp.concatenate(lower, axis=0)
    own[...] = jnp.concatenate([upper[0], bottom], axis=0).astype(BF16)
    everything = jnp.concatenate(list(upper) + [bottom], axis=0).astype(BF16)
    place, count = lax.axis_index("plane"), messages.shape[0]
    for j, offset in enumerate(OFFSETS):
        at = slice(j * slot, (j + 1) * slot)
        target = place + offset

        @pl.when((target >= 0) & (target < count))
        def _():
            messages[target, : 4 * rows + 16, :] = everything[:, at]
            messages[target, 4 * rows + 16 :, :] = data[:, at]


def pick_kernel(fields, below, corners, upper, lower):
    rows = fields.shape[0]
    table = jnp.concatenate([node_table(fields), below_table(below[...])], axis=0)
    elems = corners.shape[1]
    chunk = min(1024, elems)

    def step(i, _):
        at = pl.ds(pl.multiple_of(i * chunk, chunk), chunk)
        bottom = []
        for c in range(4):
            picked, ends = pick_both(table, corners[c : c + 1, at], rows)
            upper[c * rows : (c + 1) * rows, at] = picked.astype(BF16)
            bottom.append(ends)
        lower[:, at] = jnp.concatenate(bottom, axis=0).astype(BF16)
        return 0

    lax.fori_loop(0, elems // chunk, step, 0)


def plane_modes(a0, a1, a2, a3):
    s01, d01, s23, d23 = a0 + a1, a1 - a0, a2 + a3, a2 - a3
    return s01 + s23, d01 + d23, s23 - s01, d23 - d01


def terms(upper, bottom, stretch, shear, thickness, rate):
    layers, n = thickness.shape
    last = lax.broadcasted_iota(jnp.int32, (layers, n), 0) == layers - 1
    plus, minus, depth = [], [], []
    for comp in range(4):
        top = plane_modes(*[upper[c][comp] for c in range(4)])
        end = plane_modes(*[bottom[c][comp] for c in range(4)])
        under = [
            jnp.where(last, jnp.broadcast_to(e, t.shape), pltpu.roll(t, layers - 1, 0))
            for t, e in zip(top, end)
        ]
        depth_parts = [top[0] - under[0]]
        plus_parts, minus_parts = [], []
        for t, u in zip(top[1:], under[1:]):
            total, half = t + u, GAUSS * (t - u)
            plus_parts.append(total + half)
            minus_parts.append(total - half)
            depth_parts.append(half)
        plus.append(plus_parts)
        minus.append(minus_parts)
        depth.append(depth_parts)
    s0, s1 = stretch[0:1] * (1.0 / 16.0), stretch[1:2] * (1.0 / 16.0)
    h0, h1 = shear[0:1] * (1.0 / 16.0), shear[1:2] * (1.0 / 16.0)
    gs0, gs1, gh0, gh1 = s0 * GAUSS, s1 * GAUSS, h0 * GAUSS, h1 * GAUSS

    def plane_fields(part, first):
        (xa, ya, wa), (xb, yb, wb) = part[first], part[first + 1]
        p1, p2 = s0 * xa + h0 * ya, h1 * xb + s1 * yb
        x1, x2 = gh0 * wa, gs1 * wb
        y1, y2 = gs0 * wa, gh1 * wb
        return (
            (p1 + p2, x1 + x2, y1 + y2),
            (p1 - p2, x1 - x2, y1 - y2),
            (
                (h1 * xa + s1 * ya) + (s0 * xb + h0 * yb),
                gs1 * wa + gh0 * wb,
                gh1 * wa + gs0 * wb,
            ),
        )

    def four(field):
        base, along_x, along_y = field
        up, um = base + along_x, base - along_x
        return up + along_y, up - along_y, um + along_y, um - along_y

    inverse = 0.125 / thickness
    inverse_g = inverse * GAUSS

    def depth_four(parts):
        q0, qx, qy, qw = (
            parts[0] * inverse,
            parts[1] * inverse,
            parts[2] * inverse,
            parts[3] * inverse_g,
        )
        p, m, r, t = q0 + qx, q0 - qx, qy + qw, qy - qw
        return p + r, p - r, m + t, m - t

    za, zb, zc, zd = [depth_four(depth[comp]) for comp in range(4)]
    shear_ff = [za[k] * za[k] + zb[k] * zb[k] + STRAIN_EPS for k in range(4)]
    shear_fa = [za[k] * zc[k] + zb[k] * zd[k] for k in range(4)]
    total = None
    for part in (plus, minus):
        flow = [four(f) for f in plane_fields(part, 0)]
        other = [four(f) for f in plane_fields(part, 2)]
        for k in range(4):
            s, d, x = flow[0][k], flow[1][k], flow[2][k]
            triple = 3.0 * s
            effective = (triple * s + d * d) + (x * x + shear_ff[k])
            paired = (triple * other[0][k] + d * other[1][k]) + (x * other[2][k] + shear_fa[k])
            value = jnp.exp(jnp.log(effective) * (-1.0 / 3.0)) * paired
            total = value if total is None else total + value
    det = stretch[0:1] * stretch[1:2] - shear[0:1] * shear[1:2]
    return total * (rate * thickness / det)


def group_maps(retention, weight, term):
    layers, n = retention.shape
    row = lax.broadcasted_iota(jnp.int32, (layers, n), 0)
    factor, offset = retention, (1.0 - retention) * weight
    step = 1
    while step < layers:
        seen = row >= step
        before_f = jnp.where(seen, pltpu.roll(factor, step, 0), 1.0)
        before_o = jnp.where(seen, pltpu.roll(offset, step, 0), 0.0)
        offset = factor * before_o + offset
        factor = factor * before_f
        step *= 2
    return jnp.concatenate(
        [
            factor[layers - 1 :],
            offset[layers - 1 :],
            jnp.sum(factor * term, axis=0, keepdims=True),
            jnp.sum(offset * term, axis=0, keepdims=True),
        ],
        axis=0,
    )


def element_maps(tops, bots, params):
    layers = (params.shape[0] - 8) // 4
    thickness, rate, retention, weight = [
        params[i * layers : (i + 1) * layers] for i in range(4)
    ]
    stretch, shear = params[4 * layers : 4 * layers + 2], params[4 * layers + 2 : 4 * layers + 4]
    return group_maps(retention, weight, terms(tops, bots, stretch, shear, thickness, rate))


def physics_kernel(upper, lower, own, messages, corners, params, out):
    elems = corners.shape[1]
    layers = (params.shape[0] - 8) // 4
    rows = 4 * layers
    slot = messages.shape[2]
    slots = 4 * slot
    place, count = lax.axis_index("plane"), messages.shape[0]
    pieces = []
    for offset in OFFSETS:
        source = place + offset
        block = messages[jnp.clip(source, 0, count - 1)]
        valid = (source >= 0) & (source < count)
        pieces.append(jnp.where(valid, block, jnp.zeros_like(block)))
    got = jnp.concatenate(pieces, axis=1)
    ghost = got[:rows]
    ghost_low = got[4 * rows : 4 * rows + 4]
    blocks = slots // SPAN
    first = elems // SPAN
    table = jnp.concatenate([ghost[:, h * SPAN : (h + 1) * SPAN] for h in range(blocks)], axis=0)
    low_table = below_table(ghost_low)
    chunk = SPAN

    def step(i, _):
        at = pl.ds(pl.multiple_of(i * chunk, chunk), chunk)
        names = corners[0:1, at]
        low, high = names & (SPAN - 1), (names >> 8) - first
        hot = one_hot(low)
        is_ghost = high >= 0
        picked = choose(jnp.dot(table, hot, preferred_element_type=F32), high, rows)
        picked_low = choose(jnp.dot(low_table, hot, preferred_element_type=F32), high, 4)
        corner0 = jnp.where(is_ghost, picked, upper[:rows, at].astype(F32))
        low_rows = lower[:, at].astype(F32)
        low0 = jnp.where(is_ghost, picked_low, low_rows[:4])
        full = [corner0] + [upper[c * rows : (c + 1) * rows, at].astype(F32) for c in (1, 2, 3)]
        ends = [low0] + [low_rows[4 * c : 4 * c + 4] for c in (1, 2, 3)]
        for k in range(chunk // LANES):
            cut = slice(k * LANES, (k + 1) * LANES)
            here = pl.ds(pl.multiple_of(i * chunk + k * LANES, LANES), LANES)
            tops = [[f[m * layers : (m + 1) * layers, cut] for m in range(4)] for f in full]
            bots = [[e[m : m + 1, cut] for m in range(4)] for e in ends]
            out[:, here] = element_maps(tops, bots, params[:, here])
        return 0

    lax.fori_loop(0, elems // chunk, step, 0)

    mine = own[...].astype(F32)
    wide = got.astype(F32)
    base = 4 * rows + 16
    data = wide[base : base + 40] + wide[base + 40 : base + 80]
    for k in range(slots // LANES):
        cut = slice(k * LANES, (k + 1) * LANES)
        tops = [[mine[m * layers : (m + 1) * layers, cut] for m in range(4)]]
        bots = [[mine[rows + m : rows + m + 1, cut] for m in range(4)]]
        for c in (1, 2, 3):
            tops.append(
                [wide[c * rows + m * layers : c * rows + (m + 1) * layers, cut] for m in range(4)]
            )
            bots.append(
                [wide[4 * rows + 4 * c + m : 4 * rows + 4 * c + m + 1, cut] for m in range(4)]
            )
        out[:, elems + k * LANES : elems + (k + 1) * LANES] = element_maps(
            tops, bots, data[:, cut]
        )


def sum_kernel(earlier, later, corners, sends, out):
    elems = corners.shape[1]
    high_count = out.shape[0]
    chunk = min(512, elems)

    def add(total, names, values):
        width = names.shape[1]
        low, high = names & (LANES - 1), names >> 7
        coarse = values.astype(BF16).astype(F32)
        fine = values - coarse
        here = lax.broadcasted_iota(jnp.int32, (high_count, width), 0) == high
        left = jnp.concatenate([jnp.where(here, coarse, 0.0), jnp.where(here, fine, 0.0)], axis=0)
        hot = (lax.broadcasted_iota(jnp.int32, (LANES, width), 0) == low).astype(F32).astype(BF16)
        return total + lax.dot_general(left.astype(BF16), hot, NT, preferred_element_type=F32)

    def column(at):
        first, second = earlier[:, at], later[:, at]
        return 0.25 * (first[3:4] + second[3:4] + first[1:2] * second[2:3])

    def step(i, total):
        at = pl.ds(pl.multiple_of(i * chunk, chunk), chunk)
        values = column(at)
        for c in range(4):
            total = add(total, corners[c : c + 1, at], values)
        return total

    total = lax.fori_loop(0, elems // chunk, step, jnp.zeros((2 * high_count, LANES), F32))
    names = sends[...]
    values = column(pl.ds(elems, names.shape[1]))
    values = jnp.where(names < elems, values, 0.0)
    total = add(total, names, values)
    out[...] = total[:high_count] + total[high_count:]


def compose(one, two):
    return jnp.stack(
        [
            one[0] * two[0],
            two[0] * one[1] + two[1],
            one[2] + one[0] * two[2],
            one[3] + two[3] + one[1] * two[2],
        ]
    )


def shards(
    velocity, adjoint, corners, shared, stretch, shear_part, thickness, rate_factor, retention, weight
):
    layers, owned = velocity.shape[1:]
    elems = corners.shape[1]
    slot = shared.shape[1]
    slots = 4 * slot
    rows = 4 * layers
    shape = jax.ShapeDtypeStruct
    parts = lax.axis_size("plane")
    fields, top, params, names, sends = kernel_call(
        fetch_kernel,
        (
            shape((rows, owned), BF16),
            shape((4, owned), BF16),
            shape((rows + 8, elems), F32),
            shape(corners.shape, jnp.int32),
            shape((1, slots), jnp.int32),
        ),
        10**6,
        velocity, adjoint, corners, shared, thickness, rate_factor, retention, weight, stretch, shear_part,
        spaces="far",
        scratch=(
            pltpu.VMEM(velocity.shape, BF16),
            pltpu.VMEM(adjoint.shape, BF16),
            pltpu.VMEM(stretch.shape, F32),
            pltpu.VMEM(shear_part.shape, F32),
            pltpu.VMEM(shared.shape, jnp.int32),
            pltpu.SemaphoreType.DMA((10,)),
        ),
    )
    below = shifted(top, "layer", -1)
    data, ids = kernel_call(
        element_kernel,
        (shape((80, slots), BF16), shape((8, slots), jnp.int32)),
        2 * 10**9,
        params, names,
    )
    own, messages = kernel_call(
        message_kernel,
        (shape((rows + 16, slots), BF16), shape((parts, 4 * rows + 96, slot), BF16)),
        10**9,
        fields, below, sends, data, ids,
    )
    incoming = lax.all_to_all(messages, "plane", 0, 0)
    upper, lower = kernel_call(
        pick_kernel,
        (shape((4 * rows, elems), BF16), shape((16, elems), BF16)),
        8 * 10**9,
        fields, below, names,
    )
    state = kernel_call(
        physics_kernel,
        shape((4, elems + slots), F32),
        4 * 10**9,
        upper, lower, own, incoming, names, params,
    )
    groups, place = lax.axis_size("layer"), lax.axis_index("layer")
    step = 1
    earlier = later = state
    while step < groups:
        if step > 1:
            state = compose(earlier, later)
        other = lax.ppermute(state, "layer", [(i, i ^ step) for i in range(groups)])
        second = (place & step) != 0
        earlier, later = jnp.where(second, other, state), jnp.where(second, state, other)
        step *= 2
    gradient = kernel_call(
        sum_kernel,
        shape((owned // LANES, LANES), F32),
        2 * 10**9,
        earlier, later, names, sends,
    )
    return gradient.reshape(owned)


def solution(mesh):
    return jax.shard_map(
        shards,
        mesh=mesh,
        in_specs=(
            P(None, "layer", "plane"),
            P(None, "layer", "plane"),
            P(None, "plane"),
            P(None, "plane"),
            P(None, "plane"),
            P(None, "plane"),
            P("layer", "plane"),
            P("layer", "plane"),
            P("layer", "plane"),
            P("layer", "plane"),
        ),
        out_specs=P("plane"),
        check_vma=False,
    )
```

```python
import math

import jax
import jax.numpy as jnp
from jax import lax
from jax.experimental import pallas as pl
from jax.experimental.pallas import tpu as pltpu
from jax.sharding import PartitionSpec as P

OFFSETS = (-2, -1, 1, 2)
STRAIN_EPS = 0.01
GAUSS = 1.0 / math.sqrt(3.0)
SPAN = 256
LANES = 128
F32, BF16 = jnp.float32, jnp.bfloat16
NT = (((1,), (1,)), ((), ()))


def shifted(value, axis, steps):
    count = lax.axis_size(axis)
    first, last = (max(0, -steps), min(count, count - steps))
    return lax.ppermute(value, axis, [(source, source + steps) for source in range(first, last)])


def kernel_call(body, out_shape, flops, *args, spaces=None, scratch=()):
    vmem = pl.BlockSpec(memory_space=pltpu.VMEM)
    far = pl.BlockSpec(memory_space=pltpu.HBM)
    if spaces == "far":
        args = [pltpu.with_memory_space_constraint(value, pltpu.HBM) for value in args]
    return pl.pallas_call(
        body,
        out_shape=out_shape,
        in_specs=[far if spaces == "far" else vmem for _ in args],
        out_specs=jax.tree.map(lambda _: vmem, out_shape),
        scratch_shapes=list(scratch),
        compiler_params=pltpu.CompilerParams(vmem_limit_bytes=48 * 2**20),
        cost_estimate=pl.CostEstimate(flops=flops, bytes_accessed=2**20, transcendentals=0),
    )(*args)


def node_table(fields):
    blocks = fields.shape[1] // SPAN
    return jnp.concatenate([fields[:, h * SPAN : (h + 1) * SPAN] for h in range(blocks)], axis=0)


def below_table(below):
    wide = below.astype(F32)
    blocks = wide.shape[1] // SPAN
    return jnp.concatenate(
        [wide[:, h * SPAN : (h + 1) * SPAN] for h in range(blocks)], axis=0
    ).astype(BF16)


def one_hot(low, dtype=BF16):
    width = low.shape[1]
    rows = lax.broadcasted_iota(jnp.int32, (SPAN, width), 0)
    return (rows == low).astype(F32).astype(dtype)


def choose(picked, high, rows):
    parts = [picked[i : i + rows] for i in range(0, picked.shape[0], rows)]
    bit = 1
    while len(parts) > 1:
        odd = (high & bit) != 0
        parts = [jnp.where(odd, parts[i + 1], parts[i]) for i in range(0, len(parts), 2)]
        bit *= 2
    return parts[0]


def pick_both(table, ids, rows):
    low, high = ids & (SPAN - 1), ids >> 8
    split = table.shape[0] * rows // (rows + 4)
    picked = jnp.dot(table, one_hot(low), preferred_element_type=F32)
    return choose(picked[:split], high, rows), choose(picked[split:], high, 4)


def fetch_kernel(
    velocity, adjoint, corners, shared, thickness, rate, retention, weight, stretch, shear,
    fields, top, params, names, sends,
    first, second, stretch_here, shear_here, shared_here, semaphores,
):
    layers, elems = thickness.shape
    pairs = [(velocity, first), (adjoint, second), (corners, names), (shared, shared_here)]
    pairs += [(stretch, stretch_here), (shear, shear_here)]
    for i, ref in enumerate((thickness, rate, retention, weight)):
        pairs.append((ref, params.at[pl.ds(i * layers, layers)]))
    copies = [
        pltpu.make_async_copy(source, target, semaphores.at[i])
        for i, (source, target) in enumerate(pairs)
    ]
    for copy in copies:
        copy.start()
    for copy in copies[:2]:
        copy.wait()
    parts = [first[0], first[1], second[0], second[1]]
    fields[...] = jnp.concatenate(parts, axis=0)
    wide = [part.astype(F32)[0:1] for part in parts]
    top[...] = jnp.concatenate(wide, axis=0).astype(BF16)
    for copy in copies[2:]:
        copy.wait()
    params[4 * layers :, :] = jnp.concatenate(
        [stretch_here[...], shear_here[...], jnp.zeros((4, elems), F32)], axis=0
    )
    sends[...] = jnp.concatenate([shared_here[j : j + 1, :] for j in range(4)], axis=1)


def element_kernel(params, names, data, ids):
    elems = names.shape[1]
    slots = data.shape[1]
    chunk = min(1024, elems)

    def step(i, total):
        at = pl.ds(pl.multiple_of(i * chunk, chunk), chunk)
        values = params[:, at]
        coarse = values.astype(BF16).astype(F32)
        here = names[:, at]
        rows = jnp.concatenate(
            [
                coarse,
                values - coarse,
                (here & (SPAN - 1)).astype(F32),
                (here >> 8).astype(F32),
                jnp.zeros((8, chunk), F32),
            ],
            axis=0,
        ).astype(BF16)
        wanted = lax.broadcasted_iota(jnp.int32, (slots, chunk), 0) + elems
        mine = (wanted == here[0:1]).astype(F32).astype(BF16)
        return total + lax.dot_general(rows, mine, NT, preferred_element_type=F32)

    total = lax.fori_loop(0, elems // chunk, step, jnp.zeros((96, slots), F32))
    data[...] = total[:80].astype(BF16)
    ids[...] = total[80:88].astype(jnp.int32)


def message_kernel(fields, below, sends, data, ids, own, messages):
    rows = fields.shape[0]
    table = jnp.concatenate([node_table(fields), below_table(below[...])], axis=0)
    slot = messages.shape[2]
    lists = [sends[...]]
    lists += [ids[c : c + 1, :] + ids[4 + c : 5 + c, :] * SPAN for c in (1, 2, 3)]
    upper, lower = zip(*[pick_both(table, names, rows) for names in lists])
    bottom = jnp.concatenate(lower, axis=0)
    own[...] = jnp.concatenate([upper[0], bottom], axis=0).astype(BF16)
    everything = jnp.concatenate(list(upper) + [bottom], axis=0).astype(BF16)
    place, count = lax.axis_index("plane"), messages.shape[0]
    for j, offset in enumerate(OFFSETS):
        at = slice(j * slot, (j + 1) * slot)
        target = place + offset

        @pl.when((target >= 0) & (target < count))
        def _():
            messages[target, : 4 * rows + 16, :] = everything[:, at]
            messages[target, 4 * rows + 16 :, :] = data[:, at]


def pick_kernel(fields, below, corners, upper, lower):
    rows = fields.shape[0]
    table = jnp.concatenate([node_table(fields), below_table(below[...])], axis=0)
    elems = corners.shape[1]
    chunk = min(1024, elems)

    def step(i, _):
        at = pl.ds(pl.multiple_of(i * chunk, chunk), chunk)
        bottom = []
        for c in range(4):
            picked, ends = pick_both(table, corners[c : c + 1, at], rows)
            upper[c * rows : (c + 1) * rows, at] = picked.astype(BF16)
            bottom.append(ends)
        lower[:, at] = jnp.concatenate(bottom, axis=0).astype(BF16)
        return 0

    lax.fori_loop(0, elems // chunk, step, 0)


def plane_modes(a0, a1, a2, a3):
    s01, d01, s23, d23 = a0 + a1, a1 - a0, a2 + a3, a2 - a3
    return s01 + s23, d01 + d23, s23 - s01, d23 - d01


def terms(upper, bottom, stretch, shear, thickness, rate):
    layers, n = thickness.shape
    last = lax.broadcasted_iota(jnp.int32, (layers, n), 0) == layers - 1
    plus, minus, depth = [], [], []
    for comp in range(4):
        top = plane_modes(*[upper[c][comp] for c in range(4)])
        end = plane_modes(*[bottom[c][comp] for c in range(4)])
        under = [
            jnp.where(last, jnp.broadcast_to(e, t.shape), pltpu.roll(t, layers - 1, 0))
            for t, e in zip(top, end)
        ]
        depth_parts = [top[0] - under[0]]
        plus_parts, minus_parts = [], []
        for t, u in zip(top[1:], under[1:]):
            total, half = t + u, GAUSS * (t - u)
            plus_parts.append(total + half)
            minus_parts.append(total - half)
            depth_parts.append(half)
        plus.append(plus_parts)
        minus.append(minus_parts)
        depth.append(depth_parts)
    s0, s1 = stretch[0:1] * (1.0 / 16.0), stretch[1:2] * (1.0 / 16.0)
    h0, h1 = shear[0:1] * (1.0 / 16.0), shear[1:2] * (1.0 / 16.0)
    gs0, gs1, gh0, gh1 = s0 * GAUSS, s1 * GAUSS, h0 * GAUSS, h1 * GAUSS

    def plane_fields(part, first):
        (xa, ya, wa), (xb, yb, wb) = part[first], part[first + 1]
        p1, p2 = s0 * xa + h0 * ya, h1 * xb + s1 * yb
        x1, x2 = gh0 * wa, gs1 * wb
        y1, y2 = gs0 * wa, gh1 * wb
        return (
            (p1 + p2, x1 + x2, y1 + y2),
            (p1 - p2, x1 - x2, y1 - y2),
            (
                (h1 * xa + s1 * ya) + (s0 * xb + h0 * yb),
                gs1 * wa + gh0 * wb,
                gh1 * wa + gs0 * wb,
            ),
        )

    def four(field):
        base, along_x, along_y = field
        up, um = base + along_x, base - along_x
        return up + along_y, up - along_y, um + along_y, um - along_y

    inverse = 0.125 / thickness
    inverse_g = inverse * GAUSS

    def depth_four(parts):
        q0, qx, qy, qw = (
            parts[0] * inverse,
            parts[1] * inverse,
            parts[2] * inverse,
            parts[3] * inverse_g,
        )
        p, m, r, t = q0 + qx, q0 - qx, qy + qw, qy - qw
        return p + r, p - r, m + t, m - t

    za, zb, zc, zd = [depth_four(depth[comp]) for comp in range(4)]
    shear_ff = [za[k] * za[k] + zb[k] * zb[k] + STRAIN_EPS for k in range(4)]
    shear_fa = [za[k] * zc[k] + zb[k] * zd[k] for k in range(4)]
    total = None
    for part in (plus, minus):
        flow = [four(f) for f in plane_fields(part, 0)]
        other = [four(f) for f in plane_fields(part, 2)]
        for k in range(4):
            s, d, x = flow[0][k], flow[1][k], flow[2][k]
            triple = 3.0 * s
            effective = (triple * s + d * d) + (x * x + shear_ff[k])
            paired = (triple * other[0][k] + d * other[1][k]) + (x * other[2][k] + shear_fa[k])
            value = jnp.exp(jnp.log(effective) * (-1.0 / 3.0)) * paired
            total = value if total is None else total + value
    det = stretch[0:1] * stretch[1:2] - shear[0:1] * shear[1:2]
    return total * (rate * thickness / det)


def group_maps(retention, weight, term):
    layers, n = retention.shape
    row = lax.broadcasted_iota(jnp.int32, (layers, n), 0)
    factor, offset = retention, (1.0 - retention) * weight
    step = 1
    while step < layers:
        seen = row >= step
        before_f = jnp.where(seen, pltpu.roll(factor, step, 0), 1.0)
        before_o = jnp.where(seen, pltpu.roll(offset, step, 0), 0.0)
        offset = factor * before_o + offset
        factor = factor * before_f
        step *= 2
    return jnp.concatenate(
        [
            factor[layers - 1 :],
            offset[layers - 1 :],
            jnp.sum(factor * term, axis=0, keepdims=True),
            jnp.sum(offset * term, axis=0, keepdims=True),
        ],
        axis=0,
    )


def element_maps(tops, bots, params):
    layers = (params.shape[0] - 8) // 4
    thickness, rate, retention, weight = [
        params[i * layers : (i + 1) * layers] for i in range(4)
    ]
    stretch, shear = params[4 * layers : 4 * layers + 2], params[4 * layers + 2 : 4 * layers + 4]
    return group_maps(retention, weight, terms(tops, bots, stretch, shear, thickness, rate))


def physics_kernel(upper, lower, own, messages, corners, params, out):
    elems = corners.shape[1]
    layers = (params.shape[0] - 8) // 4
    rows = 4 * layers
    slot = messages.shape[2]
    slots = 4 * slot
    place, count = lax.axis_index("plane"), messages.shape[0]
    pieces = []
    for offset in OFFSETS:
        source = place + offset
        block = messages[jnp.clip(source, 0, count - 1)]
        valid = (source >= 0) & (source < count)
        pieces.append(jnp.where(valid, block, jnp.zeros_like(block)))
    got = jnp.concatenate(pieces, axis=1)
    ghost = got[:rows]
    ghost_low = got[4 * rows : 4 * rows + 4]
    blocks = slots // SPAN
    first = elems // SPAN
    table = jnp.concatenate([ghost[:, h * SPAN : (h + 1) * SPAN] for h in range(blocks)], axis=0)
    low_table = below_table(ghost_low)
    chunk = SPAN

    def step(i, _):
        at = pl.ds(pl.multiple_of(i * chunk, chunk), chunk)
        names = corners[0:1, at]
        low, high = names & (SPAN - 1), (names >> 8) - first
        hot = one_hot(low)
        is_ghost = high >= 0
        picked = choose(jnp.dot(table, hot, preferred_element_type=F32), high, rows)
        picked_low = choose(jnp.dot(low_table, hot, preferred_element_type=F32), high, 4)
        corner0 = jnp.where(is_ghost, picked, upper[:rows, at].astype(F32))
        low_rows = lower[:, at].astype(F32)
        low0 = jnp.where(is_ghost, picked_low, low_rows[:4])
        full = [corner0] + [upper[c * rows : (c + 1) * rows, at].astype(F32) for c in (1, 2, 3)]
        ends = [low0] + [low_rows[4 * c : 4 * c + 4] for c in (1, 2, 3)]
        for k in range(chunk // LANES):
            cut = slice(k * LANES, (k + 1) * LANES)
            here = pl.ds(pl.multiple_of(i * chunk + k * LANES, LANES), LANES)
            tops = [[f[m * layers : (m + 1) * layers, cut] for m in range(4)] for f in full]
            bots = [[e[m : m + 1, cut] for m in range(4)] for e in ends]
            out[:, here] = element_maps(tops, bots, params[:, here])
        return 0

    lax.fori_loop(0, elems // chunk, step, 0)

    mine = own[...].astype(F32)
    wide = got.astype(F32)
    base = 4 * rows + 16
    data = wide[base : base + 40] + wide[base + 40 : base + 80]
    for k in range(slots // LANES):
        cut = slice(k * LANES, (k + 1) * LANES)
        tops = [[mine[m * layers : (m + 1) * layers, cut] for m in range(4)]]
        bots = [[mine[rows + m : rows + m + 1, cut] for m in range(4)]]
        for c in (1, 2, 3):
            tops.append(
                [wide[c * rows + m * layers : c * rows + (m + 1) * layers, cut] for m in range(4)]
            )
            bots.append(
                [wide[4 * rows + 4 * c + m : 4 * rows + 4 * c + m + 1, cut] for m in range(4)]
            )
        out[:, elems + k * LANES : elems + (k + 1) * LANES] = element_maps(
            tops, bots, data[:, cut]
        )


def sum_kernel(earlier, later, corners, sends, out):
    elems = corners.shape[1]
    high_count = out.shape[0]
    chunk = min(512, elems)

    def add(total, names, values):
        width = names.shape[1]
        low, high = names & (LANES - 1), names >> 7
        coarse = values.astype(BF16).astype(F32)
        fine = values - coarse
        here = lax.broadcasted_iota(jnp.int32, (high_count, width), 0) == high
        left = jnp.concatenate([jnp.where(here, coarse, 0.0), jnp.where(here, fine, 0.0)], axis=0)
        hot = (lax.broadcasted_iota(jnp.int32, (LANES, width), 0) == low).astype(F32).astype(BF16)
        return total + lax.dot_general(left.astype(BF16), hot, NT, preferred_element_type=F32)

    def column(at):
        first, second = earlier[:, at], later[:, at]
        return 0.25 * (first[3:4] + second[3:4] + first[1:2] * second[2:3])

    def step(i, total):
        at = pl.ds(pl.multiple_of(i * chunk, chunk), chunk)
        values = column(at)
        for c in range(4):
            total = add(total, corners[c : c + 1, at], values)
        return total

    total = lax.fori_loop(0, elems // chunk, step, jnp.zeros((2 * high_count, LANES), F32))
    names = sends[...]
    values = column(pl.ds(elems, names.shape[1]))
    values = jnp.where(names < elems, values, 0.0)
    total = add(total, names, values)
    out[...] = total[:high_count] + total[high_count:]


def compose(one, two):
    return jnp.stack(
        [
            one[0] * two[0],
            two[0] * one[1] + two[1],
            one[2] + one[0] * two[2],
            one[3] + two[3] + one[1] * two[2],
        ]
    )


def shards(
    velocity, adjoint, corners, shared, stretch, shear_part, thickness, rate_factor, retention, weight
):
    layers, owned = velocity.shape[1:]
    elems = corners.shape[1]
    slot = shared.shape[1]
    slots = 4 * slot
    rows = 4 * layers
    shape = jax.ShapeDtypeStruct
    parts = lax.axis_size("plane")
    fields, top, params, names, sends = kernel_call(
        fetch_kernel,
        (
            shape((rows, owned), BF16),
            shape((4, owned), BF16),
            shape((rows + 8, elems), F32),
            shape(corners.shape, jnp.int32),
            shape((1, slots), jnp.int32),
        ),
        10**6,
        velocity, adjoint, corners, shared, thickness, rate_factor, retention, weight, stretch, shear_part,
        spaces="far",
        scratch=(
            pltpu.VMEM(velocity.shape, BF16),
            pltpu.VMEM(adjoint.shape, BF16),
            pltpu.VMEM(stretch.shape, F32),
            pltpu.VMEM(shear_part.shape, F32),
            pltpu.VMEM(shared.shape, jnp.int32),
            pltpu.SemaphoreType.DMA((10,)),
        ),
    )
    below = shifted(top, "layer", -1)
    data, ids = kernel_call(
        element_kernel,
        (shape((80, slots), BF16), shape((8, slots), jnp.int32)),
        2 * 10**9,
        params, names,
    )
    own, messages = kernel_call(
        message_kernel,
        (shape((rows + 16, slots), BF16), shape((parts, 4 * rows + 96, slot), BF16)),
        10**9,
        fields, below, sends, data, ids,
    )
    incoming = lax.all_to_all(messages, "plane", 0, 0)
    upper, lower = kernel_call(
        pick_kernel,
        (shape((4 * rows, elems), BF16), shape((16, elems), BF16)),
        8 * 10**9,
        fields, below, names,
    )
    state = kernel_call(
        physics_kernel,
        shape((4, elems + slots), F32),
        4 * 10**9,
        upper, lower, own, incoming, names, params,
    )
    groups, place = lax.axis_size("layer"), lax.axis_index("layer")
    step = 1
    earlier = later = state
    while step < groups:
        if step > 1:
            state = compose(earlier, later)
        other = lax.ppermute(state, "layer", [(i, i ^ step) for i in range(groups)])
        second = (place & step) != 0
        earlier, later = jnp.where(second, other, state), jnp.where(second, state, other)
        step *= 2
    gradient = kernel_call(
        sum_kernel,
        shape((owned // LANES, LANES), F32),
        2 * 10**9,
        earlier, later, names, sends,
    )
    return gradient.reshape(owned)


def solution(mesh):
    return jax.shard_map(
        shards,
        mesh=mesh,
        in_specs=(
            P(None, "layer", "plane"),
            P(None, "layer", "plane"),
            P(None, "plane"),
            P(None, "plane"),
            P(None, "plane"),
            P(None, "plane"),
            P("layer", "plane"),
            P("layer", "plane"),
            P("layer", "plane"),
            P("layer", "plane"),
        ),
        out_specs=P("plane"),
        check_vma=False,
    )
```

```python
import math

import jax
import jax.numpy as jnp
from jax import lax
from jax.experimental import pallas as pl
from jax.experimental.pallas import tpu as pltpu
from jax.sharding import PartitionSpec as P

OFFSETS = (-2, -1, 1, 2)
STRAIN_EPS = 0.01
GAUSS = 1.0 / math.sqrt(3.0)
SPAN = 256
LANES = 128
F32, BF16 = jnp.float32, jnp.bfloat16
NT = (((1,), (1,)), ((), ()))


def shifted(value, axis, steps):
    count = lax.axis_size(axis)
    first, last = (max(0, -steps), min(count, count - steps))
    return lax.ppermute(value, axis, [(source, source + steps) for source in range(first, last)])


def kernel_call(body, out_shape, flops, *args, spaces=None, scratch=()):
    vmem = pl.BlockSpec(memory_space=pltpu.VMEM)
    far = pl.BlockSpec(memory_space=pltpu.HBM)
    if spaces == "far":
        args = [pltpu.with_memory_space_constraint(value, pltpu.HBM) for value in args]
    return pl.pallas_call(
        body,
        out_shape=out_shape,
        in_specs=[far if spaces == "far" else vmem for _ in args],
        out_specs=jax.tree.map(lambda _: vmem, out_shape),
        scratch_shapes=list(scratch),
        compiler_params=pltpu.CompilerParams(vmem_limit_bytes=48 * 2**20),
        cost_estimate=pl.CostEstimate(flops=flops, bytes_accessed=2**20, transcendentals=0),
    )(*args)


def node_table(fields):
    blocks = fields.shape[1] // SPAN
    return jnp.concatenate([fields[:, h * SPAN : (h + 1) * SPAN] for h in range(blocks)], axis=0)


def below_table(below):
    wide = below.astype(F32)
    blocks = wide.shape[1] // SPAN
    return jnp.concatenate(
        [wide[:, h * SPAN : (h + 1) * SPAN] for h in range(blocks)], axis=0
    ).astype(BF16)


def one_hot(low, dtype=BF16):
    width = low.shape[1]
    rows = lax.broadcasted_iota(jnp.int32, (SPAN, width), 0)
    return (rows == low).astype(F32).astype(dtype)


def choose(picked, high, rows):
    parts = [picked[i : i + rows] for i in range(0, picked.shape[0], rows)]
    bit = 1
    while len(parts) > 1:
        odd = (high & bit) != 0
        parts = [jnp.where(odd, parts[i + 1], parts[i]) for i in range(0, len(parts), 2)]
        bit *= 2
    return parts[0]


def pick_both(table, ids, rows):
    low, high = ids & (SPAN - 1), ids >> 8
    split = table.shape[0] * rows // (rows + 4)
    picked = jnp.dot(table, one_hot(low), preferred_element_type=F32)
    return choose(picked[:split], high, rows), choose(picked[split:], high, 4)


def fetch_kernel(
    velocity, adjoint, corners, shared, thickness, rate, retention, weight, stretch, shear,
    fields, top, params, names, sends,
    first, second, stretch_here, shear_here, shared_here, semaphores,
):
    layers, elems = thickness.shape
    pairs = [(velocity, first), (adjoint, second), (corners, names), (shared, shared_here)]
    pairs += [(stretch, stretch_here), (shear, shear_here)]
    for i, ref in enumerate((thickness, rate, retention, weight)):
        pairs.append((ref, params.at[pl.ds(i * layers, layers)]))
    copies = [
        pltpu.make_async_copy(source, target, semaphores.at[i])
        for i, (source, target) in enumerate(pairs)
    ]
    for copy in copies:
        copy.start()
    for copy in copies[:2]:
        copy.wait()
    parts = [first[0], first[1], second[0], second[1]]
    fields[...] = jnp.concatenate(parts, axis=0)
    wide = [part.astype(F32)[0:1] for part in parts]
    top[...] = jnp.concatenate(wide, axis=0).astype(BF16)
    for copy in copies[2:]:
        copy.wait()
    params[4 * layers :, :] = jnp.concatenate(
        [stretch_here[...], shear_here[...], jnp.zeros((4, elems), F32)], axis=0
    )
    sends[...] = jnp.concatenate([shared_here[j : j + 1, :] for j in range(4)], axis=1)


def element_kernel(params, names, sends, fields, data, lists, picked):
    owned = fields.shape[1]
    elems = names.shape[1]
    slots = data.shape[1]
    rows = fields.shape[0]
    held = params.shape[0]
    chunk = min(1024, elems)

    def step(i, total):
        at = pl.ds(pl.multiple_of(i * chunk, chunk), chunk)
        values = params[:, at]
        coarse = values.astype(BF16).astype(F32)
        here = names[:, at]
        left = jnp.concatenate(
            [
                coarse,
                values - coarse,
                (here & (SPAN - 1)).astype(F32),
                (here >> 8).astype(F32),
                jnp.ones((8, chunk), F32),
            ],
            axis=0,
        ).astype(BF16)
        wanted = lax.broadcasted_iota(jnp.int32, (slots, chunk), 0) + owned
        mine = (wanted == here[0:1]).astype(F32).astype(BF16)
        return total + lax.dot_general(left, mine, NT, preferred_element_type=F32)

    total = lax.fori_loop(0, elems // chunk, step, jnp.zeros((2 * held + 16, slots), F32))
    data[...] = total[: 2 * held].astype(BF16)
    ids = (total[2 * held : 2 * held + 4] + total[2 * held + 4 : 2 * held + 8] * SPAN).astype(jnp.int32)
    ids = jnp.where(total[2 * held + 8 : 2 * held + 9] > 0.5, ids, owned)
    lists[...] = jnp.concatenate([sends[...], ids[1:4]], axis=0)
    table = node_table(fields)
    for c in range(4):
        wanted = lists[c : c + 1, :]
        got = jnp.dot(table, one_hot(wanted & (SPAN - 1)), preferred_element_type=F32)
        picked[c * rows : (c + 1) * rows, :] = choose(got, wanted >> 8, rows).astype(BF16)


def message_kernel(below, lists, data, picked, low, messages):
    table = below_table(below[...])
    slot = messages.shape[2]
    split = picked.shape[0]
    lower = []
    for c in range(4):
        wanted = lists[c : c + 1, :]
        got = jnp.dot(table, one_hot(wanted & (SPAN - 1)), preferred_element_type=F32)
        lower.append(choose(got, wanted >> 8, 4))
    low[...] = jnp.concatenate(lower, axis=0).astype(BF16)
    place, count = lax.axis_index("plane"), messages.shape[0]
    for j, offset in enumerate(OFFSETS):
        at = slice(j * slot, (j + 1) * slot)
        target = place + offset

        @pl.when((target >= 0) & (target < count))
        def _():
            messages[target, :split, :] = picked[:, at]
            messages[target, split : split + 16, :] = low[:, at]
            messages[target, split + 16 :, :] = data[:, at]


def plane_modes(a0, a1, a2, a3):
    s01, d01, s23, d23 = a0 + a1, a1 - a0, a2 + a3, a2 - a3
    return s01 + s23, d01 + d23, s23 - s01, d23 - d01


def terms(upper, bottom, stretch, shear, thickness, rate):
    layers, n = thickness.shape
    last = lax.broadcasted_iota(jnp.int32, (layers, n), 0) == layers - 1
    plus, minus, depth = [], [], []
    ends = plane_modes(*bottom)
    for comp in range(4):
        top = plane_modes(*[upper[c][comp] for c in range(4)])
        end = [mode[comp : comp + 1] for mode in ends]
        under = [
            jnp.where(last, jnp.broadcast_to(e, t.shape), pltpu.roll(t, layers - 1, 0))
            for t, e in zip(top, end)
        ]
        depth_parts = [top[0] - under[0]]
        plus_parts, minus_parts = [], []
        for t, u in zip(top[1:], under[1:]):
            total, half = t + u, GAUSS * (t - u)
            plus_parts.append(total + half)
            minus_parts.append(total - half)
            depth_parts.append(half)
        plus.append(plus_parts)
        minus.append(minus_parts)
        depth.append(depth_parts)
    s0, s1 = stretch[0:1] * (1.0 / 16.0), stretch[1:2] * (1.0 / 16.0)
    h0, h1 = shear[0:1] * (1.0 / 16.0), shear[1:2] * (1.0 / 16.0)
    gs0, gs1, gh0, gh1 = s0 * GAUSS, s1 * GAUSS, h0 * GAUSS, h1 * GAUSS

    def plane_fields(part, first):
        (xa, ya, wa), (xb, yb, wb) = part[first], part[first + 1]
        p1, p2 = s0 * xa + h0 * ya, h1 * xb + s1 * yb
        x1, x2 = gh0 * wa, gs1 * wb
        y1, y2 = gs0 * wa, gh1 * wb
        return (
            (p1 + p2, x1 + x2, y1 + y2),
            (p1 - p2, x1 - x2, y1 - y2),
            (
                (h1 * xa + s1 * ya) + (s0 * xb + h0 * yb),
                gs1 * wa + gh0 * wb,
                gh1 * wa + gs0 * wb,
            ),
        )

    def four(field):
        base, along_x, along_y = field
        up, um = base + along_x, base - along_x
        return up + along_y, up - along_y, um + along_y, um - along_y

    inverse = 0.125 / thickness
    inverse_g = inverse * GAUSS

    def depth_four(parts):
        q0, qx, qy, qw = (
            parts[0] * inverse,
            parts[1] * inverse,
            parts[2] * inverse,
            parts[3] * inverse_g,
        )
        p, m, r, t = q0 + qx, q0 - qx, qy + qw, qy - qw
        return p + r, p - r, m + t, m - t

    za, zb, zc, zd = [depth_four(depth[comp]) for comp in range(4)]
    shear_ff = [za[k] * za[k] + zb[k] * zb[k] + STRAIN_EPS for k in range(4)]
    shear_fa = [za[k] * zc[k] + zb[k] * zd[k] for k in range(4)]
    total = None
    for part in (plus, minus):
        flow = [four(f) for f in plane_fields(part, 0)]
        other = [four(f) for f in plane_fields(part, 2)]
        for k in range(4):
            s, d, x = flow[0][k], flow[1][k], flow[2][k]
            triple = 3.0 * s
            effective = (triple * s + d * d) + (x * x + shear_ff[k])
            paired = (triple * other[0][k] + d * other[1][k]) + (x * other[2][k] + shear_fa[k])
            value = jnp.exp(jnp.log(effective) * (-1.0 / 3.0)) * paired
            total = value if total is None else total + value
    det = stretch[0:1] * stretch[1:2] - shear[0:1] * shear[1:2]
    return total * (rate * thickness / det)


def group_maps(retention, weight, term):
    layers, n = retention.shape
    row = lax.broadcasted_iota(jnp.int32, (layers, n), 0)
    factor, offset = retention, (1.0 - retention) * weight
    step = 1
    while step < layers:
        seen = row >= step
        before_f = jnp.where(seen, pltpu.roll(factor, step, 0), 1.0)
        before_o = jnp.where(seen, pltpu.roll(offset, step, 0), 0.0)
        offset = factor * before_o + offset
        factor = factor * before_f
        step *= 2
    return jnp.concatenate(
        [
            factor[layers - 1 :],
            offset[layers - 1 :],
            jnp.sum(factor * term, axis=0, keepdims=True),
            jnp.sum(offset * term, axis=0, keepdims=True),
        ],
        axis=0,
    )


def element_maps(tops, bots, params):
    layers = (params.shape[0] - 8) // 4
    thickness, rate, retention, weight = [
        params[i * layers : (i + 1) * layers] for i in range(4)
    ]
    stretch, shear = params[4 * layers : 4 * layers + 2], params[4 * layers + 2 : 4 * layers + 4]
    return group_maps(retention, weight, terms(tops, bots, stretch, shear, thickness, rate))


def physics_kernel(fields, below, names, params, out, first, second):
    rows = fields.shape[0]
    layers = rows // 4
    elems = names.shape[1]
    chunk = first.shape[1]
    count = elems // chunk
    table = jnp.concatenate([node_table(fields), below_table(below[...])], axis=0)

    def gather(i, c, held):
        at = pl.ds(pl.multiple_of(i * chunk, chunk), chunk)
        values, ends = pick_both(table, names[c : c + 1, at], rows)
        held[c * rows : (c + 1) * rows, :] = values
        held[4 * rows + 8 * c : 4 * rows + 8 * c + 4, :] = ends

    def work(i, k, held):
        cut = slice(k * LANES, (k + 1) * LANES)
        here = pl.ds(pl.multiple_of(i * chunk + k * LANES, LANES), LANES)
        tops = [
            [held[c * rows + m * layers : c * rows + (m + 1) * layers, cut] for m in range(4)]
            for c in range(4)
        ]
        ends = [held[4 * rows + 8 * c : 4 * rows + 8 * c + 4, cut] for c in range(4)]
        out[:, here] = element_maps(tops, ends, params[:, here])

    def both(i, following, held, other):
        cuts = chunk // LANES
        for k in range(4):
            gather(following, k, other)
            if (k + 1) * cuts % 4 == 0:
                work(i, (k + 1) * cuts // 4 - 1, held)

    for c in range(4):
        gather(0, c, first)

    def step(j, _):
        both(2 * j, 2 * j + 1, first, second)
        both(2 * j + 1, jnp.minimum(2 * j + 2, count - 1), second, first)
        return 0

    lax.fori_loop(0, count // 2, step, 0)


def border_kernel(state, data, picked, low, messages, out):
    elems = state.shape[1]
    rows = picked.shape[0] // 4
    layers = rows // 4
    slot = messages.shape[2]
    slots = 4 * slot
    place, count = lax.axis_index("plane"), messages.shape[0]
    out[:, :elems] = state[...]
    pieces = []
    for offset in OFFSETS:
        source = place + offset
        pieces.append(messages[jnp.clip(source, 0, count - 1)])
    got = jnp.concatenate(pieces, axis=1).astype(F32)
    mine = picked[...].astype(F32)
    ends = low[...].astype(F32)
    split = 4 * rows + 16
    half = (got.shape[0] - split) // 2
    here = data[...].astype(F32)
    sides = (
        (got, mine, got[4 * rows : split], ends, here[:half] + here[half:]),
        (mine, got, ends, got[4 * rows : split], got[split : split + half] + got[split + half :]),
    )
    for side, (corner0, others, end0, end_others, params) in enumerate(sides):
        for k in range(slots // LANES):
            cut = slice(k * LANES, (k + 1) * LANES)
            tops = [
                [
                    (others if c else corner0)[c * rows + m * layers : c * rows + (m + 1) * layers, cut]
                    for m in range(4)
                ]
                for c in range(4)
            ]
            bots = [(end_others if c else end0)[4 * c : 4 * c + 4, cut] for c in range(4)]
            start = elems + side * slots + k * LANES
            out[:, start : start + LANES] = element_maps(tops, bots, params[:, cut])


def sum_kernel(earlier, later, corners, lists, out):
    elems = corners.shape[1]
    owned = out.shape[0] * out.shape[1]
    slots = lists.shape[1]
    high_count = out.shape[0]
    chunk = min(512, elems)

    def add(total, names, values):
        width = names.shape[1]
        low, high = names & (LANES - 1), names >> 7
        coarse = values.astype(BF16).astype(F32)
        fine = values - coarse
        here = lax.broadcasted_iota(jnp.int32, (high_count, width), 0) == high
        left = jnp.concatenate([jnp.where(here, coarse, 0.0), jnp.where(here, fine, 0.0)], axis=0)
        hot = (lax.broadcasted_iota(jnp.int32, (LANES, width), 0) == low).astype(F32).astype(BF16)
        return total + lax.dot_general(left.astype(BF16), hot, NT, preferred_element_type=F32)

    def column(at):
        first, second = earlier[:, at], later[:, at]
        return 0.25 * (first[3:4] + second[3:4] + first[1:2] * second[2:3])

    def step(i, total):
        at = pl.ds(pl.multiple_of(i * chunk, chunk), chunk)
        values = jnp.where(corners[0:1, at] < owned, column(at), 0.0)
        for c in range(4):
            total = add(total, corners[c : c + 1, at], values)
        return total

    total = lax.fori_loop(0, elems // chunk, step, jnp.zeros((2 * high_count, LANES), F32))
    ghost, near = column(pl.ds(elems, slots)), column(pl.ds(elems + slots, slots))
    for c in range(4):
        names = lists[c : c + 1, :]
        total = add(total, names, jnp.where(names < owned, ghost if c else near, 0.0))
    out[...] = total[:high_count] + total[high_count:]


def compose(one, two):
    return jnp.stack(
        [
            one[0] * two[0],
            two[0] * one[1] + two[1],
            one[2] + one[0] * two[2],
            one[3] + two[3] + one[1] * two[2],
        ]
    )


def shards(
    velocity, adjoint, corners, shared, stretch, shear_part, thickness, rate_factor, retention, weight
):
    layers, owned = velocity.shape[1:]
    elems = corners.shape[1]
    slot = shared.shape[1]
    slots = 4 * slot
    rows = 4 * layers
    shape = jax.ShapeDtypeStruct
    parts = lax.axis_size("plane")
    fields, top, params, names, sends = kernel_call(
        fetch_kernel,
        (
            shape((rows, owned), BF16),
            shape((4, owned), BF16),
            shape((rows + 8, elems), F32),
            shape(corners.shape, jnp.int32),
            shape((1, slots), jnp.int32),
        ),
        10**6,
        velocity, adjoint, corners, shared, thickness, rate_factor, retention, weight, stretch, shear_part,
        spaces="far",
        scratch=(
            pltpu.VMEM(velocity.shape, BF16),
            pltpu.VMEM(adjoint.shape, BF16),
            pltpu.VMEM(stretch.shape, F32),
            pltpu.VMEM(shear_part.shape, F32),
            pltpu.VMEM(shared.shape, jnp.int32),
            pltpu.SemaphoreType.DMA((10,)),
        ),
    )
    below = shifted(top, "layer", -1)
    data, lists, picked = kernel_call(
        element_kernel,
        (
            shape((2 * rows + 16, slots), BF16),
            shape((4, slots), jnp.int32),
            shape((4 * rows, slots), BF16),
        ),
        2 * 10**9,
        params, names, sends, fields,
    )
    low, messages = kernel_call(
        message_kernel,
        (shape((16, slots), BF16), shape((parts, 6 * rows + 32, slot), BF16)),
        10**9,
        below, lists, data, picked,
    )
    incoming = lax.all_to_all(messages, "plane", 0, 0)
    chunk = min(SPAN, elems // 2)
    state = kernel_call(
        physics_kernel,
        shape((4, elems), F32),
        10**10,
        fields, below, names, params,
        scratch=(pltpu.VMEM((4 * rows + 32, chunk), F32),) * 2,
    )
    state = kernel_call(
        border_kernel,
        shape((4, elems + 2 * slots), F32),
        10**9,
        state, data, picked, low, incoming,
    )
    groups, place = lax.axis_size("layer"), lax.axis_index("layer")
    step = 1
    earlier = later = state
    while step < groups:
        if step > 1:
            state = compose(earlier, later)
        other = lax.ppermute(state, "layer", [(i, i ^ step) for i in range(groups)])
        second = (place & step) != 0
        earlier, later = jnp.where(second, other, state), jnp.where(second, state, other)
        step *= 2
    gradient = kernel_call(
        sum_kernel,
        shape((owned // LANES, LANES), F32),
        2 * 10**9,
        earlier, later, names, lists,
    )
    return gradient.reshape(owned)


def solution(mesh):
    return jax.shard_map(
        shards,
        mesh=mesh,
        in_specs=(
            P(None, "layer", "plane"),
            P(None, "layer", "plane"),
            P(None, "plane"),
            P(None, "plane"),
            P(None, "plane"),
            P(None, "plane"),
            P("layer", "plane"),
            P("layer", "plane"),
            P("layer", "plane"),
            P("layer", "plane"),
        ),
        out_specs=P("plane"),
        check_vma=False,
    )
```

```python
import math

import jax
import jax.numpy as jnp
from jax import lax
from jax.experimental import pallas as pl
from jax.experimental.pallas import tpu as pltpu
from jax.sharding import PartitionSpec as P

OFFSETS = (-2, -1, 1, 2)
STRAIN_EPS = 0.01
GAUSS = 1.0 / math.sqrt(3.0)
SPAN = 256
LANES = 128
F32, BF16 = jnp.float32, jnp.bfloat16
NT = (((1,), (1,)), ((), ()))


def shifted(value, axis, steps):
    count = lax.axis_size(axis)
    first, last = (max(0, -steps), min(count, count - steps))
    return lax.ppermute(value, axis, [(source, source + steps) for source in range(first, last)])


def kernel_call(body, out_shape, flops, *args, spaces=None, scratch=()):
    vmem = pl.BlockSpec(memory_space=pltpu.VMEM)
    far = pl.BlockSpec(memory_space=pltpu.HBM)
    if spaces == "far":
        args = [pltpu.with_memory_space_constraint(value, pltpu.HBM) for value in args]
    return pl.pallas_call(
        body,
        out_shape=out_shape,
        in_specs=[far if spaces == "far" else vmem for _ in args],
        out_specs=jax.tree.map(lambda _: vmem, out_shape),
        scratch_shapes=list(scratch),
        compiler_params=pltpu.CompilerParams(vmem_limit_bytes=48 * 2**20),
        cost_estimate=pl.CostEstimate(flops=flops, bytes_accessed=2**20, transcendentals=0),
    )(*args)


def node_table(fields):
    blocks = fields.shape[1] // SPAN
    return jnp.concatenate([fields[:, h * SPAN : (h + 1) * SPAN] for h in range(blocks)], axis=0)


def below_table(below):
    wide = below.astype(F32)
    blocks = wide.shape[1] // SPAN
    return jnp.concatenate(
        [wide[:, h * SPAN : (h + 1) * SPAN] for h in range(blocks)], axis=0
    ).astype(BF16)


def one_hot(low, dtype=BF16):
    width = low.shape[1]
    rows = lax.broadcasted_iota(jnp.int32, (SPAN, width), 0)
    return (rows == low).astype(F32).astype(dtype)


def choose(picked, high, rows):
    parts = [picked[i : i + rows] for i in range(0, picked.shape[0], rows)]
    bit = 1
    while len(parts) > 1:
        odd = (high & bit) != 0
        parts = [jnp.where(odd, parts[i + 1], parts[i]) for i in range(0, len(parts), 2)]
        bit *= 2
    return parts[0]


def pick_both(table, ids, rows):
    low, high = ids & (SPAN - 1), ids >> 8
    split = table.shape[0] * rows // (rows + 4)
    picked = jnp.dot(table, one_hot(low), preferred_element_type=F32)
    return choose(picked[:split], high, rows), choose(picked[split:], high, 4)


def fetch_kernel(
    velocity, adjoint, corners, shared, thickness, rate, retention, weight, stretch, shear,
    fields, top, params, names, sends,
    first, second, stretch_here, shear_here, shared_here, semaphores,
):
    layers, elems = thickness.shape
    pairs = [(velocity, first), (adjoint, second), (corners, names), (shared, shared_here)]
    pairs += [(stretch, stretch_here), (shear, shear_here)]
    for i, ref in enumerate((thickness, rate, retention, weight)):
        pairs.append((ref, params.at[pl.ds(i * layers, layers)]))
    copies = [
        pltpu.make_async_copy(source, target, semaphores.at[i])
        for i, (source, target) in enumerate(pairs)
    ]
    for copy in copies:
        copy.start()
    for copy in copies[:2]:
        copy.wait()
    parts = [first[0], first[1], second[0], second[1]]
    fields[...] = jnp.concatenate(parts, axis=0)
    wide = [part.astype(F32)[0:1] for part in parts]
    top[...] = jnp.concatenate(wide, axis=0).astype(BF16)
    for copy in copies[2:]:
        copy.wait()
    params[4 * layers :, :] = jnp.concatenate(
        [stretch_here[...], shear_here[...], jnp.zeros((4, elems), F32)], axis=0
    )
    sends[...] = jnp.concatenate([shared_here[j : j + 1, :] for j in range(4)], axis=1)


def element_kernel(params, names, sends, fields, data, lists, picked):
    owned = fields.shape[1]
    elems = names.shape[1]
    slots = data.shape[1]
    rows = fields.shape[0]
    held = params.shape[0]
    chunk = min(1024, elems)

    def step(i, total):
        at = pl.ds(pl.multiple_of(i * chunk, chunk), chunk)
        values = params[:, at]
        coarse = values.astype(BF16).astype(F32)
        here = names[:, at]
        left = jnp.concatenate(
            [
                coarse,
                values - coarse,
                (here & (SPAN - 1)).astype(F32),
                (here >> 8).astype(F32),
                jnp.ones((8, chunk), F32),
            ],
            axis=0,
        ).astype(BF16)
        wanted = lax.broadcasted_iota(jnp.int32, (slots, chunk), 0) + owned
        mine = (wanted == here[0:1]).astype(F32).astype(BF16)
        return total + lax.dot_general(left, mine, NT, preferred_element_type=F32)

    total = lax.fori_loop(0, elems // chunk, step, jnp.zeros((2 * held + 16, slots), F32))
    data[...] = total[: 2 * held].astype(BF16)
    ids = (total[2 * held : 2 * held + 4] + total[2 * held + 4 : 2 * held + 8] * SPAN).astype(jnp.int32)
    ids = jnp.where(total[2 * held + 8 : 2 * held + 9] > 0.5, ids, owned)
    lists[...] = jnp.concatenate([sends[...], ids[1:4]], axis=0)
    table = node_table(fields)
    for c in range(4):
        wanted = lists[c : c + 1, :]
        got = jnp.dot(table, one_hot(wanted & (SPAN - 1)), preferred_element_type=F32)
        picked[c * rows : (c + 1) * rows, :] = choose(got, wanted >> 8, rows).astype(BF16)


def message_kernel(below, lists, data, picked, low, messages):
    table = below_table(below[...])
    slot = messages.shape[2]
    split = picked.shape[0]
    lower = []
    for c in range(4):
        wanted = lists[c : c + 1, :]
        got = jnp.dot(table, one_hot(wanted & (SPAN - 1)), preferred_element_type=F32)
        lower.append(choose(got, wanted >> 8, 4))
    low[...] = jnp.concatenate(lower, axis=0).astype(BF16)
    place, count = lax.axis_index("plane"), messages.shape[0]
    for j, offset in enumerate(OFFSETS):
        at = slice(j * slot, (j + 1) * slot)
        target = place + offset

        @pl.when((target >= 0) & (target < count))
        def _():
            messages[target, :split, :] = picked[:, at]
            messages[target, split : split + 16, :] = low[:, at]
            messages[target, split + 16 :, :] = data[:, at]


def plane_modes(a0, a1, a2, a3):
    s01, d01, s23, d23 = a0 + a1, a1 - a0, a2 + a3, a2 - a3
    return s01 + s23, d01 + d23, s23 - s01, d23 - d01


def terms(upper, bottom, stretch, shear, thickness, rate):
    layers, n = thickness.shape
    last = lax.broadcasted_iota(jnp.int32, (layers, n), 0) == layers - 1
    plus, minus, depth = [], [], []
    ends = plane_modes(*bottom)
    for comp in range(4):
        top = plane_modes(*[upper[c][comp] for c in range(4)])
        end = [mode[comp : comp + 1] for mode in ends]
        under = [
            jnp.where(last, jnp.broadcast_to(e, t.shape), pltpu.roll(t, layers - 1, 0))
            for t, e in zip(top, end)
        ]
        depth_parts = [top[0] - under[0]]
        plus_parts, minus_parts = [], []
        for t, u in zip(top[1:], under[1:]):
            total, half = t + u, GAUSS * (t - u)
            plus_parts.append(total + half)
            minus_parts.append(total - half)
            depth_parts.append(half)
        plus.append(plus_parts)
        minus.append(minus_parts)
        depth.append(depth_parts)
    s0, s1 = stretch[0:1] * (1.0 / 16.0), stretch[1:2] * (1.0 / 16.0)
    h0, h1 = shear[0:1] * (1.0 / 16.0), shear[1:2] * (1.0 / 16.0)
    gs0, gs1, gh0, gh1 = s0 * GAUSS, s1 * GAUSS, h0 * GAUSS, h1 * GAUSS

    def plane_fields(part, first):
        (xa, ya, wa), (xb, yb, wb) = part[first], part[first + 1]
        p1, p2 = s0 * xa + h0 * ya, h1 * xb + s1 * yb
        x1, x2 = gh0 * wa, gs1 * wb
        y1, y2 = gs0 * wa, gh1 * wb
        return (
            (p1 + p2, x1 + x2, y1 + y2),
            (p1 - p2, x1 - x2, y1 - y2),
            (
                (h1 * xa + s1 * ya) + (s0 * xb + h0 * yb),
                gs1 * wa + gh0 * wb,
                gh1 * wa + gs0 * wb,
            ),
        )

    def four(field):
        base, along_x, along_y = field
        up, um = base + along_x, base - along_x
        return up + along_y, up - along_y, um + along_y, um - along_y

    inverse = 0.125 / thickness
    inverse_g = inverse * GAUSS

    def depth_four(parts):
        q0, qx, qy, qw = (
            parts[0] * inverse,
            parts[1] * inverse,
            parts[2] * inverse,
            parts[3] * inverse_g,
        )
        p, m, r, t = q0 + qx, q0 - qx, qy + qw, qy - qw
        return p + r, p - r, m + t, m - t

    za, zb, zc, zd = [depth_four(depth[comp]) for comp in range(4)]
    shear_ff = [za[k] * za[k] + zb[k] * zb[k] + STRAIN_EPS for k in range(4)]
    shear_fa = [za[k] * zc[k] + zb[k] * zd[k] for k in range(4)]
    total = None
    for part in (plus, minus):
        flow = [four(f) for f in plane_fields(part, 0)]
        other = [four(f) for f in plane_fields(part, 2)]
        for k in range(4):
            s, d, x = flow[0][k], flow[1][k], flow[2][k]
            triple = 3.0 * s
            effective = (triple * s + d * d) + (x * x + shear_ff[k])
            paired = (triple * other[0][k] + d * other[1][k]) + (x * other[2][k] + shear_fa[k])
            value = jnp.exp(jnp.log(effective) * (-1.0 / 3.0)) * paired
            total = value if total is None else total + value
    det = stretch[0:1] * stretch[1:2] - shear[0:1] * shear[1:2]
    return total * (rate * thickness / det)


def group_maps(retention, weight, term):
    layers, n = retention.shape
    row = lax.broadcasted_iota(jnp.int32, (layers, n), 0)
    factor, offset = retention, (1.0 - retention) * weight
    step = 1
    while step < layers:
        seen = row >= step
        before_f = jnp.where(seen, pltpu.roll(factor, step, 0), 1.0)
        before_o = jnp.where(seen, pltpu.roll(offset, step, 0), 0.0)
        offset = factor * before_o + offset
        factor = factor * before_f
        step *= 2
    return jnp.concatenate(
        [
            factor[layers - 1 :],
            offset[layers - 1 :],
            jnp.sum(factor * term, axis=0, keepdims=True),
            jnp.sum(offset * term, axis=0, keepdims=True),
        ],
        axis=0,
    )


def element_maps(tops, bots, params):
    layers = (params.shape[0] - 8) // 4
    thickness, rate, retention, weight = [
        params[i * layers : (i + 1) * layers] for i in range(4)
    ]
    stretch, shear = params[4 * layers : 4 * layers + 2], params[4 * layers + 2 : 4 * layers + 4]
    return group_maps(retention, weight, terms(tops, bots, stretch, shear, thickness, rate))


def physics_kernel(fields, below, names, params, out, first, second):
    rows = fields.shape[0]
    layers = rows // 4
    elems = names.shape[1]
    chunk = first.shape[1]
    count = elems // chunk
    table = jnp.concatenate([node_table(fields), below_table(below[...])], axis=0)

    def gather(i, c, held):
        at = pl.ds(pl.multiple_of(i * chunk, chunk), chunk)
        values, ends = pick_both(table, names[c : c + 1, at], rows)
        held[c * rows : (c + 1) * rows, :] = values
        held[4 * rows + 8 * c : 4 * rows + 8 * c + 4, :] = ends

    def work(i, k, held):
        cut = slice(k * LANES, (k + 1) * LANES)
        here = pl.ds(pl.multiple_of(i * chunk + k * LANES, LANES), LANES)
        tops = [
            [held[c * rows + m * layers : c * rows + (m + 1) * layers, cut] for m in range(4)]
            for c in range(4)
        ]
        ends = [held[4 * rows + 8 * c : 4 * rows + 8 * c + 4, cut] for c in range(4)]
        out[:, here] = element_maps(tops, ends, params[:, here])

    def both(i, following, held, other):
        cuts = chunk // LANES
        for k in range(4):
            gather(following, k, other)
            if (k + 1) * cuts % 4 == 0:
                work(i, (k + 1) * cuts // 4 - 1, held)

    for c in range(4):
        gather(0, c, first)

    def step(j, _):
        both(2 * j, 2 * j + 1, first, second)
        both(2 * j + 1, jnp.minimum(2 * j + 2, count - 1), second, first)
        return 0

    lax.fori_loop(0, count // 2, step, 0)


def border_kernel(state, data, picked, low, messages, out):
    elems = state.shape[1]
    rows = picked.shape[0] // 4
    layers = rows // 4
    slot = messages.shape[2]
    slots = 4 * slot
    place, count = lax.axis_index("plane"), messages.shape[0]
    out[:, :elems] = state[...]
    pieces = []
    for offset in OFFSETS:
        source = place + offset
        pieces.append(messages[jnp.clip(source, 0, count - 1)])
    got = jnp.concatenate(pieces, axis=1).astype(F32)
    mine = picked[...].astype(F32)
    ends = low[...].astype(F32)
    split = 4 * rows + 16
    half = (got.shape[0] - split) // 2
    here = data[...].astype(F32)
    sides = (
        (got, mine, got[4 * rows : split], ends, here[:half] + here[half:]),
        (mine, got, ends, got[4 * rows : split], got[split : split + half] + got[split + half :]),
    )
    for side, (corner0, others, end0, end_others, params) in enumerate(sides):
        for k in range(slots // LANES):
            cut = slice(k * LANES, (k + 1) * LANES)
            tops = [
                [
                    (others if c else corner0)[c * rows + m * layers : c * rows + (m + 1) * layers, cut]
                    for m in range(4)
                ]
                for c in range(4)
            ]
            bots = [(end_others if c else end0)[4 * c : 4 * c + 4, cut] for c in range(4)]
            start = elems + side * slots + k * LANES
            out[:, start : start + LANES] = element_maps(tops, bots, params[:, cut])


def sum_kernel(first, second, corners, lists, out):
    elems = corners.shape[1]
    slots = lists.shape[1]
    high_count = out.shape[0]
    owned = high_count * LANES
    column = 0.25 * (first[1:2, :] + second[1:2, :] + first[0:1, :] * second[0:1, :])
    main, ghost, near = (
        column[:, :elems],
        column[:, elems : elems + slots],
        column[:, elems + slots :],
    )
    main = jnp.where(corners[0:1, :] < owned, main, 0.0)
    work = [(corners[c : c + 1, :], main) for c in range(4)]
    work += [(lists[c : c + 1, :], ghost if c else near) for c in range(4)]
    total = None
    for at, (names, values) in enumerate(work):
        width = names.shape[1]
        if at >= 4:
            values = jnp.where(names < owned, values, 0.0)
        low, high = names & (LANES - 1), names >> 7
        coarse = values.astype(BF16).astype(F32)
        here = lax.broadcasted_iota(jnp.int32, (high_count, width), 0) == high
        parts = [jnp.where(here, coarse, 0.0), jnp.where(here, values - coarse, 0.0)]
        parts = jnp.concatenate(parts, axis=0).astype(BF16)
        hot = (lax.broadcasted_iota(jnp.int32, (LANES, width), 0) == low).astype(F32).astype(BF16)
        added = lax.dot_general(hot, parts, NT, preferred_element_type=F32)
        total = added if total is None else total + added
    total = total.T
    out[...] = total[:high_count] + total[high_count:]


def compose(one, two):
    return jnp.stack(
        [
            one[0] * two[0],
            two[0] * one[1] + two[1],
            one[2] + one[0] * two[2],
            one[3] + two[3] + one[1] * two[2],
        ]
    )


def shards(
    velocity, adjoint, corners, shared, stretch, shear_part, thickness, rate_factor, retention, weight
):
    layers, owned = velocity.shape[1:]
    elems = corners.shape[1]
    slot = shared.shape[1]
    slots = 4 * slot
    rows = 4 * layers
    shape = jax.ShapeDtypeStruct
    parts = lax.axis_size("plane")
    fields, top, params, names, sends = kernel_call(
        fetch_kernel,
        (
            shape((rows, owned), BF16),
            shape((4, owned), BF16),
            shape((rows + 8, elems), F32),
            shape(corners.shape, jnp.int32),
            shape((1, slots), jnp.int32),
        ),
        10**6,
        velocity, adjoint, corners, shared, thickness, rate_factor, retention, weight, stretch, shear_part,
        spaces="far",
        scratch=(
            pltpu.VMEM(velocity.shape, BF16),
            pltpu.VMEM(adjoint.shape, BF16),
            pltpu.VMEM(stretch.shape, F32),
            pltpu.VMEM(shear_part.shape, F32),
            pltpu.VMEM(shared.shape, jnp.int32),
            pltpu.SemaphoreType.DMA((10,)),
        ),
    )
    below = shifted(top, "layer", -1)
    data, lists, picked = kernel_call(
        element_kernel,
        (
            shape((2 * rows + 16, slots), BF16),
            shape((4, slots), jnp.int32),
            shape((4 * rows, slots), BF16),
        ),
        2 * 10**9,
        params, names, sends, fields,
    )
    low, messages = kernel_call(
        message_kernel,
        (shape((16, slots), BF16), shape((parts, 6 * rows + 32, slot), BF16)),
        10**9,
        below, lists, data, picked,
    )
    incoming = lax.all_to_all(messages, "plane", 0, 0)
    chunk = min(SPAN, elems // 2)
    state = kernel_call(
        physics_kernel,
        shape((4, elems), F32),
        10**10,
        fields, below, names, params,
        scratch=(pltpu.VMEM((4 * rows + 32, chunk), F32),) * 2,
    )
    state = kernel_call(
        border_kernel,
        shape((4, elems + 2 * slots), F32),
        10**9,
        state, data, picked, low, incoming,
    )
    groups, place = lax.axis_size("layer"), lax.axis_index("layer")
    step = 1
    while 2 * step < groups:
        other = lax.ppermute(state, "layer", [(i, i ^ step) for i in range(groups)])
        second = (place & step) != 0
        state = compose(jnp.where(second, other, state), jnp.where(second, state, other))
        step *= 2
    mine = jnp.stack([jnp.where((place & step) != 0, state[2], state[1]), state[3]])
    other = jnp.zeros_like(mine)
    if groups > 1:
        other = lax.ppermute(mine, "layer", [(i, i ^ step) for i in range(groups)])
    gradient = kernel_call(
        sum_kernel,
        shape((owned // LANES, LANES), F32),
        2 * 10**9,
        mine, other, names, lists,
    )
    return gradient.reshape(owned)


def solution(mesh):
    return jax.shard_map(
        shards,
        mesh=mesh,
        in_specs=(
            P(None, "layer", "plane"),
            P(None, "layer", "plane"),
            P(None, "plane"),
            P(None, "plane"),
            P(None, "plane"),
            P(None, "plane"),
            P("layer", "plane"),
            P("layer", "plane"),
            P("layer", "plane"),
            P("layer", "plane"),
        ),
        out_specs=P("plane"),
        check_vma=False,
    )
```

```python
import math

import jax
import jax.numpy as jnp
from jax import lax
from jax.experimental import pallas as pl
from jax.experimental.pallas import tpu as pltpu
from jax.sharding import PartitionSpec as P

OFFSETS = (-2, -1, 1, 2)
STRAIN_EPS = 0.01
GAUSS = 1.0 / math.sqrt(3.0)
SPAN = 256
LANES = 128
F32, BF16 = jnp.float32, jnp.bfloat16
NT = (((1,), (1,)), ((), ()))


def shifted(value, axis, steps):
    count = lax.axis_size(axis)
    first, last = (max(0, -steps), min(count, count - steps))
    return lax.ppermute(value, axis, [(source, source + steps) for source in range(first, last)])


def kernel_call(body, out_shape, flops, *args, spaces=None, scratch=()):
    vmem = pl.BlockSpec(memory_space=pltpu.VMEM)
    far = pl.BlockSpec(memory_space=pltpu.HBM)
    if spaces == "far":
        args = [pltpu.with_memory_space_constraint(value, pltpu.HBM) for value in args]
    return pl.pallas_call(
        body,
        out_shape=out_shape,
        in_specs=[far if spaces == "far" else vmem for _ in args],
        out_specs=jax.tree.map(lambda _: vmem, out_shape),
        scratch_shapes=list(scratch),
        compiler_params=pltpu.CompilerParams(vmem_limit_bytes=48 * 2**20),
        cost_estimate=pl.CostEstimate(flops=flops, bytes_accessed=2**20, transcendentals=0),
    )(*args)


def node_table(fields):
    blocks = fields.shape[1] // SPAN
    return jnp.concatenate([fields[:, h * SPAN : (h + 1) * SPAN] for h in range(blocks)], axis=0)


def below_table(below):
    wide = below.astype(F32)
    blocks = wide.shape[1] // SPAN
    return jnp.concatenate(
        [wide[:, h * SPAN : (h + 1) * SPAN] for h in range(blocks)], axis=0
    ).astype(BF16)


def one_hot(low):
    shape = (SPAN, low.shape[1])
    rows = lax.broadcasted_iota(jnp.int32, shape, 0).astype(F32).astype(BF16)
    wanted = jnp.broadcast_to(low.astype(F32).astype(BF16), shape)
    return jnp.where(rows == wanted, jnp.ones(shape, BF16), jnp.zeros(shape, BF16))


def choose(picked, high, rows):
    parts = [picked[i : i + rows] for i in range(0, picked.shape[0], rows)]
    bit = 1
    while len(parts) > 1:
        odd = (high & bit) != 0
        parts = [jnp.where(odd, parts[i + 1], parts[i]) for i in range(0, len(parts), 2)]
        bit *= 2
    return parts[0]


def alternate(first, second, ratio):
    pieces = [(first, 1), (second, ratio)]
    while pieces:
        left = []
        for piece, turns in pieces:
            for _ in range(turns):
                if next(piece, piece) is piece:
                    break
            else:
                left.append((piece, turns))
        pieces = left


def drain(piece):
    while True:
        try:
            next(piece)
        except StopIteration as end:
            return end.value


def fetch_kernel(
    velocity, adjoint, corners, shared, thickness, rate, retention, weight, stretch, shear,
    fields, top, params, names, sends,
    first, second, stretch_here, shear_here, shared_here, semaphores,
):
    layers, elems = thickness.shape
    pairs = [(velocity, first), (adjoint, second), (corners, names), (shared, shared_here)]
    pairs += [(stretch, stretch_here), (shear, shear_here)]
    for i, ref in enumerate((thickness, rate, retention, weight)):
        pairs.append((ref, params.at[pl.ds(i * layers, layers)]))
    copies = [
        pltpu.make_async_copy(source, target, semaphores.at[i])
        for i, (source, target) in enumerate(pairs)
    ]
    for copy in copies:
        copy.start()
    for copy in copies[:2]:
        copy.wait()
    parts = [first[0], first[1], second[0], second[1]]
    fields[...] = jnp.concatenate(parts, axis=0)
    wide = [part.astype(F32)[0:1] for part in parts]
    top[...] = jnp.concatenate(wide, axis=0).astype(BF16)
    for copy in copies[2:]:
        copy.wait()
    params[4 * layers :, :] = jnp.concatenate(
        [stretch_here[...], shear_here[...], jnp.zeros((4, elems), F32)], axis=0
    )
    sends[...] = jnp.concatenate([shared_here[j : j + 1, :] for j in range(4)], axis=1)


def element_kernel(params, names, sends, fields, data, lists, picked):
    owned = fields.shape[1]
    elems = names.shape[1]
    slots = data.shape[1]
    rows = fields.shape[0]
    held = params.shape[0]
    chunk = min(1024, elems)

    def step(i, total):
        at = pl.ds(pl.multiple_of(i * chunk, chunk), chunk)
        values = params[:, at]
        coarse = values.astype(BF16).astype(F32)
        here = names[:, at]
        left = jnp.concatenate(
            [
                coarse,
                values - coarse,
                (here & (SPAN - 1)).astype(F32),
                (here >> 8).astype(F32),
                jnp.ones((8, chunk), F32),
            ],
            axis=0,
        ).astype(BF16)
        wanted = lax.broadcasted_iota(jnp.int32, (slots, chunk), 0) + owned
        mine = (wanted == here[0:1]).astype(F32).astype(BF16)
        return total + lax.dot_general(left, mine, NT, preferred_element_type=F32)

    total = lax.fori_loop(0, elems // chunk, step, jnp.zeros((2 * held + 16, slots), F32))
    data[...] = total[: 2 * held].astype(BF16)
    ids = (total[2 * held : 2 * held + 4] + total[2 * held + 4 : 2 * held + 8] * SPAN).astype(jnp.int32)
    ids = jnp.where(total[2 * held + 8 : 2 * held + 9] > 0.5, ids, owned)
    lists[...] = jnp.concatenate([sends[...], ids[1:4]], axis=0)
    table = node_table(fields)
    for c in range(4):
        wanted = lists[c : c + 1, :]
        got = jnp.dot(table, one_hot(wanted & (SPAN - 1)), preferred_element_type=F32)
        picked[c * rows : (c + 1) * rows, :] = choose(got, wanted >> 8, rows).astype(BF16)


def message_kernel(below, lists, data, picked, low, messages):
    table = below_table(below[...])
    slot = messages.shape[2]
    split = picked.shape[0]
    lower = []
    for c in range(4):
        wanted = lists[c : c + 1, :]
        got = jnp.dot(table, one_hot(wanted & (SPAN - 1)), preferred_element_type=F32)
        lower.append(choose(got, wanted >> 8, 4))
    low[...] = jnp.concatenate(lower, axis=0).astype(BF16)
    place, count = lax.axis_index("plane"), messages.shape[0]
    for j, offset in enumerate(OFFSETS):
        at = slice(j * slot, (j + 1) * slot)
        target = place + offset

        @pl.when((target >= 0) & (target < count))
        def _():
            messages[target, :split, :] = picked[:, at]
            messages[target, split : split + 16, :] = low[:, at]
            messages[target, split + 16 :, :] = data[:, at]


def plane_modes(a0, a1, a2, a3):
    s01, d01, s23, d23 = a0 + a1, a1 - a0, a2 + a3, a2 - a3
    return s01 + s23, d01 + d23, s23 - s01, d23 - d01


def terms(upper, bottom, stretch, shear, thickness, rate):
    layers, n = thickness.shape
    last = lax.broadcasted_iota(jnp.int32, (layers, n), 0) == layers - 1
    plus, minus, depth = [], [], []
    ends = plane_modes(*bottom)
    for comp in range(4):
        top = plane_modes(*[upper[c][comp] for c in range(4)])
        end = [mode[comp : comp + 1] for mode in ends]
        under = [
            jnp.where(last, jnp.broadcast_to(e, t.shape), pltpu.roll(t, layers - 1, 0))
            for t, e in zip(top, end)
        ]
        depth_parts = [top[0] - under[0]]
        plus_parts, minus_parts = [], []
        for t, u in zip(top[1:], under[1:]):
            total, half = t + u, GAUSS * (t - u)
            plus_parts.append(total + half)
            minus_parts.append(total - half)
            depth_parts.append(half)
        plus.append(plus_parts)
        minus.append(minus_parts)
        depth.append(depth_parts)
        yield
    s0, s1 = stretch[0:1] * (1.0 / 16.0), stretch[1:2] * (1.0 / 16.0)
    h0, h1 = shear[0:1] * (1.0 / 16.0), shear[1:2] * (1.0 / 16.0)
    gs0, gs1, gh0, gh1 = s0 * GAUSS, s1 * GAUSS, h0 * GAUSS, h1 * GAUSS

    def plane_fields(part, first):
        (xa, ya, wa), (xb, yb, wb) = part[first], part[first + 1]
        p1, p2 = s0 * xa + h0 * ya, h1 * xb + s1 * yb
        x1, x2 = gh0 * wa, gs1 * wb
        y1, y2 = gs0 * wa, gh1 * wb
        return (
            (p1 + p2, x1 + x2, y1 + y2),
            (p1 - p2, x1 - x2, y1 - y2),
            (
                (h1 * xa + s1 * ya) + (s0 * xb + h0 * yb),
                gs1 * wa + gh0 * wb,
                gh1 * wa + gs0 * wb,
            ),
        )

    def four(field):
        base, along_x, along_y = field
        up, um = base + along_x, base - along_x
        return up + along_y, up - along_y, um + along_y, um - along_y

    inverse = 0.125 / thickness
    inverse_g = inverse * GAUSS

    def depth_four(parts):
        q0, qx, qy, qw = (
            parts[0] * inverse,
            parts[1] * inverse,
            parts[2] * inverse,
            parts[3] * inverse_g,
        )
        p, m, r, t = q0 + qx, q0 - qx, qy + qw, qy - qw
        return p + r, p - r, m + t, m - t

    za, zb, zc, zd = [depth_four(depth[comp]) for comp in range(4)]
    shear_ff = [za[k] * za[k] + zb[k] * zb[k] + STRAIN_EPS for k in range(4)]
    shear_fa = [za[k] * zc[k] + zb[k] * zd[k] for k in range(4)]
    yield
    total = None
    for part in (plus, minus):
        flow = [four(f) for f in plane_fields(part, 0)]
        other = [four(f) for f in plane_fields(part, 2)]
        for k in range(4):
            s, d, x = flow[0][k], flow[1][k], flow[2][k]
            triple = 3.0 * s
            effective = (triple * s + d * d) + (x * x + shear_ff[k])
            paired = (triple * other[0][k] + d * other[1][k]) + (x * other[2][k] + shear_fa[k])
            value = jnp.exp2(jnp.log2(effective) * (-1.0 / 3.0)) * paired
            total = value if total is None else total + value
            yield
    det = stretch[0:1] * stretch[1:2] - shear[0:1] * shear[1:2]
    return total * (rate * thickness / det)


def group_maps(retention, weight, term):
    layers, n = retention.shape
    row = lax.broadcasted_iota(jnp.int32, (layers, n), 0)
    factor, offset = retention, (1.0 - retention) * weight
    step = 1
    while step < layers:
        seen = row >= step
        before_f = jnp.where(seen, pltpu.roll(factor, step, 0), 1.0)
        before_o = jnp.where(seen, pltpu.roll(offset, step, 0), 0.0)
        offset = factor * before_o + offset
        factor = factor * before_f
        step *= 2
    return jnp.concatenate(
        [
            factor[layers - 1 :],
            offset[layers - 1 :],
            jnp.sum(factor * term, axis=0, keepdims=True),
            jnp.sum(offset * term, axis=0, keepdims=True),
        ],
        axis=0,
    )


def element_maps(tops, bots, params):
    layers = (params.shape[0] - 8) // 4
    thickness, rate, retention, weight = [
        params[i * layers : (i + 1) * layers] for i in range(4)
    ]
    stretch, shear = params[4 * layers : 4 * layers + 2], params[4 * layers + 2 : 4 * layers + 4]
    term = yield from terms(tops, bots, stretch, shear, thickness, rate)
    return group_maps(retention, weight, term)


def physics_kernel(fields, below, names, params, out, first, second):
    rows = fields.shape[0]
    layers = rows // 4
    elems = names.shape[1]
    chunk = first.shape[1]
    count = elems // chunk
    table = jnp.concatenate([node_table(fields), below_table(below[...])], axis=0)
    split = table.shape[0] * rows // (rows + 4)

    def gather(i, held):
        for c in range(4):
            wanted = names[c : c + 1, i * chunk : (i + 1) * chunk]
            high = wanted >> 8
            hot = one_hot(wanted & (SPAN - 1))
            picked = jnp.dot(table, hot, preferred_element_type=F32)
            yield
            for r in range(0, rows, 8):
                some = [picked[h + r : h + r + 8] for h in range(0, split, rows)]
                held[c * rows + r : c * rows + r + 8, :] = choose(
                    jnp.concatenate(some, axis=0), high, 8
                )
                yield
            low = 4 * rows + 8 * c
            held[low : low + 4, :] = choose(picked[split:], high, 4)

    def work(i, held):
        for k in range(chunk // LANES):
            cut = slice(k * LANES, (k + 1) * LANES)
            here = slice(i * chunk + k * LANES, i * chunk + (k + 1) * LANES)
            tops = [
                [
                    held[c * rows + m * layers : c * rows + (m + 1) * layers, cut]
                    for m in range(4)
                ]
                for c in range(4)
            ]
            ends = [held[4 * rows + 8 * c : 4 * rows + 8 * c + 4, cut] for c in range(4)]
            out[:, here] = yield from element_maps(tops, ends, params[:, here])

    held = (first, second)
    drain(gather(0, first))
    for i in range(count - 1):
        alternate(gather(i + 1, held[(i + 1) % 2]), work(i, held[i % 2]), 3)
    drain(work(count - 1, held[(count - 1) % 2]))


def border_kernel(state, data, picked, low, messages, out):
    elems = state.shape[1]
    rows = picked.shape[0] // 4
    layers = rows // 4
    slot = messages.shape[2]
    slots = 4 * slot
    place, count = lax.axis_index("plane"), messages.shape[0]
    out[:, :elems] = state[...]
    pieces = []
    for offset in OFFSETS:
        source = place + offset
        pieces.append(messages[jnp.clip(source, 0, count - 1)])
    got = jnp.concatenate(pieces, axis=1).astype(F32)
    mine = picked[...].astype(F32)
    ends = low[...].astype(F32)
    split = 4 * rows + 16
    half = (got.shape[0] - split) // 2
    here = data[...].astype(F32)
    sides = (
        (got, mine, got[4 * rows : split], ends, here[:half] + here[half:]),
        (mine, got, ends, got[4 * rows : split], got[split : split + half] + got[split + half :]),
    )
    for side, (corner0, others, end0, end_others, params) in enumerate(sides):
        for k in range(slots // LANES):
            cut = slice(k * LANES, (k + 1) * LANES)
            tops = [
                [
                    (others if c else corner0)[c * rows + m * layers : c * rows + (m + 1) * layers, cut]
                    for m in range(4)
                ]
                for c in range(4)
            ]
            bots = [(end_others if c else end0)[4 * c : 4 * c + 4, cut] for c in range(4)]
            start = elems + side * slots + k * LANES
            out[:, start : start + LANES] = drain(element_maps(tops, bots, params[:, cut]))


def sum_kernel(first, second, corners, lists, out):
    elems = corners.shape[1]
    slots = lists.shape[1]
    high_count = out.shape[0]
    owned = high_count * LANES
    column = 0.25 * (first[1:2, :] + second[1:2, :] + first[0:1, :] * second[0:1, :])
    main, ghost, near = (
        column[:, :elems],
        column[:, elems : elems + slots],
        column[:, elems + slots :],
    )
    main = jnp.where(corners[0:1, :] < owned, main, 0.0)
    work = [(corners[c : c + 1, :], main) for c in range(4)]
    work += [(lists[c : c + 1, :], ghost if c else near) for c in range(4)]
    total = None
    for at, (names, values) in enumerate(work):
        width = names.shape[1]
        if at >= 4:
            values = jnp.where(names < owned, values, 0.0)
        low, high = names & (LANES - 1), names >> 7
        coarse = values.astype(BF16).astype(F32)
        here = lax.broadcasted_iota(jnp.int32, (high_count, width), 0) == high
        parts = [jnp.where(here, coarse, 0.0), jnp.where(here, values - coarse, 0.0)]
        parts = jnp.concatenate(parts, axis=0).astype(BF16)
        hot = (lax.broadcasted_iota(jnp.int32, (LANES, width), 0) == low).astype(F32).astype(BF16)
        added = lax.dot_general(hot, parts, NT, preferred_element_type=F32)
        total = added if total is None else total + added
    total = total.T
    out[...] = total[:high_count] + total[high_count:]


def compose(one, two):
    return jnp.stack(
        [
            one[0] * two[0],
            two[0] * one[1] + two[1],
            one[2] + one[0] * two[2],
            one[3] + two[3] + one[1] * two[2],
        ]
    )


def shards(
    velocity, adjoint, corners, shared, stretch, shear_part, thickness, rate_factor, retention, weight
):
    layers, owned = velocity.shape[1:]
    elems = corners.shape[1]
    slot = shared.shape[1]
    slots = 4 * slot
    rows = 4 * layers
    shape = jax.ShapeDtypeStruct
    parts = lax.axis_size("plane")
    fields, top, params, names, sends = kernel_call(
        fetch_kernel,
        (
            shape((rows, owned), BF16),
            shape((4, owned), BF16),
            shape((rows + 8, elems), F32),
            shape(corners.shape, jnp.int32),
            shape((1, slots), jnp.int32),
        ),
        10**6,
        velocity, adjoint, corners, shared, thickness, rate_factor, retention, weight, stretch, shear_part,
        spaces="far",
        scratch=(
            pltpu.VMEM(velocity.shape, BF16),
            pltpu.VMEM(adjoint.shape, BF16),
            pltpu.VMEM(stretch.shape, F32),
            pltpu.VMEM(shear_part.shape, F32),
            pltpu.VMEM(shared.shape, jnp.int32),
            pltpu.SemaphoreType.DMA((10,)),
        ),
    )
    below = shifted(top, "layer", -1)
    data, lists, picked = kernel_call(
        element_kernel,
        (
            shape((2 * rows + 16, slots), BF16),
            shape((4, slots), jnp.int32),
            shape((4 * rows, slots), BF16),
        ),
        2 * 10**9,
        params, names, sends, fields,
    )
    low, messages = kernel_call(
        message_kernel,
        (shape((16, slots), BF16), shape((parts, 6 * rows + 32, slot), BF16)),
        10**9,
        below, lists, data, picked,
    )
    incoming = lax.all_to_all(messages, "plane", 0, 0)
    chunk = min(1024, elems)
    state = kernel_call(
        physics_kernel,
        shape((4, elems), F32),
        10**10,
        fields, below, names, params,
        scratch=(pltpu.VMEM((4 * rows + 32, chunk), F32),) * 2,
    )
    state = kernel_call(
        border_kernel,
        shape((4, elems + 2 * slots), F32),
        10**9,
        state, data, picked, low, incoming,
    )
    groups, place = lax.axis_size("layer"), lax.axis_index("layer")
    step = 1
    while 2 * step < groups:
        other = lax.ppermute(state, "layer", [(i, i ^ step) for i in range(groups)])
        second = (place & step) != 0
        state = compose(jnp.where(second, other, state), jnp.where(second, state, other))
        step *= 2
    mine = jnp.stack([jnp.where((place & step) != 0, state[2], state[1]), state[3]])
    other = jnp.zeros_like(mine)
    if groups > 1:
        other = lax.ppermute(mine, "layer", [(i, i ^ step) for i in range(groups)])
    gradient = kernel_call(
        sum_kernel,
        shape((owned // LANES, LANES), F32),
        2 * 10**9,
        mine, other, names, lists,
    )
    return gradient.reshape(owned)


def solution(mesh):
    return jax.shard_map(
        shards,
        mesh=mesh,
        in_specs=(
            P(None, "layer", "plane"),
            P(None, "layer", "plane"),
            P(None, "plane"),
            P(None, "plane"),
            P(None, "plane"),
            P(None, "plane"),
            P("layer", "plane"),
            P("layer", "plane"),
            P("layer", "plane"),
            P("layer", "plane"),
        ),
        out_specs=P("plane"),
        check_vma=False,
    )
```

```python
import math

import jax
import jax.numpy as jnp
from jax import lax
from jax.experimental import pallas as pl
from jax.experimental.pallas import tpu as pltpu
from jax.sharding import PartitionSpec as P

OFFSETS = (-2, -1, 1, 2)
STRAIN_EPS = 0.01
GAUSS = 1.0 / math.sqrt(3.0)
SPAN = 256
LANES = 128
TURN = 5
F32, BF16 = jnp.float32, jnp.bfloat16
NT = (((1,), (1,)), ((), ()))


def shifted(value, axis, steps):
    count = lax.axis_size(axis)
    first, last = (max(0, -steps), min(count, count - steps))
    return lax.ppermute(value, axis, [(source, source + steps) for source in range(first, last)])


def kernel_call(body, out_shape, flops, *args, spaces=None, scratch=()):
    vmem = pl.BlockSpec(memory_space=pltpu.VMEM)
    far = pl.BlockSpec(memory_space=pltpu.HBM)
    if spaces == "far":
        args = [pltpu.with_memory_space_constraint(value, pltpu.HBM) for value in args]
    return pl.pallas_call(
        body,
        out_shape=out_shape,
        in_specs=[far if spaces == "far" else vmem for _ in args],
        out_specs=jax.tree.map(lambda _: vmem, out_shape),
        scratch_shapes=list(scratch),
        compiler_params=pltpu.CompilerParams(vmem_limit_bytes=48 * 2**20),
        cost_estimate=pl.CostEstimate(flops=flops, bytes_accessed=2**20, transcendentals=0),
    )(*args)


def node_table(fields):
    blocks = fields.shape[1] // SPAN
    return jnp.concatenate([fields[:, h * SPAN : (h + 1) * SPAN] for h in range(blocks)], axis=0)


def below_table(below):
    wide = below.astype(F32)
    blocks = wide.shape[1] // SPAN
    return jnp.concatenate(
        [wide[:, h * SPAN : (h + 1) * SPAN] for h in range(blocks)], axis=0
    ).astype(BF16)


def one_hot(low):
    shape = (SPAN, low.shape[1])
    rows = lax.broadcasted_iota(jnp.int32, shape, 0).astype(F32).astype(BF16)
    wanted = jnp.broadcast_to(low.astype(F32).astype(BF16), shape)
    return jnp.where(rows == wanted, jnp.ones(shape, BF16), jnp.zeros(shape, BF16))


def choose(picked, high, rows):
    parts = [picked[i : i + rows] for i in range(0, picked.shape[0], rows)]
    bit = 1
    while len(parts) > 1:
        odd = (high & bit) != 0
        parts = [jnp.where(odd, parts[i + 1], parts[i]) for i in range(0, len(parts), 2)]
        bit *= 2
    return parts[0]


def alternate(first, second, ratio):
    pieces = [(first, 1), (second, ratio)]
    while pieces:
        left = []
        for piece, turns in pieces:
            for _ in range(turns):
                if next(piece, piece) is piece:
                    break
            else:
                left.append((piece, turns))
        pieces = left


def drain(piece):
    while True:
        try:
            next(piece)
        except StopIteration as end:
            return end.value


def fetch_kernel(
    velocity, adjoint, corners, shared, thickness, rate, retention, weight, stretch, shear,
    fields, top, params, names, sends,
    first, second, stretch_here, shear_here, shared_here, semaphores,
):
    layers, elems = thickness.shape
    pairs = [(velocity, first), (adjoint, second), (corners, names), (shared, shared_here)]
    pairs += [(stretch, stretch_here), (shear, shear_here)]
    for i, ref in enumerate((thickness, rate, retention, weight)):
        pairs.append((ref, params.at[pl.ds(i * layers, layers)]))
    copies = [
        pltpu.make_async_copy(source, target, semaphores.at[i])
        for i, (source, target) in enumerate(pairs)
    ]
    for copy in copies:
        copy.start()
    for copy in copies[:2]:
        copy.wait()
    parts = [first[0], first[1], second[0], second[1]]
    fields[...] = jnp.concatenate(parts, axis=0)
    wide = [part.astype(F32)[0:1] for part in parts]
    top[...] = jnp.concatenate(wide, axis=0).astype(BF16)
    for copy in copies[2:]:
        copy.wait()
    params[4 * layers :, :] = jnp.concatenate(
        [stretch_here[...], shear_here[...], jnp.zeros((4, elems), F32)], axis=0
    )
    sends[...] = jnp.concatenate([shared_here[j : j + 1, :] for j in range(4)], axis=1)


def turned(index, count):
    return index ^ TURN if count % 8 == 0 else index


def element_kernel(params, names, sends, fields, data, lists, picked, hots, messages):
    rows, owned = fields.shape
    layers = rows // 4
    elems = names.shape[1]
    slots = data.shape[1]
    slot = messages.shape[2]
    held = params.shape[0]
    here = names[...]
    values = params[...]
    coarse = values.astype(BF16).astype(F32)
    left = jnp.concatenate(
        [
            coarse,
            values - coarse,
            (here & (SPAN - 1)).astype(F32),
            (here >> 8).astype(F32),
            jnp.ones((8, elems), F32),
        ],
        axis=0,
    ).astype(BF16)
    wanted = lax.broadcasted_iota(jnp.int32, (slots, elems), 0) + owned
    mine = (wanted == here[0:1]).astype(F32).astype(BF16)
    total = lax.dot_general(left, mine, NT, preferred_element_type=F32)
    ids = (total[2 * held : 2 * held + 4] + total[2 * held + 4 : 2 * held + 8] * SPAN).astype(jnp.int32)
    ids = jnp.where(total[2 * held + 8 : 2 * held + 9] > 0.5, ids, owned)
    lists[...] = jnp.concatenate([sends[...], ids[1:4]], axis=0)
    stretch, shear, thickness, alpha, beta, factor, offset = group_maps(
        total[:held] + total[held : 2 * held]
    )
    data[...] = jnp.concatenate(
        [
            alpha, beta, thickness, stretch, shear,
            factor[layers - 1 :], offset[layers - 1 :], jnp.zeros((2, slots), F32),
        ],
        axis=0,
    )
    table = node_table(fields)
    for c in range(4):
        wanted = lists[c : c + 1, :]
        hot = one_hot(wanted & (SPAN - 1))
        hots[:, c * slots : (c + 1) * slots] = hot
        got = jnp.dot(table, hot, preferred_element_type=F32)
        picked[c * rows : (c + 1) * rows, :] = choose(got, wanted >> 8, rows).astype(BF16)
    place, count = lax.axis_index("plane"), messages.shape[0]
    coarse = data[...].astype(BF16)
    fine = (data[...] - coarse.astype(F32)).astype(BF16)
    for j, offset in enumerate(OFFSETS):
        at = slice(j * slot, (j + 1) * slot)
        target = place + offset

        @pl.when((target >= 0) & (target < count))
        def _():
            block = turned(target, count)
            messages[block, : 4 * rows, :] = picked[:, at]
            messages[block, 4 * rows + 16 :, :] = jnp.concatenate([coarse[:, at], fine[:, at]], axis=0)


def message_kernel(below, lists, hots, messages, low, out):
    table = below_table(below[...])
    slots = lists.shape[1]
    slot = out.shape[2]
    split = out.shape[1] - 80
    lower = []
    for c in range(4):
        hot = hots[:, c * slots : (c + 1) * slots]
        got = jnp.dot(table, hot, preferred_element_type=F32)
        lower.append(choose(got, lists[c : c + 1, :] >> 8, 4))
    low[...] = jnp.concatenate(lower, axis=0).astype(BF16)
    out[...] = messages[...]
    place, count = lax.axis_index("plane"), out.shape[0]
    for j, offset in enumerate(OFFSETS):
        at = slice(j * slot, (j + 1) * slot)
        target = place + offset

        @pl.when((target >= 0) & (target < count))
        def _():
            out[turned(target, count), split : split + 16, :] = low[:, at]


def plane_modes(a0, a1, a2, a3):
    s01, d01, s23, d23 = a0 + a1, a1 - a0, a2 + a3, a2 - a3
    return s01 + s23, d01 + d23, s23 - s01, d23 - d01


def terms(upper, bottom, stretch, shear, thickness):
    layers, n = thickness.shape
    last = lax.broadcasted_iota(jnp.int32, (layers, n), 0) == layers - 1
    plus, minus, depth = [], [], []
    ends = plane_modes(*bottom)
    for comp in range(4):
        top = plane_modes(*[upper[c][comp] for c in range(4)])
        end = [mode[comp : comp + 1] for mode in ends]
        under = [
            jnp.where(last, jnp.broadcast_to(e, t.shape), pltpu.roll(t, layers - 1, 0))
            for t, e in zip(top, end)
        ]
        depth_parts = [top[0] - under[0]]
        plus_parts, minus_parts = [], []
        for t, u in zip(top[1:], under[1:]):
            total, half = t + u, GAUSS * (t - u)
            plus_parts.append(total + half)
            minus_parts.append(total - half)
            depth_parts.append(half)
        plus.append(plus_parts)
        minus.append(minus_parts)
        depth.append(depth_parts)
        yield
    s0, s1 = stretch[0:1] * (1.0 / 16.0), stretch[1:2] * (1.0 / 16.0)
    h0, h1 = shear[0:1] * (1.0 / 16.0), shear[1:2] * (1.0 / 16.0)
    gs0, gs1, gh0, gh1 = s0 * GAUSS, s1 * GAUSS, h0 * GAUSS, h1 * GAUSS

    def plane_fields(part, first):
        (xa, ya, wa), (xb, yb, wb) = part[first], part[first + 1]
        p1, p2 = s0 * xa + h0 * ya, h1 * xb + s1 * yb
        x1, x2 = gh0 * wa, gs1 * wb
        y1, y2 = gs0 * wa, gh1 * wb
        return (
            (p1 + p2, x1 + x2, y1 + y2),
            (p1 - p2, x1 - x2, y1 - y2),
            (
                (h1 * xa + s1 * ya) + (s0 * xb + h0 * yb),
                gs1 * wa + gh0 * wb,
                gh1 * wa + gs0 * wb,
            ),
        )

    def four(field):
        base, along_x, along_y = field
        up, um = base + along_x, base - along_x
        return up + along_y, up - along_y, um + along_y, um - along_y

    inverse = 0.125 / thickness
    inverse_g = inverse * GAUSS

    def depth_four(parts):
        q0, qx, qy, qw = (
            parts[0] * inverse,
            parts[1] * inverse,
            parts[2] * inverse,
            parts[3] * inverse_g,
        )
        p, m, r, t = q0 + qx, q0 - qx, qy + qw, qy - qw
        return p + r, p - r, m + t, m - t

    za, zb, zc, zd = [depth_four(depth[comp]) for comp in range(4)]
    shear_ff = [za[k] * za[k] + zb[k] * zb[k] + STRAIN_EPS for k in range(4)]
    shear_fa = [za[k] * zc[k] + zb[k] * zd[k] for k in range(4)]
    yield
    total = None
    for part in (plus, minus):
        flow = [four(f) for f in plane_fields(part, 0)]
        other = [four(f) for f in plane_fields(part, 2)]
        for k in range(4):
            s, d, x = flow[0][k], flow[1][k], flow[2][k]
            triple = 3.0 * s
            effective = (triple * s + d * d) + (x * x + shear_ff[k])
            paired = (triple * other[0][k] + d * other[1][k]) + (x * other[2][k] + shear_fa[k])
            value = jnp.exp2(jnp.log2(effective) * (-1.0 / 3.0)) * paired
            total = value if total is None else total + value
            yield
    return total


def group_maps(params):
    layers = (params.shape[0] - 8) // 4
    thickness, rate, retention, weight = [
        params[i * layers : (i + 1) * layers] for i in range(4)
    ]
    stretch, shear = params[4 * layers : 4 * layers + 2], params[4 * layers + 2 : 4 * layers + 4]
    row = lax.broadcasted_iota(jnp.int32, retention.shape, 0)
    factor, offset = retention, (1.0 - retention) * weight
    step = 1
    while step < layers:
        seen = row >= step
        before_f = jnp.where(seen, pltpu.roll(factor, step, 0), 1.0)
        before_o = jnp.where(seen, pltpu.roll(offset, step, 0), 0.0)
        offset = factor * before_o + offset
        factor = factor * before_f
        step *= 2
    det = stretch[0:1] * stretch[1:2] - shear[0:1] * shear[1:2]
    gain = rate * thickness / det
    return stretch, shear, thickness, factor * gain, offset * gain, factor, offset


def column_state(factor, offset, alpha, beta, term):
    return jnp.concatenate(
        [
            factor,
            offset,
            jnp.sum(alpha * term, axis=0, keepdims=True),
            jnp.sum(beta * term, axis=0, keepdims=True),
        ],
        axis=0,
    )


def element_maps(tops, ends, params):
    stretch, shear, thickness, alpha, beta, factor, offset = group_maps(params)
    layers = thickness.shape[0]
    term = yield from terms(tops, ends, stretch, shear, thickness)
    return column_state(factor[layers - 1 :], offset[layers - 1 :], alpha, beta, term)


def physics_kernel(fields, below, names, params, out, first, second):
    rows = fields.shape[0]
    layers = rows // 4
    elems = names.shape[1]
    chunk = first.shape[1]
    count = elems // chunk
    table = jnp.concatenate([node_table(fields), below_table(below[...])], axis=0)
    split = table.shape[0] * rows // (rows + 4)

    def gather(i, held):
        for c in range(4):
            wanted = names[c : c + 1, i * chunk : (i + 1) * chunk]
            high = wanted >> 8
            hot = one_hot(wanted & (SPAN - 1))
            picked = jnp.dot(table, hot, preferred_element_type=F32)
            yield
            for r in range(0, rows, 8):
                some = [picked[h + r : h + r + 8] for h in range(0, split, rows)]
                held[c * rows + r : c * rows + r + 8, :] = choose(
                    jnp.concatenate(some, axis=0), high, 8
                )
                yield
            low = 4 * rows + 8 * c
            held[low : low + 4, :] = choose(picked[split:], high, 4)

    def work(i, held):
        for k in range(chunk // LANES):
            cut = slice(k * LANES, (k + 1) * LANES)
            here = slice(i * chunk + k * LANES, i * chunk + (k + 1) * LANES)
            tops = [
                [
                    held[c * rows + m * layers : c * rows + (m + 1) * layers, cut]
                    for m in range(4)
                ]
                for c in range(4)
            ]
            ends = [held[4 * rows + 8 * c : 4 * rows + 8 * c + 4, cut] for c in range(4)]
            out[:, here] = yield from element_maps(tops, ends, params[:, here])

    held = (first, second)
    drain(gather(0, first))
    for i in range(count - 1):
        alternate(gather(i + 1, held[(i + 1) % 2]), work(i, held[i % 2]), 3)
    drain(work(count - 1, held[(count - 1) % 2]))


def border_kernel(state, data, picked, low, messages, out):
    elems = state.shape[1]
    rows = picked.shape[0] // 4
    layers = rows // 4
    slot = messages.shape[2]
    slots = 4 * slot
    place, count = lax.axis_index("plane"), messages.shape[0]
    out[:, :elems] = state[...]
    pieces = []
    for offset in OFFSETS:
        source = jnp.clip(place + offset, 0, count - 1)
        pieces.append(messages[turned(source, count)])
    got = jnp.concatenate(pieces, axis=1).astype(F32)
    mine = picked[...].astype(F32)
    ends = low[...].astype(F32)
    split = 4 * rows + 16
    half = (got.shape[0] - split) // 2
    sides = (
        (got, mine, got[4 * rows : split], ends, data[...]),
        (mine, got, ends, got[4 * rows : split], got[split : split + half] + got[split + half :]),
    )
    for side, (corner0, others, end0, end_others, params) in enumerate(sides):
        for k in range(slots // LANES):
            cut = slice(k * LANES, (k + 1) * LANES)
            tops = [
                [
                    (others if c else corner0)[c * rows + m * layers : c * rows + (m + 1) * layers, cut]
                    for m in range(4)
                ]
                for c in range(4)
            ]
            bots = [(end_others if c else end0)[4 * c : 4 * c + 4, cut] for c in range(4)]
            start = elems + side * slots + k * LANES
            part = params[:, cut]
            alpha, beta, thickness = [part[i * layers : (i + 1) * layers] for i in range(3)]
            rest = part[3 * layers :]
            term = drain(terms(tops, bots, rest[:2], rest[2:4], thickness))
            out[:, start : start + LANES] = column_state(rest[4:5], rest[5:6], alpha, beta, term)


def sum_kernel(first, second, corners, lists, out):
    elems = corners.shape[1]
    slots = lists.shape[1]
    high_count = out.shape[0]
    owned = high_count * LANES
    column = 0.25 * (first[1:2, :] + second[1:2, :] + first[0:1, :] * second[0:1, :])
    main, ghost, near = (
        column[:, :elems],
        column[:, elems : elems + slots],
        column[:, elems + slots :],
    )
    main = jnp.where(corners[0:1, :] < owned, main, 0.0)
    work = [(corners[c : c + 1, :], main) for c in range(4)]
    work += [(lists[c : c + 1, :], ghost if c else near) for c in range(4)]
    total = None
    for at, (names, values) in enumerate(work):
        width = names.shape[1]
        if at >= 4:
            values = jnp.where(names < owned, values, 0.0)
        low, high = names & (LANES - 1), names >> 7
        coarse = values.astype(BF16).astype(F32)
        here = lax.broadcasted_iota(jnp.int32, (high_count, width), 0) == high
        parts = [jnp.where(here, coarse, 0.0), jnp.where(here, values - coarse, 0.0)]
        parts = jnp.concatenate(parts, axis=0).astype(BF16)
        hot = (lax.broadcasted_iota(jnp.int32, (LANES, width), 0) == low).astype(F32).astype(BF16)
        added = lax.dot_general(hot, parts, NT, preferred_element_type=F32)
        total = added if total is None else total + added
    total = total.T
    out[...] = total[:high_count] + total[high_count:]


def compose(one, two):
    return jnp.stack(
        [
            one[0] * two[0],
            two[0] * one[1] + two[1],
            one[2] + one[0] * two[2],
            one[3] + two[3] + one[1] * two[2],
        ]
    )


def shards(
    velocity, adjoint, corners, shared, stretch, shear_part, thickness, rate_factor, retention, weight
):
    layers, owned = velocity.shape[1:]
    elems = corners.shape[1]
    slot = shared.shape[1]
    slots = 4 * slot
    rows = 4 * layers
    shape = jax.ShapeDtypeStruct
    parts = lax.axis_size("plane")
    fields, top, params, names, sends = kernel_call(
        fetch_kernel,
        (
            shape((rows, owned), BF16),
            shape((4, owned), BF16),
            shape((rows + 8, elems), F32),
            shape(corners.shape, jnp.int32),
            shape((1, slots), jnp.int32),
        ),
        10**6,
        velocity, adjoint, corners, shared, thickness, rate_factor, retention, weight, stretch, shear_part,
        spaces="far",
        scratch=(
            pltpu.VMEM(velocity.shape, BF16),
            pltpu.VMEM(adjoint.shape, BF16),
            pltpu.VMEM(stretch.shape, F32),
            pltpu.VMEM(shear_part.shape, F32),
            pltpu.VMEM(shared.shape, jnp.int32),
            pltpu.SemaphoreType.DMA((10,)),
        ),
    )
    below = shifted(top, "layer", -1)
    data, lists, picked, hots, messages = kernel_call(
        element_kernel,
        (
            shape((rows, slots), F32),
            shape((4, slots), jnp.int32),
            shape((4 * rows, slots), BF16),
            shape((SPAN, 4 * slots), BF16),
            shape((parts, 6 * rows + 16, slot), BF16),
        ),
        2 * 10**9,
        params, names, sends, fields,
    )
    low, messages = kernel_call(
        message_kernel,
        (shape((16, slots), BF16), shape(messages.shape, BF16)),
        10**9,
        below, lists, hots, messages,
    )
    order = [turned(i, parts) for i in range(parts)]
    incoming = lax.all_to_all(messages, "plane", 0, 0, axis_index_groups=[order])
    chunk = min(1024, elems)
    state = kernel_call(
        physics_kernel,
        shape((4, elems), F32),
        10**10,
        fields, below, names, params,
        scratch=(pltpu.VMEM((4 * rows + 32, chunk), F32),) * 2,
    )
    state = kernel_call(
        border_kernel,
        shape((4, elems + 2 * slots), F32),
        10**9,
        state, data, picked, low, incoming,
    )
    groups, place = lax.axis_size("layer"), lax.axis_index("layer")
    step = 1
    while 2 * step < groups:
        other = lax.ppermute(state, "layer", [(i, i ^ step) for i in range(groups)])
        second = (place & step) != 0
        state = compose(jnp.where(second, other, state), jnp.where(second, state, other))
        step *= 2
    mine = jnp.stack([jnp.where((place & step) != 0, state[2], state[1]), state[3]])
    other = jnp.zeros_like(mine)
    if groups > 1:
        other = lax.ppermute(mine, "layer", [(i, i ^ step) for i in range(groups)])
    gradient = kernel_call(
        sum_kernel,
        shape((owned // LANES, LANES), F32),
        2 * 10**9,
        mine, other, names, lists,
    )
    return gradient.reshape(owned)


def solution(mesh):
    return jax.shard_map(
        shards,
        mesh=mesh,
        in_specs=(
            P(None, "layer", "plane"),
            P(None, "layer", "plane"),
            P(None, "plane"),
            P(None, "plane"),
            P(None, "plane"),
            P(None, "plane"),
            P("layer", "plane"),
            P("layer", "plane"),
            P("layer", "plane"),
            P("layer", "plane"),
        ),
        out_specs=P("plane"),
        check_vma=False,
    )
```

```python
import math

import jax
import jax.numpy as jnp
from jax import lax
from jax.experimental import pallas as pl
from jax.experimental.pallas import tpu as pltpu
from jax.sharding import PartitionSpec as P

OFFSETS = (-2, -1, 1, 2)
STRAIN_EPS = 0.01
GAUSS = 1.0 / math.sqrt(3.0)
SPAN = 256
LANES = 128
TURN = 5
F32, BF16 = jnp.float32, jnp.bfloat16
NT = (((1,), (1,)), ((), ()))


def shifted(value, axis, steps):
    count = lax.axis_size(axis)
    first, last = (max(0, -steps), min(count, count - steps))
    return lax.ppermute(value, axis, [(source, source + steps) for source in range(first, last)])


def kernel_call(body, out_shape, flops, *args, spaces=None, scratch=()):
    vmem = pl.BlockSpec(memory_space=pltpu.VMEM)
    far = pl.BlockSpec(memory_space=pltpu.HBM)
    if spaces == "far":
        args = [pltpu.with_memory_space_constraint(value, pltpu.HBM) for value in args]
    return pl.pallas_call(
        body,
        out_shape=out_shape,
        in_specs=[far if spaces == "far" else vmem for _ in args],
        out_specs=jax.tree.map(lambda _: vmem, out_shape),
        scratch_shapes=list(scratch),
        compiler_params=pltpu.CompilerParams(vmem_limit_bytes=48 * 2**20),
        cost_estimate=pl.CostEstimate(flops=flops, bytes_accessed=2**20, transcendentals=0),
    )(*args)


def node_table(fields):
    blocks = fields.shape[1] // SPAN
    return jnp.concatenate([fields[:, h * SPAN : (h + 1) * SPAN] for h in range(blocks)], axis=0)


def below_table(below):
    wide = below.astype(F32)
    blocks = wide.shape[1] // SPAN
    return jnp.concatenate(
        [wide[:, h * SPAN : (h + 1) * SPAN] for h in range(blocks)], axis=0
    ).astype(BF16)


def one_hot(low):
    shape = (SPAN, low.shape[1])
    rows = lax.broadcasted_iota(jnp.int32, shape, 0).astype(F32).astype(BF16)
    wanted = jnp.broadcast_to(low.astype(F32).astype(BF16), shape)
    return jnp.where(rows == wanted, jnp.ones(shape, BF16), jnp.zeros(shape, BF16))


def bit_masks(high, blocks):
    wide = jnp.broadcast_to(high, (8, high.shape[1]))
    return [(wide & (1 << k)) != 0 for k in range(blocks.bit_length() - 1)]


def choose(parts, masks):
    for mask in masks:
        parts = [jnp.where(mask, parts[i + 1], parts[i]) for i in range(0, len(parts), 2)]
    return parts[0]


def choose_rows(picked, masks, rows, r):
    return choose([picked[h + r : h + r + 8] for h in range(0, picked.shape[0], rows)], masks)


def choose_low(picked, masks):
    pair = choose([picked[h : h + 8] for h in range(0, picked.shape[0], 8)], masks[1:])
    return jnp.where(masks[0][:4], pair[4:], pair[:4])


def product(table, hot):
    return jnp.dot(table, hot, preferred_element_type=F32)


def alternate(first, second, ratio):
    pieces = [(first, 1), (second, ratio)]
    while pieces:
        left = []
        for piece, turns in pieces:
            for _ in range(turns):
                if next(piece, piece) is piece:
                    break
            else:
                left.append((piece, turns))
        pieces = left


def drain(piece):
    while True:
        try:
            next(piece)
        except StopIteration as end:
            return end.value


def fetch_kernel(
    velocity, adjoint, corners, shared, thickness, rate, retention, weight, stretch, shear,
    fields, top, params, names, sends,
    first, second, stretch_here, shear_here, shared_here, semaphores,
):
    layers, elems = thickness.shape
    pairs = [(velocity, first), (adjoint, second), (corners, names), (shared, shared_here)]
    pairs += [(stretch, stretch_here), (shear, shear_here)]
    for i, ref in enumerate((thickness, rate, retention, weight)):
        pairs.append((ref, params.at[pl.ds(i * layers, layers)]))
    copies = [
        pltpu.make_async_copy(source, target, semaphores.at[i])
        for i, (source, target) in enumerate(pairs)
    ]
    for copy in copies:
        copy.start()
    for copy in copies[:2]:
        copy.wait()
    parts = [first[0], first[1], second[0], second[1]]
    fields[...] = jnp.concatenate(parts, axis=0)
    wide = [part.astype(F32)[0:1] for part in parts]
    top[...] = jnp.concatenate(wide, axis=0).astype(BF16)
    for copy in copies[2:]:
        copy.wait()
    params[4 * layers :, :] = jnp.concatenate(
        [stretch_here[...], shear_here[...], jnp.zeros((4, elems), F32)], axis=0
    )
    sends[...] = jnp.concatenate([shared_here[j : j + 1, :] for j in range(4)], axis=1)


def turned(index, count):
    return index ^ TURN if count % 8 == 0 else index


def element_kernel(
    params, names, sends, fields, data, lists, picked, hots, messages, early, early_hots
):
    rows, owned = fields.shape
    layers = rows // 4
    elems = names.shape[1]
    slots = data.shape[1]
    slot = messages.shape[2]
    held = params.shape[0]
    here = names[...]
    values = params[...]
    coarse = values.astype(BF16).astype(F32)
    left = jnp.concatenate(
        [
            coarse,
            values - coarse,
            (here & (SPAN - 1)).astype(F32),
            (here >> 8).astype(F32),
            jnp.ones((8, elems), F32),
        ],
        axis=0,
    ).astype(BF16)
    wanted = lax.broadcasted_iota(jnp.int32, (slots, elems), 0) + owned
    mine = (wanted == here[0:1]).astype(F32).astype(BF16)
    total = lax.dot_general(left, mine, NT, preferred_element_type=F32)
    ids = (total[2 * held : 2 * held + 4] + total[2 * held + 4 : 2 * held + 8] * SPAN).astype(jnp.int32)
    ids = jnp.where(total[2 * held + 8 : 2 * held + 9] > 0.5, ids, owned)
    lists[...] = jnp.concatenate([sends[...], ids[1:4]], axis=0)
    stretch, shear, thickness, alpha, beta, factor, offset = group_maps(
        total[:held] + total[held : 2 * held]
    )
    data[...] = jnp.concatenate(
        [
            alpha, beta, thickness, stretch, shear,
            factor[layers - 1 :], offset[layers - 1 :], jnp.zeros((2, slots), F32),
        ],
        axis=0,
    )
    table = node_table(fields)
    for c in range(4):
        wanted = lists[c : c + 1, :]
        hot = one_hot(wanted & (SPAN - 1))
        hots[:, c * slots : (c + 1) * slots] = hot
        got = product(table, hot)
        masks = bit_masks(wanted >> 8, owned // SPAN)
        for r in range(0, rows, 8):
            at = slice(c * rows + r, c * rows + r + 8)
            picked[at, :] = choose_rows(got, masks, rows, r).astype(BF16)
    chunk = early.shape[1]
    for c in range(4):
        wanted = names[c : c + 1, :chunk]
        hot = one_hot(wanted & (SPAN - 1))
        early_hots[:, c * chunk : (c + 1) * chunk] = hot
        got = product(table, hot)
        masks = bit_masks(wanted >> 8, owned // SPAN)
        for r in range(0, rows, 8):
            early[c * rows + r : c * rows + r + 8, :] = choose_rows(got, masks, rows, r)
    place, count = lax.axis_index("plane"), messages.shape[0]
    coarse = data[...].astype(BF16)
    fine = (data[...] - coarse.astype(F32)).astype(BF16)
    for j, offset in enumerate(OFFSETS):
        at = slice(j * slot, (j + 1) * slot)
        target = place + offset

        @pl.when((target >= 0) & (target < count))
        def _():
            block = turned(target, count)
            messages[block, : 4 * rows, :] = picked[:, at]
            messages[block, 4 * rows + 16 :, :] = jnp.concatenate([coarse[:, at], fine[:, at]], axis=0)


def message_kernel(below, lists, hots, messages, low, out):
    table = below_table(below[...])
    slots = lists.shape[1]
    slot = out.shape[2]
    split = out.shape[1] - 80
    lower = []
    for c in range(4):
        hot = hots[:, c * slots : (c + 1) * slots]
        masks = bit_masks(lists[c : c + 1, :] >> 8, below.shape[1] // SPAN)
        lower.append(choose_low(product(table, hot), masks))
    low[...] = jnp.concatenate(lower, axis=0).astype(BF16)
    out[...] = messages[...]
    place, count = lax.axis_index("plane"), out.shape[0]
    for j, offset in enumerate(OFFSETS):
        at = slice(j * slot, (j + 1) * slot)
        target = place + offset

        @pl.when((target >= 0) & (target < count))
        def _():
            out[turned(target, count), split : split + 16, :] = low[:, at]


def plane_modes(a0, a1, a2, a3):
    s01, d01, s23, d23 = a0 + a1, a1 - a0, a2 + a3, a2 - a3
    return s01 + s23, d01 + d23, s23 - s01, d23 - d01


def terms(upper, bottom, stretch, shear, thickness):
    layers, n = thickness.shape
    last = lax.broadcasted_iota(jnp.int32, (layers, n), 0) == layers - 1
    plus, minus, depth = [], [], []
    ends = plane_modes(*bottom)
    for comp in range(4):
        top = plane_modes(*[upper[c][comp] for c in range(4)])
        end = [mode[comp : comp + 1] for mode in ends]
        under = [
            jnp.where(last, jnp.broadcast_to(e, t.shape), pltpu.roll(t, layers - 1, 0))
            for t, e in zip(top, end)
        ]
        depth_parts = [top[0] - under[0]]
        plus_parts, minus_parts = [], []
        for t, u in zip(top[1:], under[1:]):
            total, half = t + u, GAUSS * (t - u)
            plus_parts.append(total + half)
            minus_parts.append(total - half)
            depth_parts.append(half)
        plus.append(plus_parts)
        minus.append(minus_parts)
        depth.append(depth_parts)
        yield
    s0, s1 = stretch[0:1] * (1.0 / 16.0), stretch[1:2] * (1.0 / 16.0)
    h0, h1 = shear[0:1] * (1.0 / 16.0), shear[1:2] * (1.0 / 16.0)
    gs0, gs1, gh0, gh1 = s0 * GAUSS, s1 * GAUSS, h0 * GAUSS, h1 * GAUSS

    def plane_fields(part, first):
        (xa, ya, wa), (xb, yb, wb) = part[first], part[first + 1]
        p1, p2 = s0 * xa + h0 * ya, h1 * xb + s1 * yb
        x1, x2 = gh0 * wa, gs1 * wb
        y1, y2 = gs0 * wa, gh1 * wb
        return (
            (p1 + p2, x1 + x2, y1 + y2),
            (p1 - p2, x1 - x2, y1 - y2),
            (
                (h1 * xa + s1 * ya) + (s0 * xb + h0 * yb),
                gs1 * wa + gh0 * wb,
                gh1 * wa + gs0 * wb,
            ),
        )

    def four(field):
        base, along_x, along_y = field
        up, um = base + along_x, base - along_x
        return up + along_y, up - along_y, um + along_y, um - along_y

    inverse = 0.125 / thickness
    inverse_g = inverse * GAUSS

    def depth_four(parts):
        q0, qx, qy, qw = (
            parts[0] * inverse,
            parts[1] * inverse,
            parts[2] * inverse,
            parts[3] * inverse_g,
        )
        p, m, r, t = q0 + qx, q0 - qx, qy + qw, qy - qw
        return p + r, p - r, m + t, m - t

    za, zb, zc, zd = [depth_four(depth[comp]) for comp in range(4)]
    shear_ff = [za[k] * za[k] + zb[k] * zb[k] + STRAIN_EPS for k in range(4)]
    shear_fa = [za[k] * zc[k] + zb[k] * zd[k] for k in range(4)]
    yield
    total = None
    for part in (plus, minus):
        flow = [four(f) for f in plane_fields(part, 0)]
        other = [four(f) for f in plane_fields(part, 2)]
        for k in range(4):
            s, d, x = flow[0][k], flow[1][k], flow[2][k]
            triple = 3.0 * s
            effective = (triple * s + d * d) + (x * x + shear_ff[k])
            paired = (triple * other[0][k] + d * other[1][k]) + (x * other[2][k] + shear_fa[k])
            value = jnp.exp2(jnp.log2(effective) * (-1.0 / 3.0)) * paired
            total = value if total is None else total + value
            yield
    return total


def group_maps(params):
    layers = (params.shape[0] - 8) // 4
    thickness, rate, retention, weight = [
        params[i * layers : (i + 1) * layers] for i in range(4)
    ]
    stretch, shear = params[4 * layers : 4 * layers + 2], params[4 * layers + 2 : 4 * layers + 4]
    row = lax.broadcasted_iota(jnp.int32, retention.shape, 0)
    factor, offset = retention, (1.0 - retention) * weight
    step = 1
    while step < layers:
        seen = row >= step
        before_f = jnp.where(seen, pltpu.roll(factor, step, 0), 1.0)
        before_o = jnp.where(seen, pltpu.roll(offset, step, 0), 0.0)
        offset = factor * before_o + offset
        factor = factor * before_f
        step *= 2
    det = stretch[0:1] * stretch[1:2] - shear[0:1] * shear[1:2]
    gain = rate * thickness / det
    return stretch, shear, thickness, factor * gain, offset * gain, factor, offset


def column_state(factor, offset, alpha, beta, term):
    return jnp.concatenate(
        [
            factor,
            offset,
            jnp.sum(alpha * term, axis=0, keepdims=True),
            jnp.sum(beta * term, axis=0, keepdims=True),
        ],
        axis=0,
    )


def element_maps(tops, ends, params):
    stretch, shear, thickness, alpha, beta, factor, offset = group_maps(params)
    layers = thickness.shape[0]
    term = yield from terms(tops, ends, stretch, shear, thickness)
    return column_state(factor[layers - 1 :], offset[layers - 1 :], alpha, beta, term)


def physics_kernel(
    fields, below, names, params, early, early_hots, out, first, second, low_first, low_second
):
    rows, owned = fields.shape
    layers = rows // 4
    elems = names.shape[1]
    chunk = first.shape[1]
    count = elems // chunk
    low_table = below_table(below[...])
    table = jnp.concatenate([node_table(fields), low_table], axis=0)
    split = table.shape[0] - low_table.shape[0]
    blocks = owned // SPAN

    def gather(i, held, low):
        for c in range(4):
            wanted = names[c : c + 1, i * chunk : (i + 1) * chunk]
            masks = bit_masks(wanted >> 8, blocks)
            picked = product(table, one_hot(wanted & (SPAN - 1)))
            yield
            for r in range(0, rows, 8):
                at = slice(c * rows + r, c * rows + r + 8)
                held[at, :] = choose_rows(picked[:split], masks, rows, r)
                yield
            low[8 * c : 8 * c + 4, :] = choose_low(picked[split:], masks)

    def work(i, held, low):
        for k in range(chunk // LANES):
            cut = slice(k * LANES, (k + 1) * LANES)
            here = slice(i * chunk + k * LANES, i * chunk + (k + 1) * LANES)
            tops = [
                [
                    held[c * rows + m * layers : c * rows + (m + 1) * layers, cut]
                    for m in range(4)
                ]
                for c in range(4)
            ]
            ends = [low[8 * c : 8 * c + 4, cut] for c in range(4)]
            out[:, here] = yield from element_maps(tops, ends, params[:, here])

    for c in range(4):
        masks = bit_masks(names[c : c + 1, :chunk] >> 8, blocks)
        picked = product(low_table, early_hots[:, c * chunk : (c + 1) * chunk])
        low_first[8 * c : 8 * c + 4, :] = choose_low(picked, masks)
    held = (early, low_first)
    spare = [(second, low_second), (first, low_first)]
    for i in range(count - 1):
        following = spare[i % 2]
        alternate(gather(i + 1, *following), work(i, *held), 3)
        held = following
    drain(work(count - 1, *held))


def border_kernel(state, data, picked, low, messages, out):
    elems = state.shape[1]
    rows = picked.shape[0] // 4
    layers = rows // 4
    slot = messages.shape[2]
    slots = 4 * slot
    place, count = lax.axis_index("plane"), messages.shape[0]
    out[:, :elems] = state[...]
    pieces = []
    for offset in OFFSETS:
        source = jnp.clip(place + offset, 0, count - 1)
        pieces.append(messages[turned(source, count)])
    got = jnp.concatenate(pieces, axis=1).astype(F32)
    mine = picked[...].astype(F32)
    ends = low[...].astype(F32)
    split = 4 * rows + 16
    half = (got.shape[0] - split) // 2
    sides = (
        (got, mine, got[4 * rows : split], ends, data[...]),
        (mine, got, ends, got[4 * rows : split], got[split : split + half] + got[split + half :]),
    )
    for side, (corner0, others, end0, end_others, params) in enumerate(sides):
        for k in range(slots // LANES):
            cut = slice(k * LANES, (k + 1) * LANES)
            tops = [
                [
                    (others if c else corner0)[c * rows + m * layers : c * rows + (m + 1) * layers, cut]
                    for m in range(4)
                ]
                for c in range(4)
            ]
            bots = [(end_others if c else end0)[4 * c : 4 * c + 4, cut] for c in range(4)]
            start = elems + side * slots + k * LANES
            part = params[:, cut]
            alpha, beta, thickness = [part[i * layers : (i + 1) * layers] for i in range(3)]
            rest = part[3 * layers :]
            term = drain(terms(tops, bots, rest[:2], rest[2:4], thickness))
            out[:, start : start + LANES] = column_state(rest[4:5], rest[5:6], alpha, beta, term)


def sum_kernel(first, second, corners, lists, out):
    elems = corners.shape[1]
    slots = lists.shape[1]
    high_count = out.shape[0]
    owned = high_count * LANES
    column = 0.25 * (first[1:2, :] + second[1:2, :] + first[0:1, :] * second[0:1, :])
    main, ghost, near = (
        column[:, :elems],
        column[:, elems : elems + slots],
        column[:, elems + slots :],
    )
    main = jnp.where(corners[0:1, :] < owned, main, 0.0)
    work = [(corners[c : c + 1, :], main) for c in range(4)]
    work += [(lists[c : c + 1, :], ghost if c else near) for c in range(4)]
    total = None
    for at, (names, values) in enumerate(work):
        width = names.shape[1]
        if at >= 4:
            values = jnp.where(names < owned, values, 0.0)
        low, high = names & (LANES - 1), names >> 7
        coarse = values.astype(BF16).astype(F32)
        here = lax.broadcasted_iota(jnp.int32, (high_count, width), 0) == high
        parts = [jnp.where(here, coarse, 0.0), jnp.where(here, values - coarse, 0.0)]
        parts = jnp.concatenate(parts, axis=0).astype(BF16)
        hot = (lax.broadcasted_iota(jnp.int32, (LANES, width), 0) == low).astype(F32).astype(BF16)
        added = lax.dot_general(hot, parts, NT, preferred_element_type=F32)
        total = added if total is None else total + added
    total = total.T
    out[...] = total[:high_count] + total[high_count:]


def compose(one, two):
    return jnp.stack(
        [
            one[0] * two[0],
            two[0] * one[1] + two[1],
            one[2] + one[0] * two[2],
            one[3] + two[3] + one[1] * two[2],
        ]
    )


def shards(
    velocity, adjoint, corners, shared, stretch, shear_part, thickness, rate_factor, retention, weight
):
    layers, owned = velocity.shape[1:]
    elems = corners.shape[1]
    slot = shared.shape[1]
    slots = 4 * slot
    rows = 4 * layers
    shape = jax.ShapeDtypeStruct
    parts = lax.axis_size("plane")
    fields, top, params, names, sends = kernel_call(
        fetch_kernel,
        (
            shape((rows, owned), BF16),
            shape((4, owned), BF16),
            shape((rows + 8, elems), F32),
            shape(corners.shape, jnp.int32),
            shape((1, slots), jnp.int32),
        ),
        10**6,
        velocity, adjoint, corners, shared, thickness, rate_factor, retention, weight, stretch, shear_part,
        spaces="far",
        scratch=(
            pltpu.VMEM(velocity.shape, BF16),
            pltpu.VMEM(adjoint.shape, BF16),
            pltpu.VMEM(stretch.shape, F32),
            pltpu.VMEM(shear_part.shape, F32),
            pltpu.VMEM(shared.shape, jnp.int32),
            pltpu.SemaphoreType.DMA((10,)),
        ),
    )
    below = shifted(top, "layer", -1)
    chunk = min(1024, elems)
    data, lists, picked, hots, messages, early, early_hots = kernel_call(
        element_kernel,
        (
            shape((rows, slots), F32),
            shape((4, slots), jnp.int32),
            shape((4 * rows, slots), BF16),
            shape((SPAN, 4 * slots), BF16),
            shape((parts, 6 * rows + 16, slot), BF16),
            shape((4 * rows, chunk), F32),
            shape((SPAN, 4 * chunk), BF16),
        ),
        2 * 10**9,
        params, names, sends, fields,
    )
    low, messages = kernel_call(
        message_kernel,
        (shape((16, slots), BF16), shape(messages.shape, BF16)),
        10**9,
        below, lists, hots, messages,
    )
    order = [turned(i, parts) for i in range(parts)]
    incoming = lax.all_to_all(messages, "plane", 0, 0, axis_index_groups=[order])
    state = kernel_call(
        physics_kernel,
        shape((4, elems), F32),
        10**10,
        fields, below, names, params, early, early_hots,
        scratch=(pltpu.VMEM((4 * rows, chunk), F32),) * 2 + (pltpu.VMEM((32, chunk), F32),) * 2,
    )
    state = kernel_call(
        border_kernel,
        shape((4, elems + 2 * slots), F32),
        10**9,
        state, data, picked, low, incoming,
    )
    groups, place = lax.axis_size("layer"), lax.axis_index("layer")
    step = 1
    while 2 * step < groups:
        other = lax.ppermute(state, "layer", [(i, i ^ step) for i in range(groups)])
        second = (place & step) != 0
        state = compose(jnp.where(second, other, state), jnp.where(second, state, other))
        step *= 2
    mine = jnp.stack([jnp.where((place & step) != 0, state[2], state[1]), state[3]])
    other = jnp.zeros_like(mine)
    if groups > 1:
        other = lax.ppermute(mine, "layer", [(i, i ^ step) for i in range(groups)])
    gradient = kernel_call(
        sum_kernel,
        shape((owned // LANES, LANES), F32),
        2 * 10**9,
        mine, other, names, lists,
    )
    return gradient.reshape(owned)


def solution(mesh):
    return jax.shard_map(
        shards,
        mesh=mesh,
        in_specs=(
            P(None, "layer", "plane"),
            P(None, "layer", "plane"),
            P(None, "plane"),
            P(None, "plane"),
            P(None, "plane"),
            P(None, "plane"),
            P("layer", "plane"),
            P("layer", "plane"),
            P("layer", "plane"),
            P("layer", "plane"),
        ),
        out_specs=P("plane"),
        check_vma=False,
    )
```

```python
import math

import jax
import jax.numpy as jnp
from jax import lax
from jax.experimental import pallas as pl
from jax.experimental.pallas import tpu as pltpu
from jax.sharding import PartitionSpec as P

OFFSETS = (-2, -1, 1, 2)
STRAIN_EPS = 0.01
GAUSS = 1.0 / math.sqrt(3.0)
SPAN = 256
LANES = 128
TURN = 5
F32, BF16 = jnp.float32, jnp.bfloat16
NT = (((1,), (1,)), ((), ()))


def shifted(value, axis, steps):
    count = lax.axis_size(axis)
    first, last = (max(0, -steps), min(count, count - steps))
    return lax.ppermute(value, axis, [(source, source + steps) for source in range(first, last)])


def kernel_call(body, out_shape, flops, *args, spaces=None, scratch=()):
    vmem = pl.BlockSpec(memory_space=pltpu.VMEM)
    far = pl.BlockSpec(memory_space=pltpu.HBM)
    if spaces == "far":
        args = [pltpu.with_memory_space_constraint(value, pltpu.HBM) for value in args]
    return pl.pallas_call(
        body,
        out_shape=out_shape,
        in_specs=[far if spaces == "far" else vmem for _ in args],
        out_specs=jax.tree.map(lambda _: vmem, out_shape),
        scratch_shapes=list(scratch),
        compiler_params=pltpu.CompilerParams(vmem_limit_bytes=24 * 2**20),
        cost_estimate=pl.CostEstimate(flops=flops, bytes_accessed=2**20, transcendentals=0),
    )(*args)


def node_table(fields):
    blocks = fields.shape[1] // SPAN
    return jnp.concatenate([fields[:, h * SPAN : (h + 1) * SPAN] for h in range(blocks)], axis=0)


def below_table(below):
    wide = below.astype(F32)
    blocks = wide.shape[1] // SPAN
    return jnp.concatenate(
        [wide[:, h * SPAN : (h + 1) * SPAN] for h in range(blocks)], axis=0
    ).astype(BF16)


def one_hot(low):
    shape = (SPAN, low.shape[1])
    rows = lax.broadcasted_iota(jnp.int32, shape, 0).astype(F32).astype(BF16)
    wanted = jnp.broadcast_to(low.astype(F32).astype(BF16), shape)
    return jnp.where(rows == wanted, jnp.ones(shape, BF16), jnp.zeros(shape, BF16))


def bit_masks(high, blocks):
    wide = jnp.broadcast_to(high, (8, high.shape[1]))
    return [(wide & (1 << k)) != 0 for k in range(blocks.bit_length() - 1)]


def choose(parts, masks):
    for mask in masks:
        parts = [jnp.where(mask, parts[i + 1], parts[i]) for i in range(0, len(parts), 2)]
    return parts[0]


def choose_rows(picked, masks, rows, r):
    return choose([picked[h + r : h + r + 8] for h in range(0, picked.shape[0], rows)], masks)


def choose_low(picked, masks):
    pair = choose([picked[h : h + 8] for h in range(0, picked.shape[0], 8)], masks[1:])
    return jnp.where(masks[0][:4], pair[4:], pair[:4])


def product(table, hot):
    return jnp.dot(table, hot, preferred_element_type=F32)


def alternate(first, second, ratio):
    pieces = [(first, 1), (second, ratio)]
    while pieces:
        left = []
        for piece, turns in pieces:
            for _ in range(turns):
                if next(piece, piece) is piece:
                    break
            else:
                left.append((piece, turns))
        pieces = left


def drain(piece):
    while True:
        try:
            next(piece)
        except StopIteration as end:
            return end.value


def fetch_kernel(
    velocity, adjoint, corners, shared, thickness, rate, retention, weight, stretch, shear,
    fields, top, params, names, sends,
    first, second, stretch_here, shear_here, shared_here, semaphores,
):
    layers, elems = thickness.shape
    pairs = [(velocity, first), (adjoint, second), (corners, names), (shared, shared_here)]
    pairs += [(stretch, stretch_here), (shear, shear_here)]
    for i, ref in enumerate((thickness, rate, retention, weight)):
        pairs.append((ref, params.at[pl.ds(i * layers, layers)]))
    copies = [
        pltpu.make_async_copy(source, target, semaphores.at[i])
        for i, (source, target) in enumerate(pairs)
    ]
    for copy in copies:
        copy.start()
    for copy in copies[:2]:
        copy.wait()
    parts = [first[0], first[1], second[0], second[1]]
    fields[...] = jnp.concatenate(parts, axis=0)
    wide = [part.astype(F32)[0:1] for part in parts]
    top[...] = jnp.concatenate(wide, axis=0).astype(BF16)
    for copy in copies[2:]:
        copy.wait()
    params[4 * layers :, :] = jnp.concatenate(
        [stretch_here[...], shear_here[...], jnp.zeros((4, elems), F32)], axis=0
    )
    sends[...] = jnp.concatenate([shared_here[j : j + 1, :] for j in range(4)], axis=1)


def turned(index, count):
    return index ^ TURN if count % 8 == 0 else index


def element_kernel(
    params, names, sends, fields, data, lists, picked, hots, messages, early, early_hots
):
    rows, owned = fields.shape
    layers = rows // 4
    elems = names.shape[1]
    slots = data.shape[1]
    slot = messages.shape[2]
    held = params.shape[0]
    here = names[...]
    values = params[...]
    coarse = values.astype(BF16).astype(F32)
    left = jnp.concatenate(
        [
            coarse,
            values - coarse,
            (here & (SPAN - 1)).astype(F32),
            (here >> 8).astype(F32),
            jnp.ones((8, elems), F32),
        ],
        axis=0,
    ).astype(BF16)
    wanted = lax.broadcasted_iota(jnp.int32, (slots, elems), 0) + owned
    mine = (wanted == here[0:1]).astype(F32).astype(BF16)
    total = lax.dot_general(left, mine, NT, preferred_element_type=F32)
    ids = (total[2 * held : 2 * held + 4] + total[2 * held + 4 : 2 * held + 8] * SPAN).astype(jnp.int32)
    ids = jnp.where(total[2 * held + 8 : 2 * held + 9] > 0.5, ids, owned)
    lists[...] = jnp.concatenate([sends[...], ids[1:4]], axis=0)
    stretch, shear, thickness, alpha, beta, factor, offset = group_maps(
        total[:held] + total[held : 2 * held]
    )
    data[...] = jnp.concatenate(
        [
            alpha, beta, thickness, stretch, shear,
            factor[layers - 1 :], offset[layers - 1 :], jnp.zeros((2, slots), F32),
        ],
        axis=0,
    )
    table = node_table(fields)
    for c in range(4):
        wanted = lists[c : c + 1, :]
        hot = one_hot(wanted & (SPAN - 1))
        hots[:, c * slots : (c + 1) * slots] = hot
        got = product(table, hot)
        masks = bit_masks(wanted >> 8, owned // SPAN)
        for r in range(0, rows, 8):
            at = slice(c * rows + r, c * rows + r + 8)
            picked[at, :] = choose_rows(got, masks, rows, r).astype(BF16)
    chunk = early.shape[1]
    for c in range(4):
        wanted = names[c : c + 1, :chunk]
        hot = one_hot(wanted & (SPAN - 1))
        early_hots[:, c * chunk : (c + 1) * chunk] = hot
        got = product(table, hot)
        masks = bit_masks(wanted >> 8, owned // SPAN)
        for r in range(0, rows, 8):
            early[c * rows + r : c * rows + r + 8, :] = choose_rows(got, masks, rows, r)
    place, count = lax.axis_index("plane"), messages.shape[0]
    coarse = data[...].astype(BF16)
    fine = (data[...] - coarse.astype(F32)).astype(BF16)
    for j, offset in enumerate(OFFSETS):
        at = slice(j * slot, (j + 1) * slot)
        target = place + offset

        @pl.when((target >= 0) & (target < count))
        def _():
            block = turned(target, count)
            messages[block, : 4 * rows, :] = picked[:, at]
            messages[block, 4 * rows + 16 :, :] = jnp.concatenate([coarse[:, at], fine[:, at]], axis=0)


def message_kernel(below, lists, hots, messages, low, out):
    table = below_table(below[...])
    slots = lists.shape[1]
    slot = out.shape[2]
    split = out.shape[1] - 80
    lower = []
    for c in range(4):
        hot = hots[:, c * slots : (c + 1) * slots]
        masks = bit_masks(lists[c : c + 1, :] >> 8, below.shape[1] // SPAN)
        lower.append(choose_low(product(table, hot), masks))
    low[...] = jnp.concatenate(lower, axis=0).astype(BF16)
    out[...] = messages[...]
    place, count = lax.axis_index("plane"), out.shape[0]
    for j, offset in enumerate(OFFSETS):
        at = slice(j * slot, (j + 1) * slot)
        target = place + offset

        @pl.when((target >= 0) & (target < count))
        def _():
            out[turned(target, count), split : split + 16, :] = low[:, at]


def plane_modes(a0, a1, a2, a3):
    s01, d01, s23, d23 = a0 + a1, a1 - a0, a2 + a3, a2 - a3
    return s01 + s23, d01 + d23, s23 - s01, d23 - d01


def terms(upper, bottom, stretch, shear, thickness):
    layers, n = thickness.shape
    last = lax.broadcasted_iota(jnp.int32, (layers, n), 0) == layers - 1
    plus, minus, depth = [], [], []
    ends = plane_modes(*bottom)
    for comp in range(4):
        top = plane_modes(*[upper[c][comp] for c in range(4)])
        end = [mode[comp : comp + 1] for mode in ends]
        under = [
            jnp.where(last, jnp.broadcast_to(e, t.shape), pltpu.roll(t, layers - 1, 0))
            for t, e in zip(top, end)
        ]
        depth_parts = [top[0] - under[0]]
        plus_parts, minus_parts = [], []
        for t, u in zip(top[1:], under[1:]):
            total, half = t + u, GAUSS * (t - u)
            plus_parts.append(total + half)
            minus_parts.append(total - half)
            depth_parts.append(half)
        plus.append(plus_parts)
        minus.append(minus_parts)
        depth.append(depth_parts)
        yield
    s0, s1 = stretch[0:1] * (1.0 / 16.0), stretch[1:2] * (1.0 / 16.0)
    h0, h1 = shear[0:1] * (1.0 / 16.0), shear[1:2] * (1.0 / 16.0)
    gs0, gs1, gh0, gh1 = s0 * GAUSS, s1 * GAUSS, h0 * GAUSS, h1 * GAUSS

    def plane_fields(part, first):
        (xa, ya, wa), (xb, yb, wb) = part[first], part[first + 1]
        p1, p2 = s0 * xa + h0 * ya, h1 * xb + s1 * yb
        x1, x2 = gh0 * wa, gs1 * wb
        y1, y2 = gs0 * wa, gh1 * wb
        return (
            (p1 + p2, x1 + x2, y1 + y2),
            (p1 - p2, x1 - x2, y1 - y2),
            (
                (h1 * xa + s1 * ya) + (s0 * xb + h0 * yb),
                gs1 * wa + gh0 * wb,
                gh1 * wa + gs0 * wb,
            ),
        )

    def four(field):
        base, along_x, along_y = field
        up, um = base + along_x, base - along_x
        return up + along_y, up - along_y, um + along_y, um - along_y

    inverse = 0.125 / thickness
    inverse_g = inverse * GAUSS

    def depth_four(parts):
        q0, qx, qy, qw = (
            parts[0] * inverse,
            parts[1] * inverse,
            parts[2] * inverse,
            parts[3] * inverse_g,
        )
        p, m, r, t = q0 + qx, q0 - qx, qy + qw, qy - qw
        return p + r, p - r, m + t, m - t

    za, zb, zc, zd = [depth_four(depth[comp]) for comp in range(4)]
    shear_ff = [za[k] * za[k] + zb[k] * zb[k] + STRAIN_EPS for k in range(4)]
    shear_fa = [za[k] * zc[k] + zb[k] * zd[k] for k in range(4)]
    yield
    total = None
    for part in (plus, minus):
        flow = [four(f) for f in plane_fields(part, 0)]
        other = [four(f) for f in plane_fields(part, 2)]
        for k in range(4):
            s, d, x = flow[0][k], flow[1][k], flow[2][k]
            triple = 3.0 * s
            effective = (triple * s + d * d) + (x * x + shear_ff[k])
            paired = (triple * other[0][k] + d * other[1][k]) + (x * other[2][k] + shear_fa[k])
            value = jnp.exp2(jnp.log2(effective) * (-1.0 / 3.0)) * paired
            total = value if total is None else total + value
            yield
    return total


def group_maps(params):
    layers = (params.shape[0] - 8) // 4
    thickness, rate, retention, weight = [
        params[i * layers : (i + 1) * layers] for i in range(4)
    ]
    stretch, shear = params[4 * layers : 4 * layers + 2], params[4 * layers + 2 : 4 * layers + 4]
    row = lax.broadcasted_iota(jnp.int32, retention.shape, 0)
    factor, offset = retention, (1.0 - retention) * weight
    step = 1
    while step < layers:
        seen = row >= step
        before_f = jnp.where(seen, pltpu.roll(factor, step, 0), 1.0)
        before_o = jnp.where(seen, pltpu.roll(offset, step, 0), 0.0)
        offset = factor * before_o + offset
        factor = factor * before_f
        step *= 2
    det = stretch[0:1] * stretch[1:2] - shear[0:1] * shear[1:2]
    gain = rate * thickness / det
    return stretch, shear, thickness, factor * gain, offset * gain, factor, offset


def column_state(factor, offset, alpha, beta, term):
    return jnp.concatenate(
        [
            factor,
            offset,
            jnp.sum(alpha * term, axis=0, keepdims=True),
            jnp.sum(beta * term, axis=0, keepdims=True),
        ],
        axis=0,
    )


def element_maps(tops, ends, params):
    stretch, shear, thickness, alpha, beta, factor, offset = group_maps(params)
    layers = thickness.shape[0]
    term = yield from terms(tops, ends, stretch, shear, thickness)
    return column_state(factor[layers - 1 :], offset[layers - 1 :], alpha, beta, term)


def physics_kernel(
    fields, below, names, params, early, early_hots, out, first, second, low_first, low_second
):
    rows, owned = fields.shape
    layers = rows // 4
    elems = names.shape[1]
    chunk = first.shape[1]
    count = elems // chunk
    low_table = below_table(below[...])
    table = jnp.concatenate([node_table(fields), low_table], axis=0)
    split = table.shape[0] - low_table.shape[0]
    blocks = owned // SPAN

    def gather(i, held, low):
        for c in range(4):
            wanted = names[c : c + 1, i * chunk : (i + 1) * chunk]
            masks = bit_masks(wanted >> 8, blocks)
            picked = product(table, one_hot(wanted & (SPAN - 1)))
            yield
            for r in range(0, rows, 8):
                at = slice(c * rows + r, c * rows + r + 8)
                held[at, :] = choose_rows(picked[:split], masks, rows, r)
                yield
            low[8 * c : 8 * c + 4, :] = choose_low(picked[split:], masks)

    def work(i, held, low):
        for k in range(chunk // LANES):
            cut = slice(k * LANES, (k + 1) * LANES)
            here = slice(i * chunk + k * LANES, i * chunk + (k + 1) * LANES)
            tops = [
                [
                    held[c * rows + m * layers : c * rows + (m + 1) * layers, cut]
                    for m in range(4)
                ]
                for c in range(4)
            ]
            ends = [low[8 * c : 8 * c + 4, cut] for c in range(4)]
            out[:, here] = yield from element_maps(tops, ends, params[:, here])

    for c in range(4):
        masks = bit_masks(names[c : c + 1, :chunk] >> 8, blocks)
        picked = product(low_table, early_hots[:, c * chunk : (c + 1) * chunk])
        low_first[8 * c : 8 * c + 4, :] = choose_low(picked, masks)
    held = (early, low_first)
    spare = [(second, low_second), (first, low_first)]
    for i in range(count - 1):
        following = spare[i % 2]
        alternate(gather(i + 1, *following), work(i, *held), 3)
        held = following
    drain(work(count - 1, *held))


def border_kernel(state, data, picked, low, messages, out):
    elems = state.shape[1]
    rows = picked.shape[0] // 4
    layers = rows // 4
    slot = messages.shape[2]
    slots = 4 * slot
    place, count = lax.axis_index("plane"), messages.shape[0]
    out[:, :elems] = state[...]
    pieces = []
    for offset in OFFSETS:
        source = jnp.clip(place + offset, 0, count - 1)
        pieces.append(messages[turned(source, count)])
    got = jnp.concatenate(pieces, axis=1).astype(F32)
    mine = picked[...].astype(F32)
    ends = low[...].astype(F32)
    split = 4 * rows + 16
    half = (got.shape[0] - split) // 2
    sides = (
        (got, mine, got[4 * rows : split], ends, data[...]),
        (mine, got, ends, got[4 * rows : split], got[split : split + half] + got[split + half :]),
    )
    for side, (corner0, others, end0, end_others, params) in enumerate(sides):
        for k in range(slots // LANES):
            cut = slice(k * LANES, (k + 1) * LANES)
            tops = [
                [
                    (others if c else corner0)[c * rows + m * layers : c * rows + (m + 1) * layers, cut]
                    for m in range(4)
                ]
                for c in range(4)
            ]
            bots = [(end_others if c else end0)[4 * c : 4 * c + 4, cut] for c in range(4)]
            start = elems + side * slots + k * LANES
            part = params[:, cut]
            alpha, beta, thickness = [part[i * layers : (i + 1) * layers] for i in range(3)]
            rest = part[3 * layers :]
            term = drain(terms(tops, bots, rest[:2], rest[2:4], thickness))
            out[:, start : start + LANES] = column_state(rest[4:5], rest[5:6], alpha, beta, term)


def sum_kernel(first, second, corners, lists, out):
    elems = corners.shape[1]
    slots = lists.shape[1]
    high_count = out.shape[0]
    owned = high_count * LANES
    column = 0.25 * (first[1:2, :] + second[1:2, :] + first[0:1, :] * second[0:1, :])
    main, ghost, near = (
        column[:, :elems],
        column[:, elems : elems + slots],
        column[:, elems + slots :],
    )
    main = jnp.where(corners[0:1, :] < owned, main, 0.0)
    work = [(corners[c : c + 1, :], main) for c in range(4)]
    work += [(lists[c : c + 1, :], ghost if c else near) for c in range(4)]
    total = None
    for at, (names, values) in enumerate(work):
        width = names.shape[1]
        if at >= 4:
            values = jnp.where(names < owned, values, 0.0)
        low, high = names & (LANES - 1), names >> 7
        coarse = values.astype(BF16).astype(F32)
        here = lax.broadcasted_iota(jnp.int32, (high_count, width), 0) == high
        parts = [jnp.where(here, coarse, 0.0), jnp.where(here, values - coarse, 0.0)]
        parts = jnp.concatenate(parts, axis=0).astype(BF16)
        hot = (lax.broadcasted_iota(jnp.int32, (LANES, width), 0) == low).astype(F32).astype(BF16)
        added = lax.dot_general(hot, parts, NT, preferred_element_type=F32)
        total = added if total is None else total + added
    total = total.T
    out[...] = total[:high_count] + total[high_count:]


def compose(one, two):
    return jnp.stack(
        [
            one[0] * two[0],
            two[0] * one[1] + two[1],
            one[2] + one[0] * two[2],
            one[3] + two[3] + one[1] * two[2],
        ]
    )


def shards(
    velocity, adjoint, corners, shared, stretch, shear_part, thickness, rate_factor, retention, weight
):
    layers, owned = velocity.shape[1:]
    elems = corners.shape[1]
    slot = shared.shape[1]
    slots = 4 * slot
    rows = 4 * layers
    shape = jax.ShapeDtypeStruct
    parts = lax.axis_size("plane")
    fields, top, params, names, sends = kernel_call(
        fetch_kernel,
        (
            shape((rows, owned), BF16),
            shape((4, owned), BF16),
            shape((rows + 8, elems), F32),
            shape(corners.shape, jnp.int32),
            shape((1, slots), jnp.int32),
        ),
        10**6,
        velocity, adjoint, corners, shared, thickness, rate_factor, retention, weight, stretch, shear_part,
        spaces="far",
        scratch=(
            pltpu.VMEM(velocity.shape, BF16),
            pltpu.VMEM(adjoint.shape, BF16),
            pltpu.VMEM(stretch.shape, F32),
            pltpu.VMEM(shear_part.shape, F32),
            pltpu.VMEM(shared.shape, jnp.int32),
            pltpu.SemaphoreType.DMA((10,)),
        ),
    )
    below = shifted(top, "layer", -1)
    chunk = min(1024, elems)
    data, lists, picked, hots, messages, early, early_hots = kernel_call(
        element_kernel,
        (
            shape((rows, slots), F32),
            shape((4, slots), jnp.int32),
            shape((4 * rows, slots), BF16),
            shape((SPAN, 4 * slots), BF16),
            shape((parts, 6 * rows + 16, slot), BF16),
            shape((4 * rows, chunk), F32),
            shape((SPAN, 4 * chunk), BF16),
        ),
        2 * 10**9,
        params, names, sends, fields,
    )
    low, messages = kernel_call(
        message_kernel,
        (shape((16, slots), BF16), shape(messages.shape, BF16)),
        10**9,
        below, lists, hots, messages,
    )
    order = [turned(i, parts) for i in range(parts)]
    incoming = lax.all_to_all(messages, "plane", 0, 0, axis_index_groups=[order])
    state = kernel_call(
        physics_kernel,
        shape((4, elems), F32),
        10**10,
        fields, below, names, params, early, early_hots,
        scratch=(pltpu.VMEM((4 * rows, chunk), F32),) * 2 + (pltpu.VMEM((32, chunk), F32),) * 2,
    )
    state = kernel_call(
        border_kernel,
        shape((4, elems + 2 * slots), F32),
        10**9,
        state, data, picked, low, incoming,
    )
    groups, place = lax.axis_size("layer"), lax.axis_index("layer")
    step = 1
    while 2 * step < groups:
        other = lax.ppermute(state, "layer", [(i, i ^ step) for i in range(groups)])
        second = (place & step) != 0
        state = compose(jnp.where(second, other, state), jnp.where(second, state, other))
        step *= 2
    mine = jnp.stack([jnp.where((place & step) != 0, state[2], state[1]), state[3]])
    other = jnp.zeros_like(mine)
    if groups > 1:
        other = lax.ppermute(mine, "layer", [(i, i ^ step) for i in range(groups)])
    gradient = kernel_call(
        sum_kernel,
        shape((owned // LANES, LANES), F32),
        2 * 10**9,
        mine, other, names, lists,
    )
    return gradient.reshape(owned)


def solution(mesh):
    return jax.shard_map(
        shards,
        mesh=mesh,
        in_specs=(
            P(None, "layer", "plane"),
            P(None, "layer", "plane"),
            P(None, "plane"),
            P(None, "plane"),
            P(None, "plane"),
            P(None, "plane"),
            P("layer", "plane"),
            P("layer", "plane"),
            P("layer", "plane"),
            P("layer", "plane"),
        ),
        out_specs=P("plane"),
        check_vma=False,
    )
```

```python
import math

import jax
import jax.numpy as jnp
from jax import lax
from jax.experimental import pallas as pl
from jax.experimental.pallas import tpu as pltpu
from jax.sharding import PartitionSpec as P

OFFSETS = (-2, -1, 1, 2)
STRAIN_EPS = 0.01
GAUSS = 1.0 / math.sqrt(3.0)
SPAN = 256
LANES = 128
TURN = 5
F32, BF16 = jnp.float32, jnp.bfloat16
NT = (((1,), (1,)), ((), ()))


def shifted(value, axis, steps):
    count = lax.axis_size(axis)
    first, last = (max(0, -steps), min(count, count - steps))
    return lax.ppermute(value, axis, [(source, source + steps) for source in range(first, last)])


def kernel_call(body, out_shape, flops, *args, spaces=None, scratch=()):
    vmem = pl.BlockSpec(memory_space=pltpu.VMEM)
    far = pl.BlockSpec(memory_space=pltpu.HBM)
    if spaces == "far":
        args = [pltpu.with_memory_space_constraint(value, pltpu.HBM) for value in args]
    return pl.pallas_call(
        body,
        out_shape=out_shape,
        in_specs=[far if spaces == "far" else vmem for _ in args],
        out_specs=jax.tree.map(lambda _: vmem, out_shape),
        scratch_shapes=list(scratch),
        compiler_params=pltpu.CompilerParams(vmem_limit_bytes=24 * 2**20),
        cost_estimate=pl.CostEstimate(flops=flops, bytes_accessed=2**20, transcendentals=0),
    )(*args)


def node_table(fields):
    blocks = fields.shape[1] // SPAN
    return jnp.concatenate([fields[:, h * SPAN : (h + 1) * SPAN] for h in range(blocks)], axis=0)


def below_table(below):
    wide = below.astype(F32)
    blocks = wide.shape[1] // SPAN
    return jnp.concatenate(
        [wide[:, h * SPAN : (h + 1) * SPAN] for h in range(blocks)], axis=0
    ).astype(BF16)


def one_hot(low):
    shape = (SPAN, low.shape[1])
    rows = lax.broadcasted_iota(jnp.int32, shape, 0).astype(F32).astype(BF16)
    wanted = jnp.broadcast_to(low.astype(F32).astype(BF16), shape)
    return jnp.where(rows == wanted, jnp.ones(shape, BF16), jnp.zeros(shape, BF16))


def bit_masks(high, blocks):
    wide = jnp.broadcast_to(high, (8, high.shape[1]))
    return [(wide & (1 << k)) != 0 for k in range(blocks.bit_length() - 1)]


def choose(parts, masks):
    for mask in masks:
        parts = [jnp.where(mask, parts[i + 1], parts[i]) for i in range(0, len(parts), 2)]
    return parts[0]


def choose_rows(picked, masks, rows, r):
    return choose([picked[h + r : h + r + 8] for h in range(0, picked.shape[0], rows)], masks)


def choose_low(picked, masks):
    pair = choose([picked[h : h + 8] for h in range(0, picked.shape[0], 8)], masks[1:])
    return jnp.where(masks[0][:4], pair[4:], pair[:4])


def product(table, hot):
    return jnp.dot(table, hot, preferred_element_type=F32)


def alternate(first, second, ratio):
    pieces = [(first, 1), (second, ratio)]
    while pieces:
        left = []
        for piece, turns in pieces:
            for _ in range(turns):
                if next(piece, piece) is piece:
                    break
            else:
                left.append((piece, turns))
        pieces = left


def drain(piece):
    while True:
        try:
            next(piece)
        except StopIteration as end:
            return end.value


def fetch_kernel(
    velocity, adjoint, corners, shared, thickness, rate, retention, weight, stretch, shear,
    fields, top, params, names, sends,
    first, second, stretch_here, shear_here, shared_here, semaphores,
):
    layers, elems = thickness.shape
    pairs = [(velocity, first), (adjoint, second), (corners, names), (shared, shared_here)]
    pairs += [(stretch, stretch_here), (shear, shear_here)]
    for i, ref in enumerate((thickness, rate, retention, weight)):
        pairs.append((ref, params.at[pl.ds(i * layers, layers)]))
    copies = [
        pltpu.make_async_copy(source, target, semaphores.at[i])
        for i, (source, target) in enumerate(pairs)
    ]
    for copy in copies:
        copy.start()
    for copy in copies[:2]:
        copy.wait()
    parts = [first[0], first[1], second[0], second[1]]
    fields[...] = jnp.concatenate(parts, axis=0)
    wide = [part.astype(F32)[0:1] for part in parts]
    top[...] = jnp.concatenate(wide, axis=0).astype(BF16)
    for copy in copies[2:]:
        copy.wait()
    params[4 * layers :, :] = jnp.concatenate(
        [stretch_here[...], shear_here[...], jnp.zeros((4, elems), F32)], axis=0
    )
    sends[...] = jnp.concatenate([shared_here[j : j + 1, :] for j in range(4)], axis=1)


def turned(index, count):
    return index ^ TURN if count % 8 == 0 else index


def element_kernel(
    params, names, sends, fields, data, lists, picked, hots, messages, early
):
    rows, owned = fields.shape
    layers = rows // 4
    elems = names.shape[1]
    slots = data.shape[1]
    slot = messages.shape[2]
    held = params.shape[0]
    here = names[...]
    values = params[...]
    coarse = values.astype(BF16).astype(F32)
    left = jnp.concatenate(
        [
            coarse,
            values - coarse,
            (here & (SPAN - 1)).astype(F32),
            (here >> 8).astype(F32),
            jnp.ones((8, elems), F32),
        ],
        axis=0,
    ).astype(BF16)
    wanted = lax.broadcasted_iota(jnp.int32, (slots, elems), 0) + owned
    mine = (wanted == here[0:1]).astype(F32).astype(BF16)
    total = lax.dot_general(left, mine, NT, preferred_element_type=F32)
    ids = (total[2 * held : 2 * held + 4] + total[2 * held + 4 : 2 * held + 8] * SPAN).astype(jnp.int32)
    ids = jnp.where(total[2 * held + 8 : 2 * held + 9] > 0.5, ids, owned)
    lists[...] = jnp.concatenate([sends[...], ids[1:4]], axis=0)
    stretch, shear, thickness, alpha, beta, factor, offset = group_maps(
        total[:held] + total[held : 2 * held]
    )
    data[...] = jnp.concatenate(
        [
            alpha, beta, thickness, stretch, shear,
            factor[layers - 1 :], offset[layers - 1 :], jnp.zeros((2, slots), F32),
        ],
        axis=0,
    )
    table = node_table(fields)
    for c in range(4):
        wanted = lists[c : c + 1, :]
        hot = one_hot(wanted & (SPAN - 1))
        hots[:, c * slots : (c + 1) * slots] = hot
        got = product(table, hot)
        masks = bit_masks(wanted >> 8, owned // SPAN)
        for r in range(0, rows, 8):
            at = slice(c * rows + r, c * rows + r + 8)
            picked[at, :] = choose_rows(got, masks, rows, r).astype(BF16)
    chunk = early.shape[1]
    for c in range(4):
        wanted = names[c : c + 1, :chunk]
        hot = one_hot(wanted & (SPAN - 1))
        got = product(table, hot)
        masks = bit_masks(wanted >> 8, owned // SPAN)
        for r in range(0, rows, 8):
            early[c * rows + r : c * rows + r + 8, :] = choose_rows(got, masks, rows, r)
    place, count = lax.axis_index("plane"), messages.shape[0]
    coarse = data[...].astype(BF16)
    fine = (data[...] - coarse.astype(F32)).astype(BF16)
    for j, offset in enumerate(OFFSETS):
        at = slice(j * slot, (j + 1) * slot)
        target = place + offset

        @pl.when((target >= 0) & (target < count))
        def _():
            block = turned(target, count)
            messages[block, : 4 * rows, :] = picked[:, at]
            messages[block, 4 * rows + 16 :, :] = jnp.concatenate([coarse[:, at], fine[:, at]], axis=0)


def message_kernel(below, lists, hots, messages, low, out):
    table = below_table(below[...])
    slots = lists.shape[1]
    slot = out.shape[2]
    split = out.shape[1] - 80
    lower = []
    for c in range(4):
        hot = hots[:, c * slots : (c + 1) * slots]
        masks = bit_masks(lists[c : c + 1, :] >> 8, below.shape[1] // SPAN)
        lower.append(choose_low(product(table, hot), masks))
    low[...] = jnp.concatenate(lower, axis=0).astype(BF16)
    out[...] = messages[...]
    place, count = lax.axis_index("plane"), out.shape[0]
    for j, offset in enumerate(OFFSETS):
        at = slice(j * slot, (j + 1) * slot)
        target = place + offset

        @pl.when((target >= 0) & (target < count))
        def _():
            out[turned(target, count), split : split + 16, :] = low[:, at]


def plane_modes(a0, a1, a2, a3):
    s01, d01, s23, d23 = a0 + a1, a1 - a0, a2 + a3, a2 - a3
    return s01 + s23, d01 + d23, s23 - s01, d23 - d01


def terms(upper, bottom, stretch, shear, thickness):
    layers, n = thickness.shape
    last = lax.broadcasted_iota(jnp.int32, (layers, n), 0) == layers - 1
    plus, minus, depth = [], [], []
    ends = plane_modes(*bottom)
    for comp in range(4):
        top = plane_modes(*[upper[c][comp] for c in range(4)])
        end = [mode[comp : comp + 1] for mode in ends]
        under = [
            jnp.where(last, jnp.broadcast_to(e, t.shape), pltpu.roll(t, layers - 1, 0))
            for t, e in zip(top, end)
        ]
        depth_parts = [top[0] - under[0]]
        plus_parts, minus_parts = [], []
        for t, u in zip(top[1:], under[1:]):
            total, half = t + u, GAUSS * (t - u)
            plus_parts.append(total + half)
            minus_parts.append(total - half)
            depth_parts.append(half)
        plus.append(plus_parts)
        minus.append(minus_parts)
        depth.append(depth_parts)
        yield
    s0, s1 = stretch[0:1] * (1.0 / 16.0), stretch[1:2] * (1.0 / 16.0)
    h0, h1 = shear[0:1] * (1.0 / 16.0), shear[1:2] * (1.0 / 16.0)
    gs0, gs1, gh0, gh1 = s0 * GAUSS, s1 * GAUSS, h0 * GAUSS, h1 * GAUSS

    def plane_fields(part, first):
        (xa, ya, wa), (xb, yb, wb) = part[first], part[first + 1]
        p1, p2 = s0 * xa + h0 * ya, h1 * xb + s1 * yb
        x1, x2 = gh0 * wa, gs1 * wb
        y1, y2 = gs0 * wa, gh1 * wb
        return (
            (p1 + p2, x1 + x2, y1 + y2),
            (p1 - p2, x1 - x2, y1 - y2),
            (
                (h1 * xa + s1 * ya) + (s0 * xb + h0 * yb),
                gs1 * wa + gh0 * wb,
                gh1 * wa + gs0 * wb,
            ),
        )

    def four(field):
        base, along_x, along_y = field
        up, um = base + along_x, base - along_x
        return up + along_y, up - along_y, um + along_y, um - along_y

    inverse = 0.125 / thickness
    inverse_g = inverse * GAUSS

    def depth_four(parts):
        q0, qx, qy, qw = (
            parts[0] * inverse,
            parts[1] * inverse,
            parts[2] * inverse,
            parts[3] * inverse_g,
        )
        p, m, r, t = q0 + qx, q0 - qx, qy + qw, qy - qw
        return p + r, p - r, m + t, m - t

    za, zb, zc, zd = [depth_four(depth[comp]) for comp in range(4)]
    shear_ff = [za[k] * za[k] + zb[k] * zb[k] + STRAIN_EPS for k in range(4)]
    shear_fa = [za[k] * zc[k] + zb[k] * zd[k] for k in range(4)]
    yield
    total = None
    for part in (plus, minus):
        flow = [four(f) for f in plane_fields(part, 0)]
        other = [four(f) for f in plane_fields(part, 2)]
        for k in range(4):
            s, d, x = flow[0][k], flow[1][k], flow[2][k]
            triple = 3.0 * s
            effective = (triple * s + d * d) + (x * x + shear_ff[k])
            paired = (triple * other[0][k] + d * other[1][k]) + (x * other[2][k] + shear_fa[k])
            value = jnp.exp2(jnp.log2(effective) * (-1.0 / 3.0)) * paired
            total = value if total is None else total + value
            yield
    return total


def group_maps(params):
    layers = (params.shape[0] - 8) // 4
    thickness, rate, retention, weight = [
        params[i * layers : (i + 1) * layers] for i in range(4)
    ]
    stretch, shear = params[4 * layers : 4 * layers + 2], params[4 * layers + 2 : 4 * layers + 4]
    row = lax.broadcasted_iota(jnp.int32, retention.shape, 0)
    factor, offset = retention, (1.0 - retention) * weight
    step = 1
    while step < layers:
        seen = row >= step
        before_f = jnp.where(seen, pltpu.roll(factor, step, 0), 1.0)
        before_o = jnp.where(seen, pltpu.roll(offset, step, 0), 0.0)
        offset = factor * before_o + offset
        factor = factor * before_f
        step *= 2
    det = stretch[0:1] * stretch[1:2] - shear[0:1] * shear[1:2]
    gain = rate * thickness / det
    return stretch, shear, thickness, factor * gain, offset * gain, factor, offset


def column_state(factor, offset, alpha, beta, term):
    return jnp.concatenate(
        [
            factor,
            offset,
            jnp.sum(alpha * term, axis=0, keepdims=True),
            jnp.sum(beta * term, axis=0, keepdims=True),
        ],
        axis=0,
    )


def element_maps(tops, ends, params):
    stretch, shear, thickness, alpha, beta, factor, offset = group_maps(params)
    layers = thickness.shape[0]
    term = yield from terms(tops, ends, stretch, shear, thickness)
    return column_state(factor[layers - 1 :], offset[layers - 1 :], alpha, beta, term)


def physics_kernel(
    fields, below, names, params, early, out, first, second, low_first, low_second
):
    rows, owned = fields.shape
    layers = rows // 4
    elems = names.shape[1]
    chunk = first.shape[1]
    count = elems // chunk
    low_table = below_table(below[...])
    table = jnp.concatenate([node_table(fields), low_table], axis=0)
    split = table.shape[0] - low_table.shape[0]
    blocks = owned // SPAN

    def gather(i, held, low):
        for c in range(4):
            wanted = names[c : c + 1, i * chunk : (i + 1) * chunk]
            masks = bit_masks(wanted >> 8, blocks)
            picked = product(table, one_hot(wanted & (SPAN - 1)))
            yield
            for r in range(0, rows, 8):
                at = slice(c * rows + r, c * rows + r + 8)
                held[at, :] = choose_rows(picked[:split], masks, rows, r)
                yield
            low[8 * c : 8 * c + 4, :] = choose_low(picked[split:], masks)

    def work(i, held, low):
        for k in range(chunk // LANES):
            cut = slice(k * LANES, (k + 1) * LANES)
            here = slice(i * chunk + k * LANES, i * chunk + (k + 1) * LANES)
            tops = [
                [
                    held[c * rows + m * layers : c * rows + (m + 1) * layers, cut]
                    for m in range(4)
                ]
                for c in range(4)
            ]
            ends = [low[8 * c : 8 * c + 4, cut] for c in range(4)]
            out[:, here] = yield from element_maps(tops, ends, params[:, here])

    for c in range(4):
        wanted = names[c : c + 1, :chunk]
        masks = bit_masks(wanted >> 8, blocks)
        picked = product(low_table, one_hot(wanted & (SPAN - 1)))
        low_first[8 * c : 8 * c + 4, :] = choose_low(picked, masks)
    held = (early, low_first)
    spare = [(second, low_second), (first, low_first)]
    for i in range(count - 1):
        following = spare[i % 2]
        alternate(gather(i + 1, *following), work(i, *held), 3)
        held = following
    drain(work(count - 1, *held))


def border_kernel(state, data, picked, low, messages, out):
    elems = state.shape[1]
    rows = picked.shape[0] // 4
    layers = rows // 4
    slot = messages.shape[2]
    slots = 4 * slot
    place, count = lax.axis_index("plane"), messages.shape[0]
    out[:, :elems] = state[...]
    pieces = []
    for offset in OFFSETS:
        source = jnp.clip(place + offset, 0, count - 1)
        pieces.append(messages[turned(source, count)])
    got = jnp.concatenate(pieces, axis=1).astype(F32)
    mine = picked[...].astype(F32)
    ends = low[...].astype(F32)
    split = 4 * rows + 16
    half = (got.shape[0] - split) // 2
    sides = (
        (got, mine, got[4 * rows : split], ends, data[...]),
        (mine, got, ends, got[4 * rows : split], got[split : split + half] + got[split + half :]),
    )
    for side, (corner0, others, end0, end_others, params) in enumerate(sides):
        for k in range(slots // LANES):
            cut = slice(k * LANES, (k + 1) * LANES)
            tops = [
                [
                    (others if c else corner0)[c * rows + m * layers : c * rows + (m + 1) * layers, cut]
                    for m in range(4)
                ]
                for c in range(4)
            ]
            bots = [(end_others if c else end0)[4 * c : 4 * c + 4, cut] for c in range(4)]
            start = elems + side * slots + k * LANES
            part = params[:, cut]
            alpha, beta, thickness = [part[i * layers : (i + 1) * layers] for i in range(3)]
            rest = part[3 * layers :]
            term = drain(terms(tops, bots, rest[:2], rest[2:4], thickness))
            out[:, start : start + LANES] = column_state(rest[4:5], rest[5:6], alpha, beta, term)


def sum_kernel(first, second, corners, lists, out):
    elems = corners.shape[1]
    slots = lists.shape[1]
    high_count = out.shape[0]
    owned = high_count * LANES
    column = 0.25 * (first[1:2, :] + second[1:2, :] + first[0:1, :] * second[0:1, :])
    main, ghost, near = (
        column[:, :elems],
        column[:, elems : elems + slots],
        column[:, elems + slots :],
    )
    main = jnp.where(corners[0:1, :] < owned, main, 0.0)
    work = [(corners[c : c + 1, :], main) for c in range(4)]
    work += [(lists[c : c + 1, :], ghost if c else near) for c in range(4)]
    total = None
    for at, (names, values) in enumerate(work):
        width = names.shape[1]
        if at >= 4:
            values = jnp.where(names < owned, values, 0.0)
        low, high = names & (LANES - 1), names >> 7
        coarse = values.astype(BF16).astype(F32)
        here = lax.broadcasted_iota(jnp.int32, (high_count, width), 0) == high
        parts = [jnp.where(here, coarse, 0.0), jnp.where(here, values - coarse, 0.0)]
        parts = jnp.concatenate(parts, axis=0).astype(BF16)
        hot = (lax.broadcasted_iota(jnp.int32, (LANES, width), 0) == low).astype(F32).astype(BF16)
        added = lax.dot_general(hot, parts, NT, preferred_element_type=F32)
        total = added if total is None else total + added
    total = total.T
    out[...] = total[:high_count] + total[high_count:]


def compose(one, two):
    return jnp.stack(
        [
            one[0] * two[0],
            two[0] * one[1] + two[1],
            one[2] + one[0] * two[2],
            one[3] + two[3] + one[1] * two[2],
        ]
    )


def shards(
    velocity, adjoint, corners, shared, stretch, shear_part, thickness, rate_factor, retention, weight
):
    layers, owned = velocity.shape[1:]
    elems = corners.shape[1]
    slot = shared.shape[1]
    slots = 4 * slot
    rows = 4 * layers
    shape = jax.ShapeDtypeStruct
    parts = lax.axis_size("plane")
    fields, top, params, names, sends = kernel_call(
        fetch_kernel,
        (
            shape((rows, owned), BF16),
            shape((4, owned), BF16),
            shape((rows + 8, elems), F32),
            shape(corners.shape, jnp.int32),
            shape((1, slots), jnp.int32),
        ),
        10**6,
        velocity, adjoint, corners, shared, thickness, rate_factor, retention, weight, stretch, shear_part,
        spaces="far",
        scratch=(
            pltpu.VMEM(velocity.shape, BF16),
            pltpu.VMEM(adjoint.shape, BF16),
            pltpu.VMEM(stretch.shape, F32),
            pltpu.VMEM(shear_part.shape, F32),
            pltpu.VMEM(shared.shape, jnp.int32),
            pltpu.SemaphoreType.DMA((10,)),
        ),
    )
    below = shifted(top, "layer", -1)
    chunk = min(1024, elems)
    data, lists, picked, hots, messages, early = kernel_call(
        element_kernel,
        (
            shape((rows, slots), F32),
            shape((4, slots), jnp.int32),
            shape((4 * rows, slots), BF16),
            shape((SPAN, 4 * slots), BF16),
            shape((parts, 6 * rows + 16, slot), BF16),
            shape((4 * rows, chunk), F32),
        ),
        2 * 10**9,
        params, names, sends, fields,
    )
    low, messages = kernel_call(
        message_kernel,
        (shape((16, slots), BF16), shape(messages.shape, BF16)),
        10**9,
        below, lists, hots, messages,
    )
    order = [turned(i, parts) for i in range(parts)]
    incoming = lax.all_to_all(messages, "plane", 0, 0, axis_index_groups=[order])
    state = kernel_call(
        physics_kernel,
        shape((4, elems), F32),
        10**10,
        fields, below, names, params, early,
        scratch=(pltpu.VMEM((4 * rows, chunk), F32),) * 2 + (pltpu.VMEM((32, chunk), F32),) * 2,
    )
    state = kernel_call(
        border_kernel,
        shape((4, elems + 2 * slots), F32),
        10**9,
        state, data, picked, low, incoming,
    )
    groups, place = lax.axis_size("layer"), lax.axis_index("layer")
    step = 1
    while 2 * step < groups:
        other = lax.ppermute(state, "layer", [(i, i ^ step) for i in range(groups)])
        second = (place & step) != 0
        state = compose(jnp.where(second, other, state), jnp.where(second, state, other))
        step *= 2
    mine = jnp.stack([jnp.where((place & step) != 0, state[2], state[1]), state[3]])
    other = jnp.zeros_like(mine)
    if groups > 1:
        other = lax.ppermute(mine, "layer", [(i, i ^ step) for i in range(groups)])
    gradient = kernel_call(
        sum_kernel,
        shape((owned // LANES, LANES), F32),
        2 * 10**9,
        mine, other, names, lists,
    )
    return gradient.reshape(owned)


def solution(mesh):
    return jax.shard_map(
        shards,
        mesh=mesh,
        in_specs=(
            P(None, "layer", "plane"),
            P(None, "layer", "plane"),
            P(None, "plane"),
            P(None, "plane"),
            P(None, "plane"),
            P(None, "plane"),
            P("layer", "plane"),
            P("layer", "plane"),
            P("layer", "plane"),
            P("layer", "plane"),
        ),
        out_specs=P("plane"),
        check_vma=False,
    )
```

```python
import math

import jax
import jax.numpy as jnp
from jax import lax
from jax.experimental import pallas as pl
from jax.experimental.pallas import tpu as pltpu
from jax.sharding import PartitionSpec as P

OFFSETS = (-2, -1, 1, 2)
STRAIN_EPS = 0.01
GAUSS = 1.0 / math.sqrt(3.0)
SPAN = 256
LANES = 128
TURN = 1
F32, BF16 = jnp.float32, jnp.bfloat16
NT = (((1,), (1,)), ((), ()))


def shifted(value, axis, steps):
    count = lax.axis_size(axis)
    first, last = (max(0, -steps), min(count, count - steps))
    return lax.ppermute(value, axis, [(source, source + steps) for source in range(first, last)])


def kernel_call(body, out_shape, flops, *args, spaces=None, scratch=(), free=()):
    vmem = pl.BlockSpec(memory_space=pltpu.VMEM)
    far = pl.BlockSpec(memory_space=pltpu.HBM)
    if spaces == "far":
        args = [pltpu.with_memory_space_constraint(value, pltpu.HBM) for value in args]
    return pl.pallas_call(
        body,
        out_shape=out_shape,
        in_specs=[far if spaces == "far" else vmem for _ in args],
        out_specs=[
            pl.BlockSpec(memory_space=pl.ANY) if i in free else vmem for i in range(len(out_shape))
        ]
        if isinstance(out_shape, tuple)
        else vmem,
        scratch_shapes=list(scratch),
        compiler_params=pltpu.CompilerParams(vmem_limit_bytes=24 * 2**20),
        cost_estimate=pl.CostEstimate(flops=flops, bytes_accessed=2**20, transcendentals=0),
    )(*args)


def node_table(fields):
    blocks = fields.shape[1] // SPAN
    return jnp.concatenate([fields[:, h * SPAN : (h + 1) * SPAN] for h in range(blocks)], axis=0)


def level_table(level):
    blocks = level.shape[1] // SPAN
    return jnp.concatenate([level[:, h * SPAN : (h + 1) * SPAN] for h in range(blocks)], axis=0)


def one_hot(low):
    shape = (SPAN, low.shape[1])
    rows = lax.broadcasted_iota(jnp.int32, shape, 0).astype(F32).astype(BF16)
    wanted = jnp.broadcast_to(low.astype(F32).astype(BF16), shape)
    return jnp.where(rows == wanted, jnp.ones(shape, BF16), jnp.zeros(shape, BF16))


def bit_masks(high, blocks):
    wide = jnp.broadcast_to(high, (8, high.shape[1]))
    return [(wide & (1 << k)) != 0 for k in range(blocks.bit_length() - 1)]


def choose(parts, masks):
    for mask in masks:
        parts = [jnp.where(mask, parts[i + 1], parts[i]) for i in range(0, len(parts), 2)]
    return parts[0]


def choose_rows(picked, masks, rows, r):
    return choose([picked[h + r : h + r + 8] for h in range(0, picked.shape[0], rows)], masks)


def choose_low(picked, masks):
    pair = choose([picked[h : h + 8] for h in range(0, picked.shape[0], 8)], masks[1:])
    return jnp.where(masks[0][:4], pair[4:], pair[:4])


def product(table, hot):
    return jnp.dot(table, hot, preferred_element_type=F32)


def alternate(first, second, ratio):
    pieces = [(first, 1), (second, ratio)]
    while pieces:
        left = []
        for piece, turns in pieces:
            for _ in range(turns):
                if next(piece, piece) is piece:
                    break
            else:
                left.append((piece, turns))
        pieces = left


def drain(piece):
    while True:
        try:
            next(piece)
        except StopIteration as end:
            return end.value


def fetch_kernel(
    velocity, adjoint, corners, shared, thickness, rate, retention, weight, stretch, shear,
    fields, top, params, names, sends,
    first, second, stretch_here, shear_here, shared_here, semaphores,
):
    layers, elems = thickness.shape
    pairs = [(velocity, first), (adjoint, second), (corners, names), (shared, shared_here)]
    pairs += [(stretch, stretch_here), (shear, shear_here)]
    for i, ref in enumerate((thickness, rate, retention, weight)):
        pairs.append((ref, params.at[pl.ds(i * layers, layers)]))
    copies = [
        pltpu.make_async_copy(source, target, semaphores.at[i])
        for i, (source, target) in enumerate(pairs)
    ]
    for copy in copies:
        copy.start()
    for copy in copies[:2]:
        copy.wait()
    parts = [first[0], first[1], second[0], second[1]]
    fields[...] = jnp.concatenate(parts, axis=0)
    wide = [part.astype(F32)[0:1] for part in parts]
    top[...] = level_table(jnp.concatenate(wide, axis=0)).astype(BF16)
    for copy in copies[2:]:
        copy.wait()
    params[4 * layers :, :] = jnp.concatenate(
        [stretch_here[...], shear_here[...], jnp.zeros((4, elems), F32)], axis=0
    )
    sends[...] = jnp.concatenate([shared_here[j : j + 1, :] for j in range(4)], axis=1)


def turned(index, count):
    return index ^ TURN if count % 8 == 0 else index


def block_of(place, offset, count):
    return turned(lax.rem(place + offset + count, count), count)


def element_kernel(
    params, names, sends, fields, data, lists, joined, picked, hots, coded, early
):
    rows, owned = fields.shape
    layers = rows // 4
    elems = names.shape[1]
    slots = data.shape[1]
    held = params.shape[0]
    here = names[...]
    values = params[...]
    coarse = values.astype(BF16).astype(F32)
    left = jnp.concatenate(
        [
            coarse,
            values - coarse,
            (here & (SPAN - 1)).astype(F32),
            (here >> 8).astype(F32),
            jnp.ones((8, elems), F32),
        ],
        axis=0,
    ).astype(BF16)
    wanted = lax.broadcasted_iota(jnp.int32, (slots, elems), 0) + owned
    mine = (wanted == here[0:1]).astype(F32).astype(BF16)
    total = lax.dot_general(left, mine, NT, preferred_element_type=F32)
    ids = (total[2 * held : 2 * held + 4] + total[2 * held + 4 : 2 * held + 8] * SPAN).astype(jnp.int32)
    ids = jnp.where(total[2 * held + 8 : 2 * held + 9] > 0.5, ids, owned)
    lists[...] = jnp.concatenate([sends[...], ids[1:4]], axis=0)
    joined[...] = jnp.concatenate([sends[...], ids[1:2], ids[2:3], ids[3:4]], axis=1)
    stretch, shear, thickness, alpha, beta, factor, offset = group_maps(
        total[:held] + total[held : 2 * held]
    )
    data[...] = jnp.concatenate(
        [
            alpha, beta, thickness, stretch, shear,
            factor[layers - 1 :], offset[layers - 1 :], jnp.zeros((2, slots), F32),
        ],
        axis=0,
    )
    table = node_table(fields)
    for c in range(4):
        wanted = lists[c : c + 1, :]
        hot = one_hot(wanted & (SPAN - 1))
        hots[:, c * slots : (c + 1) * slots] = hot
        got = product(table, hot)
        masks = bit_masks(wanted >> 8, owned // SPAN)
        for r in range(0, rows, 8):
            at = slice(c * rows + r, c * rows + r + 8)
            picked[at, :] = choose_rows(got, masks, rows, r).astype(BF16)
    chunk = early.shape[1]
    for c in range(4):
        wanted = names[c : c + 1, :chunk]
        hot = one_hot(wanted & (SPAN - 1))
        got = product(table, hot)
        masks = bit_masks(wanted >> 8, owned // SPAN)
        for r in range(0, rows, 8):
            early[c * rows + r : c * rows + r + 8, :] = choose_rows(got, masks, rows, r)
    coarse = data[...].astype(BF16)
    coded[...] = jnp.concatenate([coarse, (data[...] - coarse.astype(F32)).astype(BF16)], axis=0)


def message_kernel(below, joined, hots, picked, coded, low, out, semaphores):
    slots = low.shape[1]
    slot = out.shape[2]
    upper, extra = picked.shape[0], coded.shape[0]
    place, count = lax.axis_index("plane"), out.shape[0]

    def sends(source, row, first):
        copies = []
        for j, offset in enumerate(OFFSETS):
            copies.append(
                pltpu.make_async_copy(
                    source.at[:, pl.ds(j * slot, slot)],
                    out.at[block_of(place, offset, count), pl.ds(row, source.shape[0]), :],
                    semaphores.at[first + j],
                )
            )
        for copy in copies:
            copy.start()
        return copies

    copies = sends(picked, 0, 0) + sends(coded, upper + 16, 4)
    masks = bit_masks(joined[...] >> 8, below.shape[0] // 4)
    values = choose_low(product(below[...], hots[...]), masks)
    lower = [values[:, c * slots : (c + 1) * slots] for c in range(4)]
    low[...] = jnp.concatenate(lower, axis=0).astype(BF16)
    copies += sends(low, upper, 8)
    for copy in copies:
        copy.wait()


def plane_modes(a0, a1, a2, a3):
    s01, d01, s23, d23 = a0 + a1, a1 - a0, a2 + a3, a2 - a3
    return s01 + s23, d01 + d23, s23 - s01, d23 - d01


def terms(upper, bottom, stretch, shear, thickness):
    layers, n = thickness.shape
    last = lax.broadcasted_iota(jnp.int32, (layers, n), 0) == layers - 1
    plus, minus, depth = [], [], []
    ends = plane_modes(*bottom)
    for comp in range(4):
        top = plane_modes(*[upper[c][comp] for c in range(4)])
        end = [mode[comp : comp + 1] for mode in ends]
        under = [
            jnp.where(last, jnp.broadcast_to(e, t.shape), pltpu.roll(t, layers - 1, 0))
            for t, e in zip(top, end)
        ]
        depth_parts = [top[0] - under[0]]
        plus_parts, minus_parts = [], []
        for t, u in zip(top[1:], under[1:]):
            total, half = t + u, GAUSS * (t - u)
            plus_parts.append(total + half)
            minus_parts.append(total - half)
            depth_parts.append(half)
        plus.append(plus_parts)
        minus.append(minus_parts)
        depth.append(depth_parts)
        yield
    s0, s1 = stretch[0:1] * (1.0 / 16.0), stretch[1:2] * (1.0 / 16.0)
    h0, h1 = shear[0:1] * (1.0 / 16.0), shear[1:2] * (1.0 / 16.0)
    gs0, gs1, gh0, gh1 = s0 * GAUSS, s1 * GAUSS, h0 * GAUSS, h1 * GAUSS

    def plane_fields(part, first):
        (xa, ya, wa), (xb, yb, wb) = part[first], part[first + 1]
        p1, p2 = s0 * xa + h0 * ya, h1 * xb + s1 * yb
        x1, x2 = gh0 * wa, gs1 * wb
        y1, y2 = gs0 * wa, gh1 * wb
        return (
            (p1 + p2, x1 + x2, y1 + y2),
            (p1 - p2, x1 - x2, y1 - y2),
            (
                (h1 * xa + s1 * ya) + (s0 * xb + h0 * yb),
                gs1 * wa + gh0 * wb,
                gh1 * wa + gs0 * wb,
            ),
        )

    def four(field):
        base, along_x, along_y = field
        up, um = base + along_x, base - along_x
        return up + along_y, up - along_y, um + along_y, um - along_y

    inverse = 0.125 / thickness
    inverse_g = inverse * GAUSS

    def depth_four(parts):
        q0, qx, qy, qw = (
            parts[0] * inverse,
            parts[1] * inverse,
            parts[2] * inverse,
            parts[3] * inverse_g,
        )
        p, m, r, t = q0 + qx, q0 - qx, qy + qw, qy - qw
        return p + r, p - r, m + t, m - t

    za, zb, zc, zd = [depth_four(depth[comp]) for comp in range(4)]
    shear_ff = [za[k] * za[k] + zb[k] * zb[k] + STRAIN_EPS for k in range(4)]
    shear_fa = [za[k] * zc[k] + zb[k] * zd[k] for k in range(4)]
    yield
    total = None
    for part in (plus, minus):
        flow = [four(f) for f in plane_fields(part, 0)]
        other = [four(f) for f in plane_fields(part, 2)]
        for k in range(4):
            s, d, x = flow[0][k], flow[1][k], flow[2][k]
            triple = 3.0 * s
            effective = (triple * s + d * d) + (x * x + shear_ff[k])
            paired = (triple * other[0][k] + d * other[1][k]) + (x * other[2][k] + shear_fa[k])
            value = jnp.exp2(jnp.log2(effective) * (-1.0 / 3.0)) * paired
            total = value if total is None else total + value
            yield
    return total


def group_maps(params):
    layers = (params.shape[0] - 8) // 4
    thickness, rate, retention, weight = [
        params[i * layers : (i + 1) * layers] for i in range(4)
    ]
    stretch, shear = params[4 * layers : 4 * layers + 2], params[4 * layers + 2 : 4 * layers + 4]
    row = lax.broadcasted_iota(jnp.int32, retention.shape, 0)
    factor, offset = retention, (1.0 - retention) * weight
    step = 1
    while step < layers:
        seen = row >= step
        before_f = jnp.where(seen, pltpu.roll(factor, step, 0), 1.0)
        before_o = jnp.where(seen, pltpu.roll(offset, step, 0), 0.0)
        offset = factor * before_o + offset
        factor = factor * before_f
        step *= 2
    det = stretch[0:1] * stretch[1:2] - shear[0:1] * shear[1:2]
    gain = rate * thickness / det
    return stretch, shear, thickness, factor * gain, offset * gain, factor, offset


def column_state(factor, offset, alpha, beta, term):
    return jnp.concatenate(
        [
            factor,
            offset,
            jnp.sum(alpha * term, axis=0, keepdims=True),
            jnp.sum(beta * term, axis=0, keepdims=True),
        ],
        axis=0,
    )


def element_maps(tops, ends, params):
    stretch, shear, thickness, alpha, beta, factor, offset = group_maps(params)
    layers = thickness.shape[0]
    term = yield from terms(tops, ends, stretch, shear, thickness)
    return column_state(factor[layers - 1 :], offset[layers - 1 :], alpha, beta, term)


def physics_kernel(
    fields, below, names, params, early, out, first, second, low_first, low_second
):
    rows, owned = fields.shape
    layers = rows // 4
    elems = names.shape[1]
    chunk = first.shape[1]
    count = elems // chunk
    low_table = below[...]
    table = jnp.concatenate([node_table(fields), low_table], axis=0)
    split = table.shape[0] - low_table.shape[0]
    blocks = owned // SPAN

    def gather(i, held, low):
        for c in range(4):
            wanted = names[c : c + 1, i * chunk : (i + 1) * chunk]
            masks = bit_masks(wanted >> 8, blocks)
            picked = product(table, one_hot(wanted & (SPAN - 1)))
            yield
            for r in range(0, rows, 8):
                at = slice(c * rows + r, c * rows + r + 8)
                held[at, :] = choose_rows(picked[:split], masks, rows, r)
                yield
            low[8 * c : 8 * c + 4, :] = choose_low(picked[split:], masks)

    def work(i, held, low):
        for k in range(chunk // LANES):
            cut = slice(k * LANES, (k + 1) * LANES)
            here = slice(i * chunk + k * LANES, i * chunk + (k + 1) * LANES)
            tops = [
                [
                    held[c * rows + m * layers : c * rows + (m + 1) * layers, cut]
                    for m in range(4)
                ]
                for c in range(4)
            ]
            ends = [low[8 * c : 8 * c + 4, cut] for c in range(4)]
            out[:, here] = yield from element_maps(tops, ends, params[:, here])

    for c in range(4):
        wanted = names[c : c + 1, :chunk]
        masks = bit_masks(wanted >> 8, blocks)
        picked = product(low_table, one_hot(wanted & (SPAN - 1)))
        low_first[8 * c : 8 * c + 4, :] = choose_low(picked, masks)
    held = (early, low_first)
    spare = [(second, low_second), (first, low_first)]
    for i in range(count - 1):
        following = spare[i % 2]
        alternate(gather(i + 1, *following), work(i, *held), 3)
        held = following
    drain(work(count - 1, *held))


def border_kernel(state, data, picked, low, messages, out):
    elems = state.shape[1]
    rows = picked.shape[0] // 4
    layers = rows // 4
    slot = messages.shape[2]
    slots = 4 * slot
    place, count = lax.axis_index("plane"), messages.shape[0]
    out[:, :elems] = state[...]
    pieces = []
    for offset in OFFSETS:
        source = jnp.clip(place + offset, 0, count - 1)
        pieces.append(messages[turned(source, count)])
    got = jnp.concatenate(pieces, axis=1).astype(F32)
    mine = picked[...].astype(F32)
    ends = low[...].astype(F32)
    split = 4 * rows + 16
    half = (got.shape[0] - split) // 2
    sides = (
        (got, mine, got[4 * rows : split], ends, data[...]),
        (mine, got, ends, got[4 * rows : split], got[split : split + half] + got[split + half :]),
    )
    for side, (corner0, others, end0, end_others, params) in enumerate(sides):
        for k in range(slots // LANES):
            cut = slice(k * LANES, (k + 1) * LANES)
            tops = [
                [
                    (others if c else corner0)[c * rows + m * layers : c * rows + (m + 1) * layers, cut]
                    for m in range(4)
                ]
                for c in range(4)
            ]
            bots = [(end_others if c else end0)[4 * c : 4 * c + 4, cut] for c in range(4)]
            start = elems + side * slots + k * LANES
            part = params[:, cut]
            alpha, beta, thickness = [part[i * layers : (i + 1) * layers] for i in range(3)]
            rest = part[3 * layers :]
            term = drain(terms(tops, bots, rest[:2], rest[2:4], thickness))
            out[:, start : start + LANES] = column_state(rest[4:5], rest[5:6], alpha, beta, term)


def sum_kernel(first, second, corners, lists, out):
    elems = corners.shape[1]
    slots = lists.shape[1]
    high_count = out.shape[0]
    owned = high_count * LANES
    column = 0.25 * (first[1:2, :] + second[1:2, :] + first[0:1, :] * second[0:1, :])
    main, ghost, near = (
        column[:, :elems],
        column[:, elems : elems + slots],
        column[:, elems + slots :],
    )
    main = jnp.where(corners[0:1, :] < owned, main, 0.0)
    work = [(corners[c : c + 1, :], main) for c in range(4)]
    work += [(lists[c : c + 1, :], ghost if c else near) for c in range(4)]
    total = None
    for at, (names, values) in enumerate(work):
        width = names.shape[1]
        if at >= 4:
            values = jnp.where(names < owned, values, 0.0)
        low, high = names & (LANES - 1), names >> 7
        coarse = values.astype(BF16).astype(F32)
        here = lax.broadcasted_iota(jnp.int32, (high_count, width), 0) == high
        parts = [jnp.where(here, coarse, 0.0), jnp.where(here, values - coarse, 0.0)]
        parts = jnp.concatenate(parts, axis=0).astype(BF16)
        hot = (lax.broadcasted_iota(jnp.int32, (LANES, width), 0) == low).astype(F32).astype(BF16)
        added = lax.dot_general(hot, parts, NT, preferred_element_type=F32)
        total = added if total is None else total + added
    total = total.T
    out[...] = total[:high_count] + total[high_count:]


def compose(one, two):
    return jnp.stack(
        [
            one[0] * two[0],
            two[0] * one[1] + two[1],
            one[2] + one[0] * two[2],
            one[3] + two[3] + one[1] * two[2],
        ]
    )


def shards(
    velocity, adjoint, corners, shared, stretch, shear_part, thickness, rate_factor, retention, weight
):
    layers, owned = velocity.shape[1:]
    elems = corners.shape[1]
    slot = shared.shape[1]
    slots = 4 * slot
    rows = 4 * layers
    shape = jax.ShapeDtypeStruct
    parts = lax.axis_size("plane")
    fields, top, params, names, sends = kernel_call(
        fetch_kernel,
        (
            shape((rows, owned), BF16),
            shape((4 * owned // SPAN, SPAN), BF16),
            shape((rows + 8, elems), F32),
            shape(corners.shape, jnp.int32),
            shape((1, slots), jnp.int32),
        ),
        10**6,
        velocity, adjoint, corners, shared, thickness, rate_factor, retention, weight, stretch, shear_part,
        spaces="far",
        scratch=(
            pltpu.VMEM(velocity.shape, BF16),
            pltpu.VMEM(adjoint.shape, BF16),
            pltpu.VMEM(stretch.shape, F32),
            pltpu.VMEM(shear_part.shape, F32),
            pltpu.VMEM(shared.shape, jnp.int32),
            pltpu.SemaphoreType.DMA((10,)),
        ),
    )
    below = shifted(top, "layer", -1)
    chunk = min(1024, elems)
    data, lists, joined, picked, hots, coded, early = kernel_call(
        element_kernel,
        (
            shape((rows, slots), F32),
            shape((4, slots), jnp.int32),
            shape((1, 4 * slots), jnp.int32),
            shape((4 * rows, slots), BF16),
            shape((SPAN, 4 * slots), BF16),
            shape((2 * rows, slots), BF16),
            shape((4 * rows, chunk), F32),
        ),
        2 * 10**9,
        params, names, sends, fields,
    )
    low, messages = kernel_call(
        message_kernel,
        (shape((16, slots), BF16), shape((parts, 6 * rows + 16, slot), BF16)),
        10**9,
        below, joined, hots, picked, coded,
        scratch=(pltpu.SemaphoreType.DMA((12,)),),
        free=(1,),
    )
    order = [turned(i, parts) for i in range(parts)]
    incoming = lax.all_to_all(messages, "plane", 0, 0, axis_index_groups=[order])
    state = kernel_call(
        physics_kernel,
        shape((4, elems), F32),
        10**10,
        fields, below, names, params, early,
        scratch=(pltpu.VMEM((4 * rows, chunk), F32),) * 2 + (pltpu.VMEM((32, chunk), F32),) * 2,
    )
    state = kernel_call(
        border_kernel,
        shape((4, elems + 2 * slots), F32),
        10**9,
        state, data, picked, low, incoming,
    )
    groups, place = lax.axis_size("layer"), lax.axis_index("layer")
    step = 1
    while 2 * step < groups:
        other = lax.ppermute(state, "layer", [(i, i ^ step) for i in range(groups)])
        second = (place & step) != 0
        state = compose(jnp.where(second, other, state), jnp.where(second, state, other))
        step *= 2
    mine = jnp.stack([jnp.where((place & step) != 0, state[2], state[1]), state[3]])
    other = jnp.zeros_like(mine)
    if groups > 1:
        other = lax.ppermute(mine, "layer", [(i, i ^ step) for i in range(groups)])
    gradient = kernel_call(
        sum_kernel,
        shape((owned // LANES, LANES), F32),
        2 * 10**9,
        mine, other, names, lists,
    )
    return gradient.reshape(owned)


def solution(mesh):
    return jax.shard_map(
        shards,
        mesh=mesh,
        in_specs=(
            P(None, "layer", "plane"),
            P(None, "layer", "plane"),
            P(None, "plane"),
            P(None, "plane"),
            P(None, "plane"),
            P(None, "plane"),
            P("layer", "plane"),
            P("layer", "plane"),
            P("layer", "plane"),
            P("layer", "plane"),
        ),
        out_specs=P("plane"),
        check_vma=False,
    )
```

```python
import functools
import math

import jax
import jax.numpy as jnp
from jax import lax
from jax.experimental import pallas as pl
from jax.experimental.pallas import tpu as pltpu
from jax.sharding import PartitionSpec as P

OFFSETS = (-2, -1, 1, 2)
STRAIN_EPS = 0.01
GAUSS = 1.0 / math.sqrt(3.0)
SPAN = 256
LANES = 128
TURN = 1
PIECES = 2
F32, BF16 = jnp.float32, jnp.bfloat16
NT = (((1,), (1,)), ((), ()))


def shifted(value, axis, steps):
    count = lax.axis_size(axis)
    first, last = (max(0, -steps), min(count, count - steps))
    return lax.ppermute(value, axis, [(source, source + steps) for source in range(first, last)])


def kernel_call(body, out_shape, flops, *args, spaces=None, scratch=(), free=()):
    vmem = pl.BlockSpec(memory_space=pltpu.VMEM)
    far = pl.BlockSpec(memory_space=pltpu.HBM)
    if spaces == "far":
        args = [pltpu.with_memory_space_constraint(value, pltpu.HBM) for value in args]
    return pl.pallas_call(
        body,
        out_shape=out_shape,
        in_specs=[far if spaces == "far" else vmem for _ in args],
        out_specs=[
            pl.BlockSpec(memory_space=pl.ANY) if i in free else vmem for i in range(len(out_shape))
        ]
        if isinstance(out_shape, tuple)
        else vmem,
        scratch_shapes=list(scratch),
        compiler_params=pltpu.CompilerParams(vmem_limit_bytes=24 * 2**20),
        cost_estimate=pl.CostEstimate(flops=flops, bytes_accessed=2**20, transcendentals=0),
    )(*args)


def node_table(fields):
    blocks = fields.shape[1] // SPAN
    return jnp.concatenate([fields[:, h * SPAN : (h + 1) * SPAN] for h in range(blocks)], axis=0)


def level_table(level):
    blocks = level.shape[1] // SPAN
    return jnp.concatenate([level[:, h * SPAN : (h + 1) * SPAN] for h in range(blocks)], axis=0)


def one_hot(low):
    shape = (SPAN, low.shape[1])
    rows = lax.broadcasted_iota(jnp.int32, shape, 0).astype(F32).astype(BF16)
    wanted = jnp.broadcast_to(low.astype(F32).astype(BF16), shape)
    return jnp.where(rows == wanted, jnp.ones(shape, BF16), jnp.zeros(shape, BF16))


def bit_masks(high, blocks):
    wide = jnp.broadcast_to(high, (8, high.shape[1]))
    return [(wide & (1 << k)) != 0 for k in range(blocks.bit_length() - 1)]


def choose(parts, masks):
    for mask in masks:
        parts = [jnp.where(mask, parts[i + 1], parts[i]) for i in range(0, len(parts), 2)]
    return parts[0]


def choose_rows(picked, masks, rows, r):
    return choose([picked[h + r : h + r + 8] for h in range(0, picked.shape[0], rows)], masks)


def choose_low(picked, masks):
    pair = choose([picked[h : h + 8] for h in range(0, picked.shape[0], 8)], masks[1:])
    return jnp.where(masks[0][:4], pair[4:], pair[:4])


def product(table, hot):
    return jnp.dot(table, hot, preferred_element_type=F32)


def alternate(first, second, ratio):
    pieces = [(first, 1), (second, ratio)]
    while pieces:
        left = []
        for piece, turns in pieces:
            for _ in range(turns):
                if next(piece, piece) is piece:
                    break
            else:
                left.append((piece, turns))
        pieces = left


def drain(piece):
    while True:
        try:
            next(piece)
        except StopIteration as end:
            return end.value


def fetch_kernel(
    velocity, adjoint, corners, shared, thickness, rate, retention, weight, stretch, shear,
    fields, top, params, names, sends,
    first, second, stretch_here, shear_here, shared_here, semaphores,
):
    layers, elems = thickness.shape
    pairs = [(velocity, first), (adjoint, second), (corners, names), (shared, shared_here)]
    pairs += [(stretch, stretch_here), (shear, shear_here)]
    for i, ref in enumerate((thickness, rate, retention, weight)):
        pairs.append((ref, params.at[pl.ds(i * layers, layers)]))
    cut = elems // PIECES
    copies = []
    for source, target in pairs:
        if source.shape[-1] == elems:
            for k in range(PIECES):
                at = pl.ds(k * cut, cut)
                lead = (slice(None),) * (len(source.shape) - 1)
                copies.append((source.at[(*lead, at)], target.at[(*lead, at)]))
        else:
            copies.append((source, target))
    copies = [
        pltpu.make_async_copy(source, target, semaphores.at[i])
        for i, (source, target) in enumerate(copies)
    ]
    for copy in copies:
        copy.start()
    for copy in copies[: 2 * PIECES]:
        copy.wait()
    parts = [first[0], first[1], second[0], second[1]]
    fields[...] = jnp.concatenate(parts, axis=0)
    wide = [part.astype(F32)[0:1] for part in parts]
    top[...] = level_table(jnp.concatenate(wide, axis=0)).astype(BF16)
    for copy in copies[2 * PIECES :]:
        copy.wait()
    params[4 * layers :, :] = jnp.concatenate(
        [stretch_here[...], shear_here[...], jnp.zeros((4, elems), F32)], axis=0
    )
    sends[...] = jnp.concatenate([shared_here[j : j + 1, :] for j in range(4)], axis=1)


def turned(index, count):
    return index ^ TURN if count % 8 == 0 else index


def block_of(place, offset, count):
    return turned(lax.rem(place + offset + count, count), count)


def element_kernel(
    params, names, sends, fields, data, lists, joined, picked, coded, early
):
    rows, owned = fields.shape
    layers = rows // 4
    elems = names.shape[1]
    slots = data.shape[1]
    held = params.shape[0]
    here = names[...]
    values = params[...]
    coarse = values.astype(BF16).astype(F32)
    left = jnp.concatenate(
        [
            coarse,
            values - coarse,
            (here & (SPAN - 1)).astype(F32),
            (here >> 8).astype(F32),
            jnp.ones((8, elems), F32),
        ],
        axis=0,
    ).astype(BF16)
    wanted = lax.broadcasted_iota(jnp.int32, (slots, elems), 0) + owned
    mine = (wanted == here[0:1]).astype(F32).astype(BF16)
    total = lax.dot_general(left, mine, NT, preferred_element_type=F32)
    ids = (total[2 * held : 2 * held + 4] + total[2 * held + 4 : 2 * held + 8] * SPAN).astype(jnp.int32)
    ids = jnp.where(total[2 * held + 8 : 2 * held + 9] > 0.5, ids, owned)
    lists[...] = jnp.concatenate([sends[...], ids[1:4]], axis=0)
    joined[...] = jnp.concatenate([sends[...], ids[1:2], ids[2:3], ids[3:4]], axis=1)
    stretch, shear, thickness, alpha, beta, factor, offset = group_maps(
        total[:held] + total[held : 2 * held]
    )
    data[...] = jnp.concatenate(
        [
            alpha, beta, thickness, stretch, shear,
            factor[layers - 1 :], offset[layers - 1 :], jnp.zeros((2, slots), F32),
        ],
        axis=0,
    )
    table = node_table(fields)
    for c in range(4):
        wanted = lists[c : c + 1, :]
        hot = one_hot(wanted & (SPAN - 1))
        got = product(table, hot)
        masks = bit_masks(wanted >> 8, owned // SPAN)
        for r in range(0, rows, 8):
            at = slice(c * rows + r, c * rows + r + 8)
            picked[at, :] = choose_rows(got, masks, rows, r).astype(BF16)
    chunk = early.shape[1]
    for c in range(4):
        wanted = names[c : c + 1, :chunk]
        hot = one_hot(wanted & (SPAN - 1))
        got = product(table, hot)
        masks = bit_masks(wanted >> 8, owned // SPAN)
        for r in range(0, rows, 8):
            early[c * rows + r : c * rows + r + 8, :] = choose_rows(got, masks, rows, r)
    coarse = data[...].astype(BF16)
    coded[...] = jnp.concatenate([coarse, (data[...] - coarse.astype(F32)).astype(BF16)], axis=0)


def message_kernel(below, joined, picked, coded, low, out, semaphores):
    slots = low.shape[1]
    slot = out.shape[2]
    upper, extra = picked.shape[0], coded.shape[0]
    place, count = lax.axis_index("plane"), out.shape[0]

    def sends(source, row, first):
        copies = []
        for j, offset in enumerate(OFFSETS):
            copies.append(
                pltpu.make_async_copy(
                    source.at[:, pl.ds(j * slot, slot)],
                    out.at[block_of(place, offset, count), pl.ds(row, source.shape[0]), :],
                    semaphores.at[first + j],
                )
            )
        for copy in copies:
            copy.start()
        return copies

    copies = sends(picked, 0, 0) + sends(coded, upper + 16, 4)
    names = joined[...]
    masks = bit_masks(names >> 8, below.shape[0] // 4)
    values = choose_low(product(below[...], one_hot(names & (SPAN - 1))), masks)
    lower = [values[:, c * slots : (c + 1) * slots] for c in range(4)]
    low[...] = jnp.concatenate(lower, axis=0).astype(BF16)
    copies += sends(low, upper, 8)
    for copy in copies:
        copy.wait()


def plane_modes(a0, a1, a2, a3):
    s01, d01, s23, d23 = a0 + a1, a1 - a0, a2 + a3, a2 - a3
    return s01 + s23, d01 + d23, s23 - s01, d23 - d01


def terms(upper, bottom, stretch, shear, thickness):
    layers, n = thickness.shape
    last = lax.broadcasted_iota(jnp.int32, (layers, n), 0) == layers - 1
    plus, minus, depth = [], [], []
    ends = plane_modes(*bottom)
    for comp in range(4):
        top = plane_modes(*[upper[c][comp] for c in range(4)])
        end = [mode[comp : comp + 1] for mode in ends]
        under = [
            jnp.where(last, jnp.broadcast_to(e, t.shape), pltpu.roll(t, layers - 1, 0))
            for t, e in zip(top, end)
        ]
        depth_parts = [top[0] - under[0]]
        plus_parts, minus_parts = [], []
        for t, u in zip(top[1:], under[1:]):
            total, half = t + u, GAUSS * (t - u)
            plus_parts.append(total + half)
            minus_parts.append(total - half)
            depth_parts.append(half)
        plus.append(plus_parts)
        minus.append(minus_parts)
        depth.append(depth_parts)
        yield
    s0, s1 = stretch[0:1] * (1.0 / 16.0), stretch[1:2] * (1.0 / 16.0)
    h0, h1 = shear[0:1] * (1.0 / 16.0), shear[1:2] * (1.0 / 16.0)
    gs0, gs1, gh0, gh1 = s0 * GAUSS, s1 * GAUSS, h0 * GAUSS, h1 * GAUSS

    def plane_fields(part, first):
        (xa, ya, wa), (xb, yb, wb) = part[first], part[first + 1]
        p1, p2 = s0 * xa + h0 * ya, h1 * xb + s1 * yb
        x1, x2 = gh0 * wa, gs1 * wb
        y1, y2 = gs0 * wa, gh1 * wb
        return (
            (p1 + p2, x1 + x2, y1 + y2),
            (p1 - p2, x1 - x2, y1 - y2),
            (
                (h1 * xa + s1 * ya) + (s0 * xb + h0 * yb),
                gs1 * wa + gh0 * wb,
                gh1 * wa + gs0 * wb,
            ),
        )

    def four(field):
        base, along_x, along_y = field
        up, um = base + along_x, base - along_x
        return up + along_y, up - along_y, um + along_y, um - along_y

    inverse = 0.125 / thickness
    inverse_g = inverse * GAUSS

    def depth_four(parts):
        q0, qx, qy, qw = (
            parts[0] * inverse,
            parts[1] * inverse,
            parts[2] * inverse,
            parts[3] * inverse_g,
        )
        p, m, r, t = q0 + qx, q0 - qx, qy + qw, qy - qw
        return p + r, p - r, m + t, m - t

    za, zb, zc, zd = [depth_four(depth[comp]) for comp in range(4)]
    shear_ff = [za[k] * za[k] + zb[k] * zb[k] + STRAIN_EPS for k in range(4)]
    shear_fa = [za[k] * zc[k] + zb[k] * zd[k] for k in range(4)]
    yield
    total = None
    for part in (plus, minus):
        flow = [four(f) for f in plane_fields(part, 0)]
        other = [four(f) for f in plane_fields(part, 2)]
        for k in range(4):
            s, d, x = flow[0][k], flow[1][k], flow[2][k]
            triple = 3.0 * s
            effective = (triple * s + d * d) + (x * x + shear_ff[k])
            paired = (triple * other[0][k] + d * other[1][k]) + (x * other[2][k] + shear_fa[k])
            value = jnp.exp2(jnp.log2(effective) * (-1.0 / 3.0)) * paired
            total = value if total is None else total + value
            yield
    return total


def group_maps(params):
    layers = (params.shape[0] - 8) // 4
    thickness, rate, retention, weight = [
        params[i * layers : (i + 1) * layers] for i in range(4)
    ]
    stretch, shear = params[4 * layers : 4 * layers + 2], params[4 * layers + 2 : 4 * layers + 4]
    row = lax.broadcasted_iota(jnp.int32, retention.shape, 0)
    factor, offset = retention, (1.0 - retention) * weight
    step = 1
    while step < layers:
        seen = row >= step
        before_f = jnp.where(seen, pltpu.roll(factor, step, 0), 1.0)
        before_o = jnp.where(seen, pltpu.roll(offset, step, 0), 0.0)
        offset = factor * before_o + offset
        factor = factor * before_f
        step *= 2
    det = stretch[0:1] * stretch[1:2] - shear[0:1] * shear[1:2]
    gain = rate * thickness / det
    return stretch, shear, thickness, factor * gain, offset * gain, factor, offset


def column_state(factor, offset, alpha, beta, term):
    return jnp.concatenate(
        [
            factor,
            offset,
            jnp.sum(alpha * term, axis=0, keepdims=True),
            jnp.sum(beta * term, axis=0, keepdims=True),
        ],
        axis=0,
    )


def element_maps(tops, ends, params):
    stretch, shear, thickness, alpha, beta, factor, offset = group_maps(params)
    layers = thickness.shape[0]
    term = yield from terms(tops, ends, stretch, shear, thickness)
    return column_state(factor[layers - 1 :], offset[layers - 1 :], alpha, beta, term)


def physics_kernel(
    fields, below, names, params, early, out, first, second, low_first, low_second
):
    rows, owned = fields.shape
    layers = rows // 4
    elems = names.shape[1]
    chunk = first.shape[1]
    count = elems // chunk
    low_table = below[...]
    table = jnp.concatenate([node_table(fields), low_table], axis=0)
    split = table.shape[0] - low_table.shape[0]
    blocks = owned // SPAN

    def gather(i, held, low):
        for c in range(4):
            wanted = names[c : c + 1, i * chunk : (i + 1) * chunk]
            masks = bit_masks(wanted >> 8, blocks)
            picked = product(table, one_hot(wanted & (SPAN - 1)))
            yield
            for r in range(0, rows, 8):
                at = slice(c * rows + r, c * rows + r + 8)
                held[at, :] = choose_rows(picked[:split], masks, rows, r)
                yield
            low[8 * c : 8 * c + 4, :] = choose_low(picked[split:], masks)

    def work(i, held, low):
        for k in range(chunk // LANES):
            cut = slice(k * LANES, (k + 1) * LANES)
            here = slice(i * chunk + k * LANES, i * chunk + (k + 1) * LANES)
            tops = [
                [
                    held[c * rows + m * layers : c * rows + (m + 1) * layers, cut]
                    for m in range(4)
                ]
                for c in range(4)
            ]
            ends = [low[8 * c : 8 * c + 4, cut] for c in range(4)]
            out[:, here] = yield from element_maps(tops, ends, params[:, here])

    for c in range(4):
        wanted = names[c : c + 1, :chunk]
        masks = bit_masks(wanted >> 8, blocks)
        picked = product(low_table, one_hot(wanted & (SPAN - 1)))
        low_first[8 * c : 8 * c + 4, :] = choose_low(picked, masks)
    held = (early, low_first)
    spare = [(second, low_second), (first, low_first)]
    for i in range(count - 1):
        following = spare[i % 2]
        alternate(gather(i + 1, *following), work(i, *held), 3)
        held = following
    drain(work(count - 1, *held))


def border_kernel(state, data, picked, low, messages, out):
    elems = state.shape[1]
    rows = picked.shape[0] // 4
    layers = rows // 4
    slot = messages.shape[2]
    slots = 4 * slot
    place, count = lax.axis_index("plane"), messages.shape[0]
    out[:, :elems] = state[...]
    pieces = []
    for offset in OFFSETS:
        source = jnp.clip(place + offset, 0, count - 1)
        pieces.append(messages[turned(source, count)])
    got = jnp.concatenate(pieces, axis=1).astype(F32)
    mine = picked[...].astype(F32)
    ends = low[...].astype(F32)
    split = 4 * rows + 16
    half = (got.shape[0] - split) // 2
    sides = (
        (got, mine, got[4 * rows : split], ends, data[...]),
        (mine, got, ends, got[4 * rows : split], got[split : split + half] + got[split + half :]),
    )
    for side, (corner0, others, end0, end_others, params) in enumerate(sides):
        for k in range(slots // LANES):
            cut = slice(k * LANES, (k + 1) * LANES)
            tops = [
                [
                    (others if c else corner0)[c * rows + m * layers : c * rows + (m + 1) * layers, cut]
                    for m in range(4)
                ]
                for c in range(4)
            ]
            bots = [(end_others if c else end0)[4 * c : 4 * c + 4, cut] for c in range(4)]
            start = elems + side * slots + k * LANES
            part = params[:, cut]
            alpha, beta, thickness = [part[i * layers : (i + 1) * layers] for i in range(3)]
            rest = part[3 * layers :]
            term = drain(terms(tops, bots, rest[:2], rest[2:4], thickness))
            out[:, start : start + LANES] = column_state(rest[4:5], rest[5:6], alpha, beta, term)


def sum_kernel(first, second, corners, lists, out):
    elems = corners.shape[1]
    slots = lists.shape[1]
    high_count = out.shape[0]
    owned = high_count * LANES
    column = 0.25 * (first[1:2, :] + second[1:2, :] + first[0:1, :] * second[0:1, :])
    main, ghost, near = (
        column[:, :elems],
        column[:, elems : elems + slots],
        column[:, elems + slots :],
    )
    main = jnp.where(corners[0:1, :] < owned, main, 0.0)
    work = [(corners[c : c + 1, :], main) for c in range(4)]
    work += [(lists[c : c + 1, :], ghost if c else near) for c in range(4)]
    total = None
    for at, (names, values) in enumerate(work):
        width = names.shape[1]
        if at >= 4:
            values = jnp.where(names < owned, values, 0.0)
        low, high = names & (LANES - 1), names >> 7
        coarse = values.astype(BF16).astype(F32)
        here = lax.broadcasted_iota(jnp.int32, (high_count, width), 0) == high
        parts = [jnp.where(here, coarse, 0.0), jnp.where(here, values - coarse, 0.0)]
        parts = jnp.concatenate(parts, axis=0).astype(BF16)
        hot = (lax.broadcasted_iota(jnp.int32, (LANES, width), 0) == low).astype(F32).astype(BF16)
        added = lax.dot_general(hot, parts, NT, preferred_element_type=F32)
        total = added if total is None else total + added
    total = total.T
    out[...] = total[:high_count] + total[high_count:]


def compose_kernel(step, last, state, other, out):
    place = lax.axis_index("layer")
    second = (place & step) != 0
    mine, theirs = state[...], other[...]
    one, two = jnp.where(second, theirs, mine), jnp.where(second, mine, theirs)
    offset = two[0:1] * one[1:2] + two[1:2]
    alpha = one[2:3] + one[0:1] * two[2:3]
    total = one[3:4] + two[3:4] + one[1:2] * two[2:3]
    if last:
        rows = [jnp.where((place & (2 * step)) != 0, alpha, offset), total]
    else:
        rows = [one[0:1] * two[0:1], offset, alpha, total]
    out[...] = jnp.concatenate(rows, axis=0)


def shards(
    velocity, adjoint, corners, shared, stretch, shear_part, thickness, rate_factor, retention, weight
):
    layers, owned = velocity.shape[1:]
    elems = corners.shape[1]
    slot = shared.shape[1]
    slots = 4 * slot
    rows = 4 * layers
    shape = jax.ShapeDtypeStruct
    parts = lax.axis_size("plane")
    fields, top, params, names, sends = kernel_call(
        fetch_kernel,
        (
            shape((rows, owned), BF16),
            shape((4 * owned // SPAN, SPAN), BF16),
            shape((rows + 8, elems), F32),
            shape(corners.shape, jnp.int32),
            shape((1, slots), jnp.int32),
        ),
        10**6,
        velocity, adjoint, corners, shared, thickness, rate_factor, retention, weight, stretch, shear_part,
        spaces="far",
        scratch=(
            pltpu.VMEM(velocity.shape, BF16),
            pltpu.VMEM(adjoint.shape, BF16),
            pltpu.VMEM(stretch.shape, F32),
            pltpu.VMEM(shear_part.shape, F32),
            pltpu.VMEM(shared.shape, jnp.int32),
            pltpu.SemaphoreType.DMA((10 * PIECES,)),
        ),
    )
    below = shifted(top, "layer", -1)
    chunk = min(1024, elems)
    data, lists, joined, picked, coded, early = kernel_call(
        element_kernel,
        (
            shape((rows, slots), F32),
            shape((4, slots), jnp.int32),
            shape((1, 4 * slots), jnp.int32),
            shape((4 * rows, slots), BF16),
            shape((2 * rows, slots), BF16),
            shape((4 * rows, chunk), F32),
        ),
        2 * 10**9,
        params, names, sends, fields,
    )
    low, messages = kernel_call(
        message_kernel,
        (shape((16, slots), BF16), shape((parts, 6 * rows + 16, slot), BF16)),
        10**9,
        below, joined, picked, coded,
        scratch=(pltpu.SemaphoreType.DMA((12,)),),
        free=(1,),
    )
    order = [turned(i, parts) for i in range(parts)]
    incoming = lax.all_to_all(messages, "plane", 0, 0, axis_index_groups=[order])
    state = kernel_call(
        physics_kernel,
        shape((4, elems), F32),
        10**10,
        fields, below, names, params, early,
        scratch=(pltpu.VMEM((4 * rows, chunk), F32),) * 2 + (pltpu.VMEM((32, chunk), F32),) * 2,
    )
    state = kernel_call(
        border_kernel,
        shape((4, elems + 2 * slots), F32),
        10**9,
        state, data, picked, low, incoming,
    )
    groups, place = lax.axis_size("layer"), lax.axis_index("layer")
    step = 1
    while 2 * step < groups:
        other = lax.ppermute(state, "layer", [(i, i ^ step) for i in range(groups)])
        last = 4 * step >= groups
        mine = state = kernel_call(
            functools.partial(compose_kernel, step, last),
            shape((2 if last else 4, state.shape[1]), F32),
            10**5,
            state, other,
        )
        step *= 2
    if step == 1:
        mine = jnp.stack([jnp.where((place & 1) != 0, state[2], state[1]), state[3]])
    other = jnp.zeros_like(mine)
    if groups > 1:
        other = lax.ppermute(mine, "layer", [(i, i ^ step) for i in range(groups)])
    gradient = kernel_call(
        sum_kernel,
        shape((owned // LANES, LANES), F32),
        2 * 10**9,
        mine, other, names, lists,
    )
    return gradient.reshape(owned)


def solution(mesh):
    return jax.shard_map(
        shards,
        mesh=mesh,
        in_specs=(
            P(None, "layer", "plane"),
            P(None, "layer", "plane"),
            P(None, "plane"),
            P(None, "plane"),
            P(None, "plane"),
            P(None, "plane"),
            P("layer", "plane"),
            P("layer", "plane"),
            P("layer", "plane"),
            P("layer", "plane"),
        ),
        out_specs=P("plane"),
        check_vma=False,
    )
```
